32 devices in a mesh: dp: 8 (over z, y), mp: 4 (over x, core).
Axes of the slice: x: 2, y: 2, z: 4, core: 2. Of those that a mesh axis runs over, the one named last changes fastest.
Arguments:
- inputs: bfloat16 [16384, 768], P(('dp', 'mp')), may hold values from -36 to 36
- cotangent: bfloat16 [16384, 768], P(('dp', 'mp')), may hold values from -6 to 6
- gain_attn: float32 [768], replicated, may hold values from 0.1 to 1.9
- shift_attn: float32 [768], replicated, may hold values from -3 to 3
- weight_query: bfloat16 [768, 768], P(None, 'mp'), may hold values from -0.21875 to 0.21875
- bias_query: float32 [768], P('mp'), may hold values from -3 to 3
- weight_key: bfloat16 [768, 768], P(None, 'mp'), may hold values from -0.21875 to 0.21875
- weight_value: bfloat16 [768, 768], P(None, 'mp'), may hold values from -0.21875 to 0.21875
- bias_value: float32 [768], P('mp'), may hold values from -3 to 3
- table_horizontal: float32 [64, 12], P(None, 'mp'), may hold values from -4 to 4
- table_vertical: float32 [64, 12], P(None, 'mp'), may hold values from -4 to 4
- weight_out: bfloat16 [768, 768], P('mp'), may hold values from -0.875 to 0.875
- bias_out: float32 [768], replicated, may hold values from -3 to 3
- gain_mlp: float32 [768], replicated, may hold values from 0.1 to 1.9
- shift_mlp: float32 [768], replicated, may hold values from -3 to 3
- weight_up: bfloat16 [768, 3072], P(None, 'mp'), may hold values from -0.21875 to 0.21875
- bias_up: float32 [3072], P('mp'), may hold values from -3 to 3
- weight_down: bfloat16 [3072, 768], P('mp'), may hold values from -0.15625 to 0.15625
- bias_down: float32 [768], replicated, may hold values from -3 to 3
- segment: int32 [32, 512], P('dp'), may hold values from 0 to 63, as said below
- valid: int32 [32, 512], P('dp'), may hold values from 0 to 1, as said below
- bucket_horizontal: int32 [32, 64, 64], P('dp'), may hold values from 0 to 63, as said below
- bucket_vertical: int32 [32, 64, 64], P('dp'), may hold values from 0 to 63, as said below
Outputs:
- result: bfloat16 [16384, 768], P(('dp', 'mp'))
- grad_inputs: bfloat16 [16384, 768], P(('dp', 'mp'))
- grad_gain_attn: float32 [768], replicated
- grad_shift_attn: float32 [768], replicated
- grad_weight_query: float32 [768, 768], P(None, 'mp')
- grad_bias_query: float32 [768], P('mp')
- grad_weight_key: float32 [768, 768], P(None, 'mp')
- grad_weight_value: float32 [768, 768], P(None, 'mp')
- grad_bias_value: float32 [768], P('mp')
- grad_table_horizontal: float32 [64, 12], P(None, 'mp')
- grad_table_vertical: float32 [64, 12], P(None, 'mp')
- grad_weight_out: float32 [768, 768], P('mp')
- grad_bias_out: float32 [768], replicated
- grad_gain_mlp: float32 [768], replicated
- grad_shift_mlp: float32 [768], replicated
- grad_weight_up: float32 [768, 3072], P(None, 'mp')
- grad_bias_up: float32 [3072], P('mp')
- grad_weight_down: float32 [3072, 768], P('mp')
- grad_bias_down: float32 [768], replicated
The draws below stay inside these ranges and needn't reach their ends.
Inputs may be any that keep to these rules, and one draw needn't show every extreme that they name: `segment`: within a page the indices start at 0, never fall and rise by at most one from a token to the next. `valid`: on each page the real tokens come first, 128 of them or more. `bucket_horizontal`: the bucket of a segment with itself is 32. `bucket_vertical`: the bucket of a segment with itself is 32.
All inputs are finite; a program needn't handle non-finite values.
Results may differ from the reference program's by a relative error of at most 0.015.
Values may be sent and summed in bfloat16 or wider, within the bound.
No kernel may reach another device: no remote copies, remote signals or barrier semaphores. Data moves between devices by JAX's collectives and lax.ppermute only.
A program may use at most 128 MiB of HBM per device.

```python
import math
import jax
import jax.numpy as jnp
from jax import lax

D = 768
HEADS = 12
HEAD = 64
FF = 3072
SEQ = 512
SEGS = 64
BINS = 64
PAGES_DEV = 4
PAGES = 32
TOKENS = 16384


def draw_inputs(key, part):
    key = jax.random.fold_in(key, 11)
    base_key, row_key, column_key = jax.random.split(key, 3)
    row_scale = jnp.exp(jax.random.uniform(row_key, (TOKENS, 1), jnp.float32, math.log(0.3), math.log(3.0)))
    column_scale = jnp.exp(jax.random.uniform(column_key, (1, D), jnp.float32, math.log(0.3), math.log(3.0)))
    base = jnp.clip(jax.random.normal(base_key, (TOKENS, D), jnp.float32), -4.0, 4.0)
    return (base * row_scale * column_scale).astype(jnp.bfloat16)


def draw_segment(key, part):
    key = jax.random.fold_in(key, 21)
    count_key, order_key = jax.random.split(key)
    page_index = jnp.arange(PAGES, dtype=jnp.int32)
    counts = jax.random.randint(count_key, (PAGES,), 3, SEGS + 1, dtype=jnp.int32)
    counts = jnp.where(page_index == 0, SEGS, counts)
    page_keys = jax.random.split(order_key, PAGES)
    ranks = jax.vmap(lambda page_key: jax.random.permutation(page_key, SEQ - 1))(page_keys).astype(jnp.int32)
    flags = (ranks < counts[:, None] - 1).astype(jnp.int32)
    starts = jnp.zeros((PAGES, 1), jnp.int32)
    return jnp.concatenate([starts, jnp.cumsum(flags, axis=1).astype(jnp.int32)], axis=1)


def draw_valid(key, part):
    key = jax.random.fold_in(key, 31)
    page_index = jnp.arange(PAGES, dtype=jnp.int32)
    lengths = jax.random.randint(key, (PAGES,), SEQ // 4, SEQ + 1, dtype=jnp.int32)
    lengths = jnp.where(page_index == 0, SEQ, lengths)
    positions = jnp.arange(SEQ, dtype=jnp.int32)
    return (positions[None, :] < lengths[:, None]).astype(jnp.int32)


def offset_buckets(key):
    coords = jax.random.randint(key, (PAGES, SEGS), 0, 1000, dtype=jnp.int32)
    page_index = jnp.arange(PAGES, dtype=jnp.int32)[:, None]
    seg_index = jnp.arange(SEGS, dtype=jnp.int32)[None, :]
    coords = jnp.where((page_index == 0) & (seg_index == 0), 0, coords)
    coords = jnp.where((page_index == 0) & (seg_index == 1), 999, coords)
    offset = coords[:, None, :] - coords[:, :, None]
    return jnp.clip((offset + 1000) * BINS // 2000, 0, BINS - 1).astype(jnp.int32)


def draw_bucket_horizontal(key, part):
    key = jax.random.fold_in(key, 41)
    return offset_buckets(key)


def draw_bucket_vertical(key, part):
    key = jax.random.fold_in(key, 51)
    return offset_buckets(key)


def block_scale(rng, shape, shards, smallest, largest):
    gain, own = 1.0, jax.random.fold_in(rng, 6)
    for axis_at, blocks in shards:
        steps = jnp.exp(jax.random.uniform(jax.random.fold_in(own, axis_at), (blocks,), jnp.float32, smallest / len(shards), largest / len(shards)))
        gain = gain * jnp.repeat(steps, shape[axis_at] // blocks).reshape([-1 if axis == axis_at else 1 for axis in range(len(shape))])
    return gain


def normal_values(own_key, shape, scale, reach, cuts=(), kind=jnp.bfloat16):
    entries = jax.random.normal(own_key, shape, jnp.float32) * scale
    if len(cuts) > 0:
        entries = block_scale(own_key, shape, cuts, -0.22, 0.18) * entries
    return jnp.clip(entries, min=-reach, max=reach).astype(kind)


def setup_inputs(seed: int = 0) -> dict:
    keys = jax.random.split(jax.random.key(seed), 24)
    inputs = draw_inputs(jax.random.fold_in(keys[23], 71), 0)
    cotangent = normal_values(keys[1], (TOKENS, D), 1.0, 6.0, ((0, 32),))
    gain_attn = jnp.clip(1.0 + 0.18 * jax.random.normal(keys[2], (D,), jnp.float32), 0.1, 1.9)
    shift_attn = normal_values(keys[3], (D,), 0.5, 3.0, (), jnp.float32)
    weight_query = normal_values(keys[4], (D, D), D ** -0.5, 0.21875, ((1, 4),))
    bias_query = normal_values(keys[5], (D,), 0.5, 3.0, ((0, 4),), jnp.float32)
    weight_key = normal_values(keys[6], (D, D), D ** -0.5, 0.21875, ((1, 4),))
    weight_value = normal_values(keys[7], (D, D), D ** -0.5, 0.21875, ((1, 4),))
    bias_value = normal_values(keys[8], (D,), 0.5, 3.0, ((0, 4),), jnp.float32)
    table_horizontal = normal_values(keys[9], (BINS, HEADS), 1.0, 4.0, ((1, 4),), jnp.float32)
    table_vertical = normal_values(keys[10], (BINS, HEADS), 1.0, 4.0, ((1, 4),), jnp.float32)
    weight_out = normal_values(keys[11], (D, D), (D // 16) ** -0.5, 0.875, ((0, 4),))
    bias_out = normal_values(keys[12], (D,), 0.5, 3.0, (), jnp.float32)
    gain_mlp = jnp.clip(1.0 + 0.18 * jax.random.normal(keys[13], (D,), jnp.float32), 0.1, 1.9)
    shift_mlp = normal_values(keys[14], (D,), 0.5, 3.0, (), jnp.float32)
    weight_up = normal_values(keys[15], (D, FF), D ** -0.5, 0.21875, ((1, 4),))
    bias_up = normal_values(keys[16], (FF,), 0.5, 3.0, ((0, 4),), jnp.float32)
    weight_down = normal_values(keys[17], (FF, D), (FF // 2) ** -0.5, 0.15625, ((0, 4),))
    bias_down = normal_values(keys[18], (D,), 0.5, 3.0, (), jnp.float32)
    segment = draw_segment(jax.random.fold_in(keys[23], 71), 0)
    valid = draw_valid(jax.random.fold_in(keys[23], 71), 0)
    bucket_horizontal = draw_bucket_horizontal(jax.random.fold_in(keys[23], 71), 0)
    bucket_vertical = draw_bucket_vertical(jax.random.fold_in(keys[23], 71), 0)
    return dict(inputs=inputs, cotangent=cotangent, gain_attn=gain_attn, shift_attn=shift_attn, weight_query=weight_query, bias_query=bias_query, weight_key=weight_key, weight_value=weight_value, bias_value=bias_value, table_horizontal=table_horizontal, table_vertical=table_vertical, weight_out=weight_out, bias_out=bias_out, gain_mlp=gain_mlp, shift_mlp=shift_mlp, weight_up=weight_up, bias_up=bias_up, weight_down=weight_down, bias_down=bias_down, segment=segment, valid=valid, bucket_horizontal=bucket_horizontal, bucket_vertical=bucket_vertical)


@jax.custom_vjp
def low(v):
    return lax.optimization_barrier(v.astype(jnp.bfloat16)).astype(jnp.float32)

@jax.custom_vjp
def low_back(v):
    return v

def low_keep(v):
    return (low(v), None)

def low_pass(kept, grad):
    return (grad,)

def back_keep(v):
    return (v, None)

def back_low(kept, grad):
    return (low(grad),)
low.defvjp(low_keep, low_pass)
low_back.defvjp(back_keep, back_low)
EPSILON = 1e-05
NEGATIVE = -1e+30
HIGH = lax.Precision.HIGHEST

def matmul(left, right):
    return jnp.dot(left, right, precision=HIGH, preferred_element_type=jnp.float32)

def norm_rows(values, gain_vec, shift_vec):
    average = lax.optimization_barrier(jnp.mean(values, axis=-1, keepdims=True))
    centered = values - average
    variance = lax.optimization_barrier(jnp.mean(centered * centered, axis=-1, keepdims=True))
    return centered * lax.rsqrt(variance + EPSILON) * gain_vec + shift_vec

def forward(residual_in, params, segment, valid, bucket_horizontal, bucket_vertical):
    gain_attn, shift_attn, weight_query, bias_query, weight_key, weight_value, bias_value, table_horizontal, table_vertical, weight_out, bias_out, gain_mlp, shift_mlp, weight_up, bias_up, weight_down, bias_down = params
    normed_attn = low(norm_rows(residual_in, gain_attn, shift_attn))
    query = low(low_back((matmul(normed_attn, weight_query) + bias_query) * 0.125))
    key_proj = low(low_back(matmul(normed_attn, weight_key)))
    value_proj = low(low_back(matmul(normed_attn, weight_value) + bias_value))
    page_count = segment.shape[0]

    def attend(items):
        query_page, key_page, value_page, segment_row, valid_row, bucket_hp, bucket_vp = items
        pair_horizontal = bucket_hp[segment_row[:, None], segment_row[None, :]]
        pair_vertical = bucket_vp[segment_row[:, None], segment_row[None, :]]
        pos_bias = jnp.transpose(table_horizontal[pair_horizontal] + table_vertical[pair_vertical], (2, 0, 1))
        scores = jnp.einsum('qhd,khd->hqk', query_page, key_page, precision=HIGH) + pos_bias
        scores = low_back(scores)
        scores = jnp.where(valid_row[None, None, :] > 0, scores, NEGATIVE)
        top_score = lax.optimization_barrier(jnp.max(scores, axis=-1, keepdims=True))
        expo_scores = jnp.exp(scores - top_score)
        probability = low(expo_scores / lax.optimization_barrier(jnp.sum(expo_scores, axis=-1, keepdims=True)))
        return jnp.einsum('hqk,khd->qhd', probability, value_page, precision=HIGH).reshape(SEQ, D)
    shape_four = (page_count, SEQ, HEADS, HEAD)
    context = lax.map(jax.checkpoint(attend), (query.reshape(shape_four), key_proj.reshape(shape_four), value_proj.reshape(shape_four), segment, valid, bucket_horizontal, bucket_vertical))
    context = low(low_back(context.reshape(page_count * SEQ, D)))
    middle = residual_in + low_back(matmul(context, weight_out)) + bias_out
    normed_mlp = low(norm_rows(middle, gain_mlp, shift_mlp))
    upper = low_back(matmul(normed_mlp, weight_up) + bias_up)
    hidden = low(jax.nn.gelu(upper, approximate=False))
    return middle + matmul(hidden, weight_down) + bias_down

def reference(inputs, cotangent, gain_attn, shift_attn, weight_query, bias_query, weight_key, weight_value, bias_value, table_horizontal, table_vertical, weight_out, bias_out, gain_mlp, shift_mlp, weight_up, bias_up, weight_down, bias_down, segment, valid, bucket_horizontal, bucket_vertical):
    params = tuple((item.astype(jnp.float32) for item in (gain_attn, shift_attn, weight_query, bias_query, weight_key, weight_value, bias_value, table_horizontal, table_vertical, weight_out, bias_out, gain_mlp, shift_mlp, weight_up, bias_up, weight_down, bias_down)))
    group_count = PAGES // PAGES_DEV
    group_rows = PAGES_DEV * SEQ
    xs = (inputs.reshape(group_count, group_rows, D), cotangent.reshape(group_count, group_rows, D), segment.reshape(group_count, PAGES_DEV, SEQ), valid.reshape(group_count, PAGES_DEV, SEQ), bucket_horizontal.reshape(group_count, PAGES_DEV, SEGS, SEGS), bucket_vertical.reshape(group_count, PAGES_DEV, SEGS, SEGS))

    def step(carry, items):
        input_block, cot_block, segment_block, valid_block, bucket_hb, bucket_vb = items

        def layer(residual_in, *weights):
            return forward(residual_in, weights, segment_block, valid_block, bucket_hb, bucket_vb)
        output, pullback = jax.vjp(layer, input_block.astype(jnp.float32), *params)
        grads = pullback(cot_block.astype(jnp.float32))
        new_carry = tuple((total + grad for total, grad in zip(carry, grads[1:])))
        return (new_carry, (output.astype(jnp.bfloat16), grads[0].astype(jnp.bfloat16)))
    init = tuple((jnp.zeros_like(item) for item in params))
    totals, (outputs, input_grads) = lax.scan(step, init, xs)
    g_gain_attn, g_shift_attn, g_weight_query, g_bias_query, g_weight_key, g_weight_value, g_bias_value, g_table_horizontal, g_table_vertical, g_weight_out, g_bias_out, g_gain_mlp, g_shift_mlp, g_weight_up, g_bias_up, g_weight_down, g_bias_down = totals
    return (outputs.reshape(TOKENS, D), input_grads.reshape(TOKENS, D), g_gain_attn, g_shift_attn, g_weight_query, g_bias_query, g_weight_key, g_weight_value, g_bias_value, g_table_horizontal, g_table_vertical, g_weight_out, g_bias_out, g_gain_mlp, g_shift_mlp, g_weight_up, g_bias_up, g_weight_down, g_bias_down)
```

```python
import functools

import jax
import jax.numpy as jnp
from jax import lax
from jax.experimental import pallas as pl
from jax.experimental.pallas import tpu as pltpu
from jax.sharding import PartitionSpec as P

EPSILON = 1e-05
NEGATIVE = -1e30
HEAD = 64
EXTRA = 16
F32 = jnp.float32
BF16 = jnp.bfloat16
LIMIT = 48 * 1024 * 1024

NN = (((1,), (0,)), ((), ()))
NT = (((1,), (1,)), ((), ()))
TN = (((0,), (0,)), ((), ()))


def mm(left, right, dims=NN):
    return lax.dot_general(left, right, dims, preferred_element_type=F32)


def call(body, outs, name, flops=0, transcendentals=0):
    def run(*args):
        moved = sum(a.size * a.dtype.itemsize for a in args)
        moved += sum(o.size * o.dtype.itemsize for o in outs)
        return pl.pallas_call(
            body,
            out_shape=outs,
            in_specs=[pl.BlockSpec(memory_space=pltpu.VMEM)] * len(args),
            out_specs=[pl.BlockSpec(memory_space=pltpu.VMEM)] * len(outs),
            compiler_params=pltpu.CompilerParams(vmem_limit_bytes=LIMIT),
            cost_estimate=pl.CostEstimate(
                flops=int(flops), bytes_accessed=int(moved), transcendentals=int(transcendentals)
            ),
            name=name,
        )(*args)

    return run


def struct(shape, dtype):
    return jax.ShapeDtypeStruct(shape, dtype)


def halves(values):
    high = values.astype(BF16)
    return high, (values - high.astype(F32)).astype(BF16)


def start_body(x_ref, gain_ref, shift_ref, seg_ref, valid_ref, bh_ref, bv_ref,
               xn_ref, mt_ref, neg_ref, ih_ref, iv_ref):
    x = x_ref[...].astype(F32)
    mean = jnp.mean(x, axis=1, keepdims=True)
    cen = x - mean
    var = jnp.mean(cen * cen, axis=1, keepdims=True)
    xn_ref[...] = (cen * lax.rsqrt(var + EPSILON) * gain_ref[...] + shift_ref[...]).astype(BF16)
    segs, seq = mt_ref.shape
    rows = lax.broadcasted_iota(jnp.int32, (segs, seq), 0)
    member = jnp.where(rows == seg_ref[...], 1.0, 0.0).astype(BF16)
    mt_ref[...] = member
    top = lax.broadcasted_iota(jnp.int32, neg_ref.shape, 0) == 0
    masked = jnp.where(valid_ref[...] > 0, 0.0, NEGATIVE)
    neg_ref[...] = jnp.where(top, masked, 0.0).astype(BF16)
    ih_ref[...] = mm(bh_ref[...].astype(F32).astype(BF16), member, TN).astype(jnp.int32)
    iv_ref[...] = mm(bv_ref[...].astype(F32).astype(BF16), member, TN).astype(jnp.int32) + segs


def lookup(table, index):
    rows, seq = index.shape
    spread = jnp.broadcast_to(table, (rows, 128))
    parts = [
        jnp.take_along_axis(
            spread, index[:, at:at + 128], axis=1, mode="promise_in_bounds"
        )
        for at in range(0, seq, 128)
    ]
    return jnp.concatenate(parts, axis=1)


def attn_body(first, *refs):
    if first:
        xn_ref, a_ref, b_ref, ih_ref, iv_ref, mt_ref, neg_ref = refs[:7]
        outs = refs[7:]
    else:
        xn_ref, a_ref, b_ref, ih_ref, iv_ref, mt_ref, neg_ref, acc_ref = refs[:8]
        outs = refs[8:]
    qkv_ref, ctx_ref, lse_ref, bias_ref, out_ref = outs
    width = b_ref.shape[0] // 2 - EXTRA // 2
    heads = width // HEAD
    seq = xn_ref.shape[0]
    xn = xn_ref[...]
    extra = a_ref[2 * width:2 * width + EXTRA, :]
    pick = jnp.where(lax.broadcasted_iota(jnp.int32, (EXTRA, seq), 0) < 2, 1.0, 0.0).astype(BF16)
    bias = mm(extra[:, heads * 128:heads * 128 + 2 * width], pick, TN)
    qk = mm(a_ref[0:2 * width, :], xn, NT)
    qkv_ref[0:width, :] = ((qk[0:width] + bias[0:width]) * 0.125).astype(BF16)
    qkv_ref[width:2 * width, :] = qk[width:].astype(BF16)
    qkv_ref[2 * width:, :] = (mm(b_ref[0:width, :], xn, NT) + bias[width:]).astype(BF16)
    tables = extra[0:1, :].astype(F32) + extra[1:2, :].astype(F32)
    member = mt_ref[...]
    ones = jnp.ones((EXTRA, seq), BF16)
    for m in range(heads):
        table = tables[:, 128 * m:128 * m + 128]
        pos = lookup(table, ih_ref[...]) + lookup(table, iv_ref[...])
        high, low = halves(pos)
        segs = member.shape[0]
        bias_ref[2 * segs * m:2 * segs * m + segs, :] = high
        bias_ref[2 * segs * m + segs:2 * segs * (m + 1), :] = low
        at = HEAD * m
        q_aug = jnp.concatenate([qkv_ref[at:at + HEAD, :], high, low, ones], axis=0)
        k_aug = jnp.concatenate(
            [qkv_ref[width + at:width + at + HEAD, :], member, member, neg_ref[...]], axis=0
        )
        scores = mm(k_aug, q_aug, TN)
        top = jnp.max(scores, axis=0, keepdims=True)
        expo = jnp.exp(scores - top).astype(BF16)
        v_aug = jnp.concatenate([qkv_ref[2 * width + at:2 * width + at + HEAD, :], ones], axis=0)
        summed = mm(v_aug, expo)
        total = summed[HEAD:HEAD + 1]
        ctx_ref[at:at + HEAD, :] = (summed[0:HEAD] / total).astype(BF16)
        lse_ref[m:m + 1, :] = top + jnp.log(total)
    lse_ref[heads:, :] = jnp.zeros((lse_ref.shape[0] - heads, seq), F32)
    out = mm(ctx_ref[...], b_ref[width:2 * width, :], TN)
    out_ref[...] = out if first else acc_ref[...] + out


def middle_body(x_ref, acc_ref, bias_ref, gain_ref, shift_ref, mid_ref, nm_ref):
    mid = x_ref[...].astype(F32) + acc_ref[...] + bias_ref[...]
    mid_ref[...] = mid
    mean = jnp.mean(mid, axis=1, keepdims=True)
    cen = mid - mean
    var = jnp.mean(cen * cen, axis=1, keepdims=True)
    nm_ref[...] = (cen * lax.rsqrt(var + EPSILON) * gain_ref[...] + shift_ref[...]).astype(BF16)


def mlp_body(first, *refs):
    nm_ref, cot_ref, u0_ref, d0_ref, u1_ref, d1_ref = refs[:6]
    if first:
        outs = refs[6:]
    else:
        acc_down_ref, acc_back_ref = refs[6:8]
        outs = refs[8:]
    down_ref, back_ref, g0_ref, g1_ref, db_ref = outs
    seq, width = nm_ref.shape
    half = d0_ref.shape[0]
    nm_left, nm_right = nm_ref[:, 0:half], nm_ref[:, half:]
    cot = cot_ref[...]
    for n, (u_ref, d_ref, g_ref) in enumerate(((u0_ref, d0_ref, g0_ref), (u1_ref, d1_ref, g1_ref))):
        bias = u_ref[half:half + 1, 0:half].astype(F32) + u_ref[half:half + 1, half:].astype(F32)
        up_left, up_right = u_ref[0:half, 0:half], u_ref[0:half, half:]
        down = d_ref[...]
        upper = mm(nm_left, up_left) + mm(nm_right, up_right) + bias
        cdf = 0.5 + 0.5 * lax.erf(upper * 0.7071067811865476)
        pdf = jnp.exp(upper * upper * -0.5) * 0.3989422804014327
        hidden = (upper * cdf).astype(BF16)
        grad_hidden = mm(cot, down, NT)
        grad_upper = (grad_hidden * (cdf + upper * pdf)).astype(BF16)
        down_out = mm(hidden, down)
        back_left = mm(grad_upper, up_left, NT)
        back_right = mm(grad_upper, up_right, NT)
        if n == 0 and first:
            down_ref[...] = down_out
            back_ref[:, 0:half] = back_left
            back_ref[:, half:] = back_right
        else:
            base_down, base_back = (acc_down_ref, acc_back_ref) if n == 0 else (down_ref, back_ref)
            down_ref[...] = base_down[...] + down_out
            back_ref[:, 0:half] = base_back[:, 0:half] + back_left
            back_ref[:, half:] = base_back[:, half:] + back_right
        g_ref[0:half, 0:half] = mm(nm_left, grad_upper, TN).astype(BF16)
        g_ref[0:half, half:] = mm(nm_right, grad_upper, TN).astype(BF16)
        g_ref[half:, :] = mm(hidden, cot, TN).astype(BF16)
        db = jnp.sum(grad_upper.astype(F32), axis=0, keepdims=True)
        db_ref[:, n * half:(n + 1) * half] = jnp.broadcast_to(db, (db_ref.shape[0], half))


def turn_body(mid_ref, down_ref, bias_ref, back_ref, cot_ref, gain_ref,
              res_ref, gmid_ref, ga_ref, rows_ref):
    mid = mid_ref[...]
    res_ref[...] = (mid + down_ref[...] + bias_ref[...]).astype(BF16)
    mean = jnp.mean(mid, axis=1, keepdims=True)
    cen = mid - mean
    var = jnp.mean(cen * cen, axis=1, keepdims=True)
    rstd = lax.rsqrt(var + EPSILON)
    n = cen * rstd
    back = back_ref[...]
    q = back * gain_ref[...]
    cot = cot_ref[...].astype(F32)
    mean_q = jnp.mean(q, axis=1, keepdims=True)
    mean_qn = jnp.mean(q * n, axis=1, keepdims=True)
    grad = cot + rstd * (q - mean_q - n * mean_qn)
    gmid_ref[...] = grad
    ga_ref[...] = grad.astype(BF16)
    rows_ref[0:1, :] = jnp.sum(grad, axis=0, keepdims=True)
    rows_ref[1:2, :] = jnp.sum(back * n, axis=0, keepdims=True)
    rows_ref[2:3, :] = jnp.sum(back, axis=0, keepdims=True)
    rows_ref[3:4, :] = jnp.sum(cot, axis=0, keepdims=True)
    rows_ref[4:, :] = jnp.zeros((rows_ref.shape[0] - 4, rows_ref.shape[1]), F32)


def attn_back_body(first, *refs):
    xn_ref, ga_ref, a_ref, b_ref, qkv_ref, ctx_ref, lse_ref, bias_ref, mt_ref, neg_ref = refs[:10]
    if first:
        outs = refs[10:]
    else:
        acc_ref = refs[10]
        outs = refs[11:]
    da_ref, db_ref, back_ref, sums_ref, seg_ref, dqkv_ref = outs
    width = ctx_ref.shape[0]
    heads = width // HEAD
    seq = xn_ref.shape[0]
    segs = mt_ref.shape[0]
    ga = ga_ref[...]
    member = mt_ref[...]
    ones = jnp.ones((EXTRA, seq), BF16)
    grad_ctx = mm(b_ref[width:2 * width, :], ga, NT).astype(BF16)
    db_ref[width:2 * width, :] = mm(ctx_ref[...], ga).astype(BF16)
    for m in range(heads):
        at = HEAD * m
        q = qkv_ref[at:at + HEAD, :]
        k = qkv_ref[width + at:width + at + HEAD, :]
        v = qkv_ref[2 * width + at:2 * width + at + HEAD, :]
        g = grad_ctx[at:at + HEAD]
        q_aug = jnp.concatenate([q, bias_ref[2 * segs * m:2 * segs * (m + 1), :], ones], axis=0)
        k_aug = jnp.concatenate([k, member, member, neg_ref[...]], axis=0)
        scores = mm(k_aug, q_aug, TN)
        probs = jnp.exp(scores - lse_ref[m:m + 1, :])
        grad_probs = mm(v, g, TN)
        delta = jnp.sum(probs * grad_probs, axis=0, keepdims=True)
        grad_scores = (probs * (grad_probs - delta)).astype(BF16)
        dqkv_ref[2 * width + at:2 * width + at + HEAD, :] = mm(g, probs.astype(BF16), NT).astype(BF16)
        dqkv_ref[width + at:width + at + HEAD, :] = mm(q, grad_scores, NT).astype(BF16)
        both = mm(jnp.concatenate([k, member], axis=0), grad_scores)
        dqkv_ref[at:at + HEAD, :] = both[0:HEAD].astype(BF16) * jnp.asarray(0.125, BF16)
        high, low = halves(both[HEAD:])
        seg_ref[m] = mm(high, member, NT) + mm(low, member, NT)
    grads = dqkv_ref[...]
    xn = xn_ref[...]
    da_ref[...] = mm(dqkv_ref[0:2 * width, :], xn).astype(BF16)
    db_ref[0:width, :] = mm(dqkv_ref[2 * width:, :], xn).astype(BF16)
    back = mm(dqkv_ref[0:2 * width, :], a_ref[0:2 * width, :], TN)
    back = back + mm(dqkv_ref[2 * width:, :], b_ref[0:width, :], TN)
    back_ref[...] = back if first else acc_ref[...] + back
    sums_ref[...] = mm(jnp.ones((8, seq), BF16), grads, NT)


def end_body(x_ref, back_ref, gmid_ref, gain_ref, gx_ref, rows_ref):
    x = x_ref[...].astype(F32)
    mean = jnp.mean(x, axis=1, keepdims=True)
    cen = x - mean
    var = jnp.mean(cen * cen, axis=1, keepdims=True)
    rstd = lax.rsqrt(var + EPSILON)
    n = cen * rstd
    back = back_ref[...]
    q = back * gain_ref[...]
    mean_q = jnp.mean(q, axis=1, keepdims=True)
    mean_qn = jnp.mean(q * n, axis=1, keepdims=True)
    gx_ref[...] = (gmid_ref[...] + rstd * (q - mean_q - n * mean_qn)).astype(BF16)
    rows_ref[0:1, :] = jnp.sum(back * n, axis=0, keepdims=True)
    rows_ref[1:2, :] = jnp.sum(back, axis=0, keepdims=True)
    rows_ref[2:, :] = jnp.zeros((rows_ref.shape[0] - 2, rows_ref.shape[1]), F32)


def on_device(
    dp_count,
    mp_count,
    inputs,
    cotangent,
    gain_attn,
    shift_attn,
    weight_query,
    bias_query,
    weight_key,
    weight_value,
    bias_value,
    table_horizontal,
    table_vertical,
    weight_out,
    bias_out,
    gain_mlp,
    shift_mlp,
    weight_up,
    bias_up,
    weight_down,
    bias_down,
    segment,
    valid,
    bucket_horizontal,
    bucket_vertical,
):
    seq, width = inputs.shape
    local = weight_query.shape[1]
    heads = table_horizontal.shape[1]
    hidden = weight_up.shape[1]
    half = hidden // 2
    segs = bucket_horizontal.shape[1]
    bins = table_horizontal.shape[0]
    shard = lax.axis_index("mp")
    pages = lax.axis_index("dp")
    side = pages % 2

    def swap(value, axis, bit):
        count = dp_count if axis == "dp" else mp_count
        return lax.ppermute(value, axis, [(i, i ^ bit) for i in range(count)])

    def core(value):
        return swap(value, "mp", 1)

    def across(value):
        return swap(value, "mp", 2)

    def beside(value):
        return swap(value, "dp", 1)

    def own_page(value):
        return lax.dynamic_index_in_dim(value, shard, 0, keepdims=False)

    def row(value):
        return value.reshape(1, -1)

    def by_side(one, other):
        return jnp.where(side == 0, one, other)

    small = jnp.concatenate(
        [
            jnp.concatenate([table_horizontal.T, table_vertical.T], axis=1).reshape(-1),
            bias_query,
            bias_value,
        ]
    )
    small_high, small_low = halves(small)
    rest = jnp.zeros((EXTRA - 2, width), BF16)
    small_rows = jnp.concatenate([row(small_high), row(small_low), rest], axis=0)
    piece_a = jnp.concatenate([weight_query.T, weight_key.T, small_rows], axis=0)
    piece_b = jnp.concatenate([weight_value.T, weight_out, small_rows], axis=0)

    def up_piece(start):
        part = lax.dynamic_slice_in_dim(weight_up, start, half, axis=1)
        high, low = halves(lax.dynamic_slice_in_dim(bias_up, start, half, axis=0))
        line = row(jnp.concatenate([high, low]))
        return jnp.concatenate(
            [
                jnp.concatenate([part[:half], part[half:]], axis=1),
                line,
                jnp.zeros((EXTRA - 1, width), BF16),
            ],
            axis=0,
        )

    first_at, second_at = side * half, (1 - side) * half
    ups = [[up_piece(first_at), up_piece(second_at)]]
    downs = [
        [
            lax.dynamic_slice_in_dim(weight_down, first_at, half, axis=0),
            lax.dynamic_slice_in_dim(weight_down, second_at, half, axis=0),
        ]
    ]
    far_0 = across(by_side(piece_a, piece_b))
    far_up_0 = across(ups[0][0])
    far_down_0 = across(downs[0][0])
    far_1 = beside(far_0)
    far_up_1 = beside(far_up_0)
    far_down_1 = beside(far_down_0)
    pieces = [(piece_a, piece_b), (core(piece_a), core(piece_b))]
    far = (by_side(far_0, far_1), by_side(far_1, far_0))
    pieces.append(far)
    pieces.append((core(far[0]), core(far[1])))
    ups.append([core(ups[0][0]), core(ups[0][1])])
    downs.append([core(downs[0][0]), core(downs[0][1])])
    ups.append([far_up_0, far_up_1])
    downs.append([far_down_0, far_down_1])
    ups.append([core(far_up_0), core(far_up_1)])
    downs.append([core(far_down_0), core(far_down_1)])

    xn, member, negative, index_h, index_v = call(
        start_body,
        [
            struct((seq, width), BF16),
            struct((segs, seq), BF16),
            struct((EXTRA, seq), BF16),
            struct((segs, seq), jnp.int32),
            struct((segs, seq), jnp.int32),
        ],
        "first_norm",
        flops=seq * width * 10,
    )(
        inputs,
        row(gain_attn),
        row(shift_attn),
        row(own_page(segment)),
        row(own_page(valid)),
        own_page(bucket_horizontal),
        own_page(bucket_vertical),
    )
    attn_flops = 2 * seq * width * 4 * local + heads * seq * seq * 256 * 2 * 2
    kept = []
    acc = None
    for k in range(4):
        first = acc is None
        given = [xn, *pieces[k], index_h, index_v, member, negative] + ([] if first else [acc])
        qkv, ctx, lse, pos, acc = call(
            functools.partial(attn_body, first),
            [
                struct((3 * local, seq), BF16),
                struct((local, seq), BF16),
                struct((8, seq), F32),
                struct((2 * segs * heads, seq), BF16),
                struct((seq, width), F32),
            ],
            "attn_%d" % k,
            flops=attn_flops,
            transcendentals=heads * seq * seq,
        )(*given)
        kept.append((qkv, ctx, lse, pos))
    middle, normed_mlp = call(
        middle_body,
        [struct((seq, width), F32), struct((seq, width), BF16)],
        "second_norm",
        flops=seq * width * 10,
    )(inputs, acc, row(bias_out), row(gain_mlp), row(shift_mlp))

    down_acc = back_acc = None
    mlp_grads = []
    up_sums = []
    for k in range(4):
        first = down_acc is None
        given = [normed_mlp, cotangent, ups[k][0], downs[k][0], ups[k][1], downs[k][1]]
        given += [] if first else [down_acc, back_acc]
        down_acc, back_acc, grad_0, grad_1, sums = call(
            functools.partial(mlp_body, first),
            [
                struct((seq, width), F32),
                struct((seq, width), F32),
                struct((2 * half, width), BF16),
                struct((2 * half, width), BF16),
                struct((8, hidden), F32),
            ],
            "mlp_%d" % k,
            flops=2 * 6 * seq * width * hidden,
            transcendentals=2 * seq * hidden,
        )(*given)
        mlp_grads.append((grad_0, grad_1))
        up_sums.append(sums[0])

    result, grad_middle, grad_attn, turn_rows = call(
        turn_body,
        [
            struct((seq, width), BF16),
            struct((seq, width), F32),
            struct((seq, width), BF16),
            struct((8, width), F32),
        ],
        "turn",
        flops=seq * width * 20,
    )(middle, down_acc, row(bias_down), back_acc, cotangent, row(gain_mlp))

    acc = None
    attn_grads = [None] * 4
    for k in (2, 3, 1, 0):
        first = acc is None
        given = [xn, grad_attn, *pieces[k], *kept[k], member, negative]
        given += [] if first else [acc]
        grad_a, grad_b, acc, sums, seg_grad, _ = call(
            functools.partial(attn_back_body, first),
            [
                struct((2 * local, width), BF16),
                struct((2 * local, width), BF16),
                struct((seq, width), F32),
                struct((8, 3 * local), F32),
                struct((heads, segs, segs), F32),
                struct((3 * local, seq), BF16),
            ],
            "attn_back_%d" % k,
            flops=2 * attn_flops,
            transcendentals=heads * seq * seq,
        )(*given)
        attn_grads[k] = (grad_a, grad_b, sums[0], seg_grad)
    grad_inputs, end_rows = call(
        end_body,
        [struct((seq, width), BF16), struct((8, width), F32)],
        "end",
        flops=seq * width * 20,
    )(inputs, acc, grad_middle, row(gain_attn))

    def chip_sums(parts):
        near = parts[0] + core(parts[1])
        off = parts[2] + core(parts[3])
        return near + across(off)

    def groups_sum(part):
        bits = [1 << b for b in range(1, dp_count.bit_length() - 1)]
        for bit in bits:
            size = part.shape[0] // 2
            mine = (pages // bit) % 2
            keep = lax.dynamic_slice_in_dim(part, mine * size, size, axis=0)
            give = lax.dynamic_slice_in_dim(part, (1 - mine) * size, size, axis=0)
            part = keep + swap(give, "dp", bit)
        for bit in reversed(bits):
            mine = (pages // bit) % 2
            other = swap(part, "dp", bit)
            part = jnp.concatenate(
                [jnp.where(mine == 0, part, other), jnp.where(mine == 0, other, part)], axis=0
            )
        return part

    def shard_total(one, other):
        total = groups_sum(one + beside(other))
        total_other = beside(total)
        return by_side(total, total_other).astype(F32), by_side(total_other, total).astype(F32)

    mlp_chip = [chip_sums([mlp_grads[k][n] for k in range(4)]) for n in (1, 0)]
    mlp_low, mlp_high = shard_total(mlp_chip[1], mlp_chip[0])
    attn_a = chip_sums([attn_grads[k][0] for k in range(4)])
    attn_b = chip_sums([attn_grads[k][1] for k in range(4)])
    attn_low, attn_high = shard_total(by_side(attn_a, attn_b), by_side(attn_b, attn_a))

    grad_up = jnp.concatenate(
        [
            jnp.concatenate([mlp_low[:half, :half], mlp_high[:half, :half]], axis=1),
            jnp.concatenate([mlp_low[:half, half:], mlp_high[:half, half:]], axis=1),
        ],
        axis=0,
    )
    grad_down = jnp.concatenate([mlp_low[half:], mlp_high[half:]], axis=0)

    bin_index = jnp.arange(bins, dtype=jnp.int32)[:, None, None]
    seg_all = jnp.stack([attn_grads[k][3] for k in range(4)])
    flat = seg_all.reshape(4 * heads, segs * segs)

    def table_grad(bucket):
        hot = (bucket.T[None] == bin_index).astype(F32).reshape(bins, segs * segs)
        return jnp.einsum("hp,bp->hb", flat, hot, precision=lax.Precision.HIGHEST)

    grad_th = table_grad(own_page(bucket_horizontal)).reshape(4, -1)
    grad_tv = table_grad(own_page(bucket_vertical)).reshape(4, -1)
    sums = jnp.stack([attn_grads[k][2] for k in range(4)])
    up_rows = jnp.stack(up_sums)
    up_rows = jnp.concatenate(
        [by_side(up_rows[:, :half], up_rows[:, half:]), by_side(up_rows[:, half:], up_rows[:, :half])],
        axis=1,
    )
    by_shard = jnp.concatenate([sums, up_rows, grad_th, grad_tv], axis=1)
    by_shard = jnp.concatenate(
        [lax.dynamic_slice_in_dim(by_shard, shard ^ k, 1, axis=0) for k in range(4)], axis=0
    )
    flat_small = jnp.concatenate(
        [by_shard.reshape(-1), turn_rows[:4].reshape(-1), end_rows[:2].reshape(-1)]
    )
    flat_small = lax.psum(flat_small, ("dp", "mp"))
    line = by_shard.shape[1]
    mine = lax.dynamic_slice_in_dim(flat_small, shard * line, line, axis=0)
    shared = flat_small[4 * line:].reshape(6, width)
    at = 3 * local + hidden
    count = heads * bins
    return (
        result,
        grad_inputs,
        shared[4],
        shared[5],
        attn_low[:local].T,
        mine[:local],
        attn_low[local:].T,
        attn_high[:local].T,
        mine[2 * local:3 * local],
        mine[at:at + count].reshape(heads, bins).T,
        mine[at + count:at + 2 * count].reshape(heads, bins).T,
        attn_high[local:],
        shared[0],
        shared[1],
        shared[2],
        grad_up,
        mine[3 * local:at],
        grad_down,
        shared[3],
    )


def solution(mesh):
    rows = P(("dp", "mp"), None)
    columns = P(None, "mp")
    split = P("mp")
    placed = (
        rows, rows, P(), P(), columns, split, columns, columns, split, columns, columns,
        P("mp", None), P(), P(), P(), columns, split, P("mp", None), P(),
        P("dp", None), P("dp", None), P("dp", None, None), P("dp", None, None),
    )
    given = (
        rows, rows, P(), P(), columns, split, columns, columns, split, columns, columns,
        P("mp", None), P(), P(), P(), columns, split, P("mp", None), P(),
    )
    return jax.shard_map(
        functools.partial(on_device, mesh.shape["dp"], mesh.shape["mp"]),
        mesh=mesh,
        in_specs=placed,
        out_specs=given,
        check_vma=False,
    )
```

```python
import functools

import jax
import jax.numpy as jnp
from jax import lax
from jax.experimental import pallas as pl
from jax.experimental.pallas import tpu as pltpu
from jax.sharding import PartitionSpec as P

EPSILON = 1e-05
NEGATIVE = -1e30
HEAD = 64
EXTRA = 16
F32 = jnp.float32
BF16 = jnp.bfloat16
LIMIT = 16 * 1024 * 1024
SCALE = 30

NN = (((1,), (0,)), ((), ()))
NT = (((1,), (1,)), ((), ()))
TN = (((0,), (0,)), ((), ()))


def mm(left, right, dims=NN):
    return lax.dot_general(left, right, dims, preferred_element_type=F32)


def struct(shape, dtype):
    return jax.ShapeDtypeStruct(shape, dtype)


class Own:
    def __init__(self, value, cuts=()):
        self.value = value
        self.cuts = cuts


class Loaded:
    def __init__(self, source, scratch, sems, cuts):
        self.scratch = scratch
        self.shape = scratch.shape
        edges = [0, *cuts, scratch.shape[0]]
        self.parts = []
        for n, (low, high) in enumerate(zip(edges, edges[1:])):
            here = pl.ds(low, high - low)
            copy = pltpu.make_async_copy(source.at[here], scratch.at[here], sems[n])
            copy.start()
            self.parts.append((low, high, copy))

    def wait(self, low, high):
        for part in list(self.parts):
            if part[0] < high and low < part[1]:
                part[2].wait()
                self.parts.remove(part)

    def __getitem__(self, at):
        first = at[0] if isinstance(at, tuple) else at
        if isinstance(first, slice):
            self.wait(first.start or 0, self.shape[0] if first.stop is None else first.stop)
        else:
            self.wait(0, self.shape[0])
        return self.scratch[at]


class Stored:
    def __init__(self, target, scratch, sem):
        self.copy = pltpu.make_async_copy(scratch, target, sem)
        self.scratch = scratch
        self.shape = scratch.shape
        self.dtype = scratch.dtype
        self.sent = False

    def __getitem__(self, at):
        return self.scratch[at]

    def __setitem__(self, at, value):
        self.scratch[at] = value

    def flush(self):
        self.copy.start()
        self.sent = True


def flush(ref):
    if isinstance(ref, Stored):
        ref.flush()


def call(body, outs, name, flops=0, transcendentals=0, scalar=False, scratch=(), alias=None, limit=LIMIT):
    def run(*args, hold=()):
        own_in = [isinstance(a, Own) for a in args]
        own_out = [isinstance(o, Own) for o in outs]
        ins = [a.value if own else a for a, own in zip(args, own_in)]
        shapes = [o.value if own else o for o, own in zip(outs, own_out)]
        moved = sum(a.size * a.dtype.itemsize for a in ins + shapes)
        count, held = len(ins), len(hold)
        total = sum(1 + len(v.cuts) for v in [*args, *outs] if isinstance(v, Own))
        copied = [v for v, own in zip(ins + shapes, own_in + own_out) if own]

        def inner(*refs):
            given, results = refs[:count], refs[count + held:count + held + len(shapes)]
            spare = refs[count + held + len(shapes):]
            slots, rest = iter(spare[:len(copied)]), spare[len(copied):]
            sems = iter(range(total))
            loaded = [
                Loaded(
                    ref, next(slots), [rest[-1].at[next(sems)] for _ in (0, *arg.cuts)], arg.cuts
                )
                if isinstance(arg, Own)
                else ref
                for ref, arg in zip(given, args)
            ]
            stored = [
                Stored(ref, next(slots), rest[-1].at[next(sems)]) if own else ref
                for ref, own in zip(results, own_out)
            ]
            body(*loaded, *stored, *(rest[:-1] if copied else rest))
            for ref in loaded:
                if isinstance(ref, Loaded):
                    ref.wait(0, ref.shape[0])
            for ref in stored:
                if isinstance(ref, Stored):
                    if not ref.sent:
                        ref.flush()
                    ref.copy.wait()

        buffers = [pltpu.VMEM(v.shape, v.dtype) for v in copied] + list(scratch)
        if copied:
            buffers.append(pltpu.SemaphoreType.DMA((total,)))
        kept = pl.BlockSpec(memory_space=pl.ANY)
        inside = pl.BlockSpec(memory_space=pltpu.VMEM)
        in_specs = [kept if own else inside for own in own_in]
        if scalar:
            in_specs[0] = pl.BlockSpec(memory_space=pltpu.SMEM)
        return pl.pallas_call(
            inner,
            out_shape=[
                (pltpu.HBM if own else pltpu.VMEM)(o.shape, o.dtype) for o, own in zip(shapes, own_out)
            ],
            in_specs=in_specs + [kept] * held,
            out_specs=[kept if own else inside for own in own_out],
            scratch_shapes=buffers,
            input_output_aliases=alias or {},
            compiler_params=pltpu.CompilerParams(vmem_limit_bytes=limit),
            cost_estimate=pl.CostEstimate(
                flops=int(flops * SCALE),
                bytes_accessed=int(moved * SCALE),
                transcendentals=int(transcendentals),
            ),
            name=name,
        )(
            *[
                v
                if scalar and n == 0
                else pltpu.with_memory_space_constraint(v, pltpu.HBM if own else pltpu.VMEM)
                for n, (v, own) in enumerate(zip(ins, own_in))
            ],
            *hold,
        )

    return run


def line(ref):
    value = ref[...]
    return value if value.ndim == 2 else value.reshape(1, value.shape[0])


def halves(values):
    high = values.astype(BF16)
    return high, (values - high.astype(F32)).astype(BF16)


def pack_attn_body(place_ref, wq_ref, wk_ref, wv_ref, wo_ref, th_ref, tv_ref, bq_ref, bv_ref,
                   all_ref, send_ref):
    local = wq_ref.shape[0]
    heads = th_ref.shape[0]
    piece = 2 * local + EXTRA
    th, tv = th_ref[...], tv_ref[...]
    parts = []
    for m in range(heads):
        parts += [th[m:m + 1], tv[m:m + 1]]
    high, low = halves(jnp.concatenate(parts + [line(bq_ref), line(bv_ref)], axis=1))
    which = lax.broadcasted_iota(jnp.int32, (EXTRA, high.shape[1]), 0)
    extra = jnp.where(which == 0, high.astype(F32), jnp.where(which == 1, low.astype(F32), 0.0))
    extra = extra.astype(BF16)
    side = place_ref[0, 0]
    for n, (one_ref, two_ref) in enumerate(((wq_ref, wv_ref), (wk_ref, wo_ref))):
        one, two = one_ref[...], two_ref[...]
        all_ref[n * local:(n + 1) * local, :] = one
        all_ref[piece + n * local:piece + (n + 1) * local, :] = two
        send_ref[n * local:(n + 1) * local, :] = jnp.where(side == 0, one, two)
    all_ref[2 * local:piece, :] = extra
    all_ref[piece + 2 * local:, :] = extra
    send_ref[2 * local:, :] = extra


def pack_mlp_body(place_ref, up_ref, bias_ref, down_ref, all_ref, up_send_ref, down_send_ref):
    half = down_ref.shape[0] // 2
    piece = 2 * half + EXTRA
    own = place_ref[0, 0] == 0
    bias = line(bias_ref)
    which = lax.broadcasted_iota(jnp.int32, (EXTRA, half), 0) == 0
    for n in (0, 1):
        one, two = pl.ds(n * half, half), pl.ds((1 - n) * half, half)
        at = n * piece
        left = jnp.where(own, up_ref[0:half, one], up_ref[0:half, two])
        right = jnp.where(own, up_ref[half:, one], up_ref[half:, two])
        high, low = halves(jnp.where(own, bias[:, n * half:(n + 1) * half], bias[:, (1 - n) * half:(2 - n) * half]))
        high = jnp.where(which, high.astype(F32), 0.0).astype(BF16)
        low = jnp.where(which, low.astype(F32), 0.0).astype(BF16)
        all_ref[at:at + half, 0:half] = left
        all_ref[at:at + half, half:] = right
        all_ref[at + half:at + half + EXTRA, 0:half] = high
        all_ref[at + half:at + half + EXTRA, half:] = low
        down = jnp.where(own, down_ref[one, :], down_ref[two, :])
        all_ref[at + half + EXTRA:at + piece, :] = down
        if n == 0:
            up_send_ref[0:half, 0:half] = left
            up_send_ref[0:half, half:] = right
            up_send_ref[half:, 0:half] = high
            up_send_ref[half:, half:] = low
            flush(up_send_ref)
            down_send_ref[...] = down
            flush(down_send_ref)


def start_body(place_ref, x_ref, gain_ref, shift_ref, seg_ref, valid_ref, bh_ref, bv_ref,
               xn_ref, mt_ref, neg_ref, ih_ref, iv_ref):
    x = x_ref[...].astype(F32)
    mean = jnp.mean(x, axis=1, keepdims=True)
    cen = x - mean
    var = jnp.mean(cen * cen, axis=1, keepdims=True)
    xn_ref[...] = (cen * lax.rsqrt(var + EPSILON) * line(gain_ref) + line(shift_ref)).astype(BF16)
    segs = mt_ref.shape[0]
    seq = x.shape[0]
    rows = lax.broadcasted_iota(jnp.int32, (segs, seq), 0)
    top = lax.broadcasted_iota(jnp.int32, (EXTRA, seq), 0) == 0
    for p in (0, 1):
        page = place_ref[0, 1 + p]
        here = pl.ds(p * seq, seq)
        member = jnp.where(rows == seg_ref[pl.ds(page, 1), :], 1.0, 0.0).astype(BF16)
        mt_ref[:, here] = member
        masked = jnp.where(valid_ref[pl.ds(page, 1), :] > 0, 0.0, NEGATIVE)
        neg_ref[:, here] = jnp.where(top, masked, 0.0).astype(BF16)
        bh, bv = bh_ref[page].astype(F32).astype(BF16), bv_ref[page].astype(F32).astype(BF16)
        ih_ref[:, here] = mm(bh, member, TN).astype(jnp.int32)
        iv_ref[:, here] = mm(bv, member, TN).astype(jnp.int32) + segs


def lookup(table, index):
    rows, seq = index.shape
    spread = jnp.broadcast_to(table, (rows, 128))
    parts = [
        jnp.take_along_axis(
            spread, index[:, at:at + 128], axis=1, mode="promise_in_bounds"
        )
        for at in range(0, seq, 128)
    ]
    return jnp.concatenate(parts, axis=1)


def attn_body(first, *refs):
    if first:
        w_ref, ih_ref, iv_ref, mt_ref, neg_ref = refs[2:7]
        given = (None, None)
        qkv_ref, ctx_ref, lse_ref, bias_ref, *outs = refs[7:]
    else:
        place_ref, own_ref, other_ref = refs[0], refs[3], refs[4]
        ih_ref, iv_ref, mt_ref, neg_ref = refs[5:9]
        given = refs[9:11]
        qkv_ref, ctx_ref, lse_ref, bias_ref, *outs, w_ref = refs[11:]
        refs = refs[1:]
        low = place_ref[0, 0] == 0
        own, other = own_ref[...], other_ref[...]
        size = own.shape[0]
        w_ref[0:size, :] = jnp.where(low, own, other)
        w_ref[size:, :] = jnp.where(low, other, own)
        flush(w_ref)
    width = ctx_ref.shape[0]
    heads = width // HEAD
    segs = mt_ref.shape[0]
    seq = refs[0].shape[0]
    second = 2 * width + EXTRA
    extra = w_ref[2 * width:second, :]
    pick = jnp.where(lax.broadcasted_iota(jnp.int32, (EXTRA, seq), 0) < 2, 1.0, 0.0).astype(BF16)
    bias = mm(extra[:, heads * 128:heads * 128 + 2 * width], pick, TN)
    tables = extra[0:1, :].astype(F32) + extra[1:2, :].astype(F32)
    ones = jnp.ones((EXTRA, seq), BF16)
    for p in (0, 1):
        xn = refs[p][...]
        here = pl.ds(p * seq, seq)
        qk = mm(w_ref[0:2 * width, :], xn, NT)
        v = mm(w_ref[second:second + width, :], xn, NT)
        qkv_ref[0:width, here] = ((qk[0:width] + bias[0:width]) * 0.125).astype(BF16)
        qkv_ref[width:2 * width, here] = qk[width:].astype(BF16)
        qkv_ref[2 * width:, here] = (v + bias[width:]).astype(BF16)
    flush(qkv_ref)
    for p in (0, 1):
        here = pl.ds(p * seq, seq)
        member = mt_ref[:, here]
        for m in range(heads):
            table = tables[:, 128 * m:128 * m + 128]
            pos = lookup(table, ih_ref[:, here]) + lookup(table, iv_ref[:, here])
            high, low = halves(pos)
            bias_ref[2 * segs * m:2 * segs * m + segs, here] = high
            bias_ref[2 * segs * m + segs:2 * segs * (m + 1), here] = low
            at = HEAD * m
            q_aug = jnp.concatenate([qkv_ref[at:at + HEAD, here], high, low, ones], axis=0)
            k_aug = jnp.concatenate(
                [qkv_ref[width + at:width + at + HEAD, here], member, member, neg_ref[:, here]],
                axis=0,
            )
            scores = mm(k_aug, q_aug, TN)
            top = jnp.max(scores, axis=0, keepdims=True)
            expo = jnp.exp(scores - top).astype(BF16)
            v_aug = jnp.concatenate(
                [qkv_ref[2 * width + at:2 * width + at + HEAD, here], ones], axis=0
            )
            summed = mm(v_aug, expo)
            total = summed[HEAD:HEAD + 1]
            ctx_ref[at:at + HEAD, here] = (summed[0:HEAD] / total).astype(BF16)
            lse_ref[m:m + 1, here] = top + jnp.log(total)
        out = mm(ctx_ref[:, here], w_ref[second + width:second + 2 * width, :], TN)
        if given[p] is not None:
            out = given[p][...] + out
        outs[p][...] = out.astype(outs[p].dtype)
    lse_ref[heads:, :] = jnp.zeros((lse_ref.shape[0] - heads, 2 * seq), F32)


def middle_body(x_ref, acc_ref, got_ref, bias_ref, gain_ref, shift_ref, mid_ref, nm_ref):
    mid = x_ref[...].astype(F32) + (acc_ref[...] + got_ref[...].astype(F32)) + line(bias_ref)
    mid_ref[...] = mid
    mean = jnp.mean(mid, axis=1, keepdims=True)
    cen = mid - mean
    var = jnp.mean(cen * cen, axis=1, keepdims=True)
    nm_ref[...] = (cen * lax.rsqrt(var + EPSILON) * line(gain_ref) + line(shift_ref)).astype(BF16)


def mlp_body(first, fused, *refs):
    nm_refs, cot_refs = refs[0:2], refs[2:4]
    at = 5 if fused else 8
    given = (None,) * 4 if first else refs[at:at + 4]
    outs = refs[at if first else at + 4:]
    accs, grads, db_ref = outs[0:4], outs[4:8], outs[8]
    half = grads[0].shape[0]
    piece = 2 * half + EXTRA
    for n in (0, 1):
        if fused:
            u_ref = d_ref = refs[4]
            up_at = n * piece
            down_at = up_at + half + EXTRA
        else:
            u_ref, d_ref = refs[4 + 2 * n:6 + 2 * n]
            up_at = down_at = 0
        extra = u_ref[up_at + half:up_at + half + EXTRA, :].astype(F32)
        bias = extra[0:1, 0:half] + extra[0:1, half:]
        up_left = u_ref[up_at:up_at + half, 0:half]
        up_right = u_ref[up_at:up_at + half, half:]
        down = d_ref[down_at:down_at + half, :]
        total = None
        for p in (0, 1):
            nm_left, nm_right = nm_refs[p][:, 0:half], nm_refs[p][:, half:]
            cot = cot_refs[p][...]
            upper = mm(nm_left, up_left) + mm(nm_right, up_right) + bias
            cdf = 0.5 + 0.5 * lax.erf(upper * 0.7071067811865476)
            pdf = jnp.exp(upper * upper * -0.5) * 0.3989422804014327
            hidden = (upper * cdf).astype(BF16)
            grad_hidden = mm(cot, down, NT)
            grad_upper = (grad_hidden * (cdf + upper * pdf)).astype(BF16)
            sums_now = (
                mm(nm_left, grad_upper, TN),
                mm(nm_right, grad_upper, TN),
                mm(hidden, cot, TN),
                jnp.sum(grad_upper.astype(F32), axis=0, keepdims=True),
            )
            total = sums_now if total is None else [a + b for a, b in zip(total, sums_now)]
            down_ref, back_ref = accs[p], accs[2 + p]
            base_down, base_back = (given[p], given[2 + p]) if n == 0 else (down_ref, back_ref)
            down_out = mm(hidden, down)
            back_left = mm(grad_upper, up_left, NT)
            back_right = mm(grad_upper, up_right, NT)
            if base_down is not None:
                down_out = base_down[...].astype(F32) + down_out
                back_left = base_back[:, 0:half].astype(F32) + back_left
                back_right = base_back[:, half:].astype(F32) + back_right
            down_ref[...] = down_out.astype(down_ref.dtype)
            back_ref[:, 0:half] = back_left.astype(back_ref.dtype)
            back_ref[:, half:] = back_right.astype(back_ref.dtype)
        up_ref, dn_ref = grads[2 * n:2 * n + 2]
        up_ref[:, 0:half] = total[0].astype(BF16)
        up_ref[:, half:] = total[1].astype(BF16)
        flush(up_ref)
        dn_ref[...] = total[2].astype(BF16)
        flush(dn_ref)
        db_ref[0:1, n * half:(n + 1) * half] = total[3]
    db_ref[1:, :] = jnp.zeros((db_ref.shape[0] - 1, 2 * half), F32)


def turn_body(mid_ref, down_ref, down_got_ref, bias_ref, back_ref, back_got_ref, cot_ref, gain_ref,
              res_ref, gmid_ref, ga_ref, rows_ref):
    mid = mid_ref[...]
    down = down_ref[...] + down_got_ref[...].astype(F32)
    res_ref[...] = (mid + down + line(bias_ref)).astype(BF16)
    mean = jnp.mean(mid, axis=1, keepdims=True)
    cen = mid - mean
    var = jnp.mean(cen * cen, axis=1, keepdims=True)
    rstd = lax.rsqrt(var + EPSILON)
    n = cen * rstd
    back = back_ref[...] + back_got_ref[...].astype(F32)
    q = back * line(gain_ref)
    cot = cot_ref[...].astype(F32)
    mean_q = jnp.mean(q, axis=1, keepdims=True)
    mean_qn = jnp.mean(q * n, axis=1, keepdims=True)
    grad = cot + rstd * (q - mean_q - n * mean_qn)
    gmid_ref[...] = grad
    ga_ref[...] = grad.astype(BF16)
    rows_ref[0:1, :] = jnp.sum(grad, axis=0, keepdims=True)
    rows_ref[1:2, :] = jnp.sum(back * n, axis=0, keepdims=True)
    rows_ref[2:3, :] = jnp.sum(back, axis=0, keepdims=True)
    rows_ref[3:4, :] = jnp.sum(cot, axis=0, keepdims=True)
    rows_ref[4:, :] = jnp.zeros((rows_ref.shape[0] - 4, rows_ref.shape[1]), F32)


def attn_back_body(first, *refs):
    place_ref, xn_refs, ga_refs = refs[0], refs[1:3], refs[3:5]
    w_ref, qkv_ref, ctx_ref, lse_ref, bias_ref, mt_ref, neg_ref = refs[5:12]
    given = (None, None) if first else refs[12:14]
    *backs, kept_ref, other_ref, sums_ref, seg_ref, dqkv_ref = refs[12 if first else 14:]
    width = ctx_ref.shape[0]
    heads = width // HEAD
    seq = xn_refs[0].shape[0]
    segs = mt_ref.shape[0]
    second = 2 * width + EXTRA
    ones = jnp.ones((EXTRA, seq), BF16)
    grad_out = None
    for p in (0, 1):
        here = pl.ds(p * seq, seq)
        ga = ga_refs[p][...]
        member = mt_ref[:, here]
        grad_ctx = mm(w_ref[second + width:second + 2 * width, :], ga, NT).astype(BF16)
        part = mm(ctx_ref[:, here], ga)
        grad_out = part if p == 0 else grad_out + part
        for m in range(heads):
            at = HEAD * m
            q = qkv_ref[at:at + HEAD, here]
            k = qkv_ref[width + at:width + at + HEAD, here]
            v = qkv_ref[2 * width + at:2 * width + at + HEAD, here]
            g = grad_ctx[at:at + HEAD]
            q_aug = jnp.concatenate(
                [q, bias_ref[2 * segs * m:2 * segs * (m + 1), here], ones], axis=0
            )
            k_aug = jnp.concatenate([k, member, member, neg_ref[:, here]], axis=0)
            scores = mm(k_aug, q_aug, TN)
            probs = jnp.exp(scores - lse_ref[m:m + 1, here])
            grad_probs = mm(v, g, TN)
            delta = jnp.sum(probs * grad_probs, axis=0, keepdims=True)
            grad_scores = (probs * (grad_probs - delta)).astype(BF16)
            grad_v = mm(g, probs.astype(BF16), NT)
            dqkv_ref[2 * width + at:2 * width + at + HEAD, here] = grad_v.astype(BF16)
            dqkv_ref[width + at:width + at + HEAD, here] = mm(q, grad_scores, NT).astype(BF16)
            both = mm(jnp.concatenate([k, member], axis=0), grad_scores)
            dqkv_ref[at:at + HEAD, here] = both[0:HEAD].astype(BF16) * jnp.asarray(0.125, BF16)
            high, low = halves(both[HEAD:])
            seg_ref[p * heads + m] = mm(member, high, NT) + mm(member, low, NT)
    grads = mm(dqkv_ref[:, 0:seq], xn_refs[0][...]) + mm(dqkv_ref[:, seq:], xn_refs[1][...])
    grads = jnp.concatenate([grads, grad_out], axis=0).astype(BF16)
    low = place_ref[0, 0] == 0
    kept_ref[...] = jnp.where(low, grads[0:2 * width], grads[2 * width:])
    flush(kept_ref)
    other_ref[...] = jnp.where(low, grads[2 * width:], grads[0:2 * width])
    flush(other_ref)
    for p in (0, 1):
        here = pl.ds(p * seq, seq)
        back = mm(dqkv_ref[0:2 * width, here], w_ref[0:2 * width, :], TN)
        back = back + mm(dqkv_ref[2 * width:, here], w_ref[second:second + width, :], TN)
        if given[p] is not None:
            back = given[p][...] + back
        backs[p][...] = back.astype(backs[p].dtype)
    sums_ref[...] = mm(jnp.ones((8, 2 * seq), BF16), dqkv_ref[...], NT)


def sum_body(counts, *refs):
    total = sum(counts)
    outs = refs[total:]
    at = 0
    for count, out in zip(counts, outs):
        value = refs[at][...].astype(F32)
        for ref in refs[at + 1:at + count]:
            value = value + ref[...].astype(F32)
        out[...] = value.astype(out.dtype)
        at += count


def sums(name, *groups, hold=()):
    outs = [struct(group[0].shape, group[0].dtype) for group in groups]
    body = functools.partial(sum_body, [len(group) for group in groups])
    flat = [value for group in groups for value in group]
    return call(body, outs, name)(*flat, hold=hold)


def split_body(which, place_ref, *refs):
    *parts, keep_ref, give_ref = refs
    size = keep_ref.shape[0]
    value = parts[0][...].astype(F32)
    for ref in parts[1:]:
        value = value + ref[...].astype(F32)
    low = place_ref[0, which] == 0
    one, two = value[0:size], value[size:]
    keep_ref[...] = jnp.where(low, one, two).astype(BF16)
    give_ref[...] = jnp.where(low, two, one).astype(BF16)


def join_body(which, place_ref, own_ref, other_ref, out_ref):
    size = own_ref.shape[0]
    low = place_ref[0, which] == 0
    own, other = own_ref[...], other_ref[...]
    out_ref[0:size, :] = jnp.where(low, own, other)
    out_ref[size:, :] = jnp.where(low, other, own)


def end_body(x_ref, back_ref, got_ref, gmid_ref, gain_ref, gx_ref, rows_ref):
    x = x_ref[...].astype(F32)
    mean = jnp.mean(x, axis=1, keepdims=True)
    cen = x - mean
    var = jnp.mean(cen * cen, axis=1, keepdims=True)
    rstd = lax.rsqrt(var + EPSILON)
    n = cen * rstd
    back = back_ref[...] + got_ref[...].astype(F32)
    q = back * line(gain_ref)
    mean_q = jnp.mean(q, axis=1, keepdims=True)
    mean_qn = jnp.mean(q * n, axis=1, keepdims=True)
    gx_ref[...] = (gmid_ref[...] + rstd * (q - mean_q - n * mean_qn)).astype(BF16)
    rows_ref[0:1, :] = jnp.sum(back * n, axis=0, keepdims=True)
    rows_ref[1:2, :] = jnp.sum(back, axis=0, keepdims=True)
    rows_ref[2:, :] = jnp.zeros((rows_ref.shape[0] - 2, rows_ref.shape[1]), F32)


def small_body(place_ref, up_near_ref, up_far_ref, sums_near_ref, sums_far_ref, seg_near_ref,
               seg_far_ref, bh_ref, bv_ref, turn_ref, end_ref, out_ref):
    count, segs, _ = seg_near_ref.shape
    heads = count // 2
    bins = lax.broadcasted_iota(jnp.int32, (segs, segs), 0)
    total = jnp.zeros((2 * EXTRA, 2 * segs), F32)
    for p in (0, 1):
        page = place_ref[0, 1 + p]
        bh, bv = bh_ref[page], bv_ref[page]
        own = pl.ds(p * heads, heads)
        for s in range(segs):
            both = jnp.concatenate(
                [
                    seg_near_ref[own, s, :],
                    seg_far_ref[own, s, :],
                    jnp.zeros((EXTRA - 2 * heads, segs), F32),
                ],
                axis=0,
            )
            hot = jnp.concatenate(
                [
                    jnp.where(bins == bh[s:s + 1, :], 1.0, 0.0),
                    jnp.where(bins == bv[s:s + 1, :], 1.0, 0.0),
                ],
                axis=0,
            ).astype(BF16)
            total = total + mm(jnp.concatenate(halves(both), axis=0), hot, NT)
    tables = total[0:EXTRA] + total[EXTRA:]
    low = place_ref[0, 0] == 0
    out_ref[...] = jnp.zeros(out_ref.shape, F32)
    width = sums_near_ref.shape[1] // 3
    half = up_near_ref.shape[1] // 2
    for k, (ups, sums_in) in enumerate(
        ((up_near_ref, sums_near_ref), (up_far_ref, sums_far_ref))
    ):
        one, two = ups[0:1, 0:half], ups[0:1, half:]
        out_ref[2 * k:2 * k + 1, 0:half] = jnp.where(low, one, two)
        out_ref[2 * k:2 * k + 1, half:] = jnp.where(low, two, one)
        parts = [sums_in[0:1, 0:width], sums_in[0:1, 2 * width:]]
        parts += [tables[k * heads + m:k * heads + m + 1] for m in range(heads)]
        out_ref[2 * k + 1:2 * k + 2, :] = jnp.concatenate(parts, axis=1)
    out_ref[4:8, :] = turn_ref[0:4, :]
    out_ref[8:10, :] = end_ref[0:2, :]


def small_core_body(own_ref, got_ref, out_ref):
    out_ref[...] = own_ref[...]
    out_ref[4:10, :] = own_ref[4:10, :] + got_ref[4:10, :]


def small_across_body(own_ref, got_ref, out_ref):
    out_ref[...] = jnp.zeros(out_ref.shape, F32)
    out_ref[0:2, :] = own_ref[0:2, :] + got_ref[2:4, :]
    out_ref[4:10, :] = own_ref[4:10, :] + got_ref[4:10, :]


def small_end_body(own_ref, got_ref, up_ref, q_ref, v_ref, th_ref, tv_ref, *vector_refs):
    value = own_ref[...] + got_ref[...]
    width = q_ref.shape[0]
    heads, bins = th_ref.shape
    up_ref[...] = value[0]
    q_ref[...] = value[1, 0:width]
    v_ref[...] = value[1, width:2 * width]
    for m in range(heads):
        at = 2 * width + 2 * bins * m
        th_ref[m:m + 1, :] = value[1:2, at:at + bins]
        tv_ref[m:m + 1, :] = value[1:2, at + bins:at + 2 * bins]
    for n, ref in enumerate(vector_refs):
        ref[...] = value[4 + n]


def unpack_mlp_body(place_ref, u_ref, d_ref, uo_ref, do_ref, up_ref, down_ref):
    half = u_ref.shape[0]
    for at in (0, 1):
        own = place_ref[0, 0] == at
        here = pl.ds(at * half, half)
        up = jnp.where(own, u_ref[...].astype(F32), uo_ref[...].astype(F32))
        up_ref[0:half, here] = up[:, 0:half]
        up_ref[half:, here] = up[:, half:]
        down_ref[here, :] = jnp.where(own, d_ref[...].astype(F32), do_ref[...].astype(F32))


def unpack_attn_body(place_ref, own_ref, other_ref, q_ref, k_ref, v_ref, o_ref):
    local = q_ref.shape[0]
    low = place_ref[0, 0] == 0
    own, other = own_ref[...].astype(F32), other_ref[...].astype(F32)
    one, two = jnp.where(low, own, other), jnp.where(low, other, own)
    q_ref[...] = one[0:local]
    k_ref[...] = one[local:]
    v_ref[...] = two[0:local]
    o_ref[...] = two[local:]


def order_body(*refs):
    pass


def gate(inside, outside, *others):
    spec = pl.BlockSpec(memory_space=pl.ANY)
    spaces = [pltpu.VMEM] * len(inside) + [pltpu.HBM] * len(outside)
    values = [*inside, *outside]
    return pl.pallas_call(
        order_body,
        out_shape=[space(v.shape, v.dtype) for space, v in zip(spaces, values)],
        in_specs=[spec] * (len(values) + len(others)),
        out_specs=[spec] * len(values),
        input_output_aliases={n: n for n in range(len(values))},
        compiler_params=pltpu.CompilerParams(vmem_limit_bytes=2**20),
        name="order",
    )(
        *[pltpu.with_memory_space_constraint(v, space) for space, v in zip(spaces, values)],
        *others,
    )


def on_device(
    dp_count,
    mp_count,
    inputs,
    cotangent,
    gain_attn,
    shift_attn,
    weight_query,
    bias_query,
    weight_key,
    weight_value,
    bias_value,
    table_horizontal,
    table_vertical,
    weight_out,
    bias_out,
    gain_mlp,
    shift_mlp,
    weight_up,
    bias_up,
    weight_down,
    bias_down,
    segment,
    valid,
    bucket_horizontal,
    bucket_vertical,
):
    seq, width = inputs.shape
    local = weight_query.shape[1]
    heads = table_horizontal.shape[1]
    hidden = weight_up.shape[1]
    half = hidden // 2
    segs = bucket_horizontal.shape[1]
    bins = table_horizontal.shape[0]
    shard = lax.axis_index("mp")
    pages = lax.axis_index("dp")
    bits = [1 << b for b in range(1, dp_count.bit_length() - 1)]
    place = jnp.stack([pages % 2, shard, shard ^ 1] + [(pages // bit) % 2 for bit in bits])
    place = place.astype(jnp.int32).reshape(1, -1)
    scalar = functools.partial(call, scalar=True)

    def swap(value, axis, bit):
        count = dp_count if axis == "dp" else mp_count
        return lax.ppermute(value, axis, [(i, i ^ bit) for i in range(count)])

    def core(value):
        return swap(value, "mp", 1)

    def across(value):
        return swap(value, "mp", 2)

    def beside(value):
        return swap(value, "dp", 1)

    piece = struct((2 * local + EXTRA, width), BF16)
    both = struct((4 * local + 2 * EXTRA, width), BF16)
    near_w, attn_send = scalar(pack_attn_body, [both, piece], "pack_attn")(
        place, Own(weight_query.T), Own(weight_key.T), Own(weight_value.T), Own(weight_out),
        Own(table_horizontal.T), Own(table_vertical.T), bias_query, bias_value,
    )
    x_attn = across(attn_send)
    cot_got = core(cotangent)
    mlp_w, up_send, down_send = scalar(
        pack_mlp_body,
        [
            Own(struct((2 * (2 * half + EXTRA), width), BF16)),
            Own(struct((half + EXTRA, width), BF16)),
            Own(struct((half, width), BF16)),
        ],
        "pack_mlp",
    )(place, Own(weight_up), bias_up, Own(weight_down))

    xn, member, negative, index_h, index_v = scalar(
        start_body,
        [
            struct((seq, width), BF16),
            struct((segs, 2 * seq), BF16),
            struct((EXTRA, 2 * seq), BF16),
            struct((segs, 2 * seq), jnp.int32),
            struct((segs, 2 * seq), jnp.int32),
        ],
        "first_norm",
    )(
        place, Own(inputs), gain_attn, shift_attn,
        Own(segment), Own(valid), Own(bucket_horizontal), Own(bucket_vertical), hold=[near_w]
    )
    attn_flops = 2 * (2 * seq * width * 4 * local + heads * seq * seq * 256 * 2 * 2)
    page = struct((seq, width), F32)
    page_low = struct((seq, width), BF16)
    xns = [xn, core(xn)]

    def owned(*values):
        return [Own(value) for value in values]

    saved = [
        struct((3 * local, 2 * seq), BF16),
        struct((local, 2 * seq), BF16),
        struct((8, 2 * seq), F32),
        struct((2 * segs * heads, 2 * seq), BF16),
    ]

    def mlp(weights, acc, name, hold=()):
        cuts = [half + EXTRA, 2 * half + EXTRA, 3 * half + 2 * EXTRA]
        first = acc is None
        if first:
            ins = [*nms, *owned(cotangent, cot_got), Own(weights[0], cuts)]
        else:
            ins = [*nms, *owned(cotangent, cot_got), *weights]
        outs = call(
            functools.partial(mlp_body, first, first),
            [page, page_low, page, page_low]
            + [struct((half, width), BF16)] * 4
            + [struct((8, hidden), F32)],
            name,
            flops=2 * 2 * 6 * seq * width * hidden,
            alias=None if first else {len(ins) + n: n for n in range(4)},
        )(*ins, *(acc or ()), hold=hold)
        return list(outs[0:4]), outs[4:8], outs[8]

    *kept_near, acc_0, acc_1 = call(
        functools.partial(attn_body, True), [*saved, page, page_low], "attn_near", flops=attn_flops
    )(*xns, near_w, index_h, index_v, member, negative, hold=[up_send])
    acc_0, acc_1, x_attn, up_send, down_send = gate(
        [acc_0, acc_1, x_attn], [up_send, down_send]
    )
    y_attn = beside(x_attn)
    x_up = across(up_send)
    x_attn, y_attn, x_up, down_send = gate([x_attn, y_attn, x_up], [down_send])
    y_up = beside(x_up)
    x_down = across(down_send)
    *kept_far, acc_0, acc_1, far_w = scalar(
        functools.partial(attn_body, False),
        [*saved, page, page_low, both],
        "attn_far",
        flops=attn_flops,
        alias={9: 4, 10: 5},
    )(
        place, *xns, x_attn, y_attn, index_h, index_v, member, negative, acc_0, acc_1
    )
    acc_0, acc_1, x_up, y_up, x_down = gate([acc_0, acc_1, x_up, y_up, x_down], [])
    middle, normed_mlp = call(middle_body, [page, page_low], "second_norm")(
        Own(inputs), acc_0, core(acc_1), bias_out, gain_mlp, shift_mlp
    )
    nms = [normed_mlp, core(normed_mlp)]
    y_down = beside(x_down)
    mlp_acc, near_mlp, ups_near = mlp([mlp_w], None, "mlp_near")
    near_up_0, near_down_0, near_up_1, near_down_1 = near_mlp
    *mlp_acc, y_down, near_up_1 = gate([*mlp_acc, y_down, near_up_1], [])
    near_y_up = beside(near_up_1)
    mlp_acc, far_mlp, ups_far = mlp([x_up, x_down, y_up, y_down], mlp_acc, "mlp_far")
    far_up_0, far_down_0, far_up_1, far_down_1 = far_mlp
    *mlp_acc, near_y_up, far_up_1, far_down_1 = gate(
        [*mlp_acc, near_y_up, far_up_1, far_down_1], []
    )
    y_far_up = beside(far_up_1)
    x_far_down = across(far_down_1)
    result, grad_middle, grad_attn, turn_rows = call(
        turn_body,
        [Own(page_low), page, page_low, struct((8, width), F32)],
        "turn",
    )(
        middle, mlp_acc[0], core(mlp_acc[1]), bias_down, mlp_acc[2], core(mlp_acc[3]),
        Own(cotangent), gain_mlp,
    )
    gas = [grad_attn, core(grad_attn)]

    def attn_back(weights, kept, acc, name, hold=()):
        first = acc is None
        ins = [
            place, *xns, *gas, weights, *kept, member, negative,
        ]
        outs = scalar(
            functools.partial(attn_back_body, first),
            [
                page,
                page_low,
                struct((2 * local, width), BF16),
                struct((2 * local, width), BF16),
                struct((8, 3 * local), F32),
                struct((2 * heads, segs, segs), F32),
            ],
            name,
            flops=2 * attn_flops,
            scratch=[pltpu.VMEM((3 * local, 2 * seq), BF16)],
            alias=None if first else {len(ins): 0, len(ins) + 1: 1},
        )(*ins, *(acc or ()), hold=hold)
        return list(outs[0:2]), outs[2:4], outs[4], outs[5]

    def groups_sum(name, *parts, holds=()):
        holds = iter([*holds] + [()] * (2 * len(bits) + 2))
        for n, bit in enumerate(bits):
            size = parts[0].shape[0] // 2
            out = struct((size, width), BF16)
            body = functools.partial(split_body, 3 + n)
            keep, give = scalar(body, [out] * 2, name + "_split")(
                place, *parts, hold=next(holds)
            )
            parts = (keep, swap(give, "dp", bit))
        (part,) = sums(name + "_sum", parts, hold=next(holds))
        for n, bit in reversed(list(enumerate(bits))):
            other = swap(part, "dp", bit)
            body = functools.partial(join_body, 3 + n)
            (part,) = scalar(
                body, [struct((2 * part.shape[0], width), BF16)], name + "_join"
            )(place, part, other, hold=next(holds))
        return part, beside(part)

    acc, (far_attn_0, far_attn_1), sums_far, seg_far = attn_back(
        far_w, kept_far, None, "attn_back_far"
    )
    *acc, y_far_up, x_far_down, far_attn_1 = gate(
        [*acc, y_far_up, x_far_down, far_attn_1], []
    )
    (x_up_send,) = sums("up_sum", (far_up_0, y_far_up))
    x_far_up = across(x_up_send)
    y_far_attn = beside(far_attn_1)
    acc, (near_attn_0, near_attn_1), sums_near, seg_near = attn_back(
        near_w, kept_near, acc, "attn_back_near", hold=[x_up_send]
    )
    *acc, x_far_up, y_far_attn, near_attn_1, far_down_0, near_up_0 = gate(
        [*acc, x_far_up, y_far_attn, near_attn_1, far_down_0, near_up_0], []
    )
    (x_attn_send,) = sums("attn_sum", (far_attn_0, y_far_attn))
    near_y_attn = beside(near_attn_1)
    x_far_attn = across(x_attn_send)
    (y_down_send,) = sums("down_sum", (near_down_1, x_far_down))
    x_far_down_0 = across(far_down_0)
    near_y_down = beside(y_down_send)
    grad_inputs, end_rows = call(
        end_body, [Own(page_low), struct((8, width), F32)], "end"
    )(Own(inputs), acc[0], core(acc[1]), grad_middle, gain_attn)

    line = struct((16, width), F32)
    (small,) = scalar(small_body, [line], "small")(
        place, ups_near, ups_far, sums_near, sums_far, seg_near, seg_far,
        Own(bucket_horizontal), Own(bucket_vertical), turn_rows, end_rows,
    )
    near_y_attn, x_far_attn = gate([near_y_attn, x_far_attn], [], small)
    (small,) = call(small_core_body, [line], "small_core")(small, core(small))
    (small,) = call(small_across_body, [line], "small_across")(small, across(small))
    steps = [small]
    for bit in [1, *bits][:-1]:
        (small,) = sums("small_sum", (small, swap(small, "dp", bit)))
        steps.append(small)
    vector = struct((width,), F32)
    short = struct((local,), F32)
    table = struct((heads, bins), F32)
    grad_bu, grad_bq, grad_bv, grad_th, grad_tv, *shared = call(
        small_end_body, [Own(v) for v in [struct((hidden,), F32), short, short, table, table] + [vector] * 6],
        "small_end",
    )(small, swap(small, "dp", [1, *bits][-1]))

    up_own, up_other = groups_sum("up", near_up_0, near_y_up, x_far_up)
    down_own, down_other = groups_sum("down", near_down_0, near_y_down, x_far_down_0)
    attn_own, attn_other = groups_sum(
        "attn", near_attn_0, near_y_attn, x_far_attn,
        holds=[()] + [[step] for step in steps] + [[grad_bu]],
    )
    grad_up, grad_down = scalar(
        unpack_mlp_body,
        [Own(struct((width, hidden), F32)), Own(struct((hidden, width), F32))],
        "unpack_mlp",
    )(place, up_own, down_own, up_other, down_other)
    grad_wq, grad_wk, grad_wv, grad_wo = scalar(
        unpack_attn_body, [Own(struct((local, width), F32))] * 4, "unpack_attn"
    )(place, attn_own, attn_other)

    return (
        result,
        grad_inputs,
        shared[4],
        shared[5],
        grad_wq.T,
        grad_bq,
        grad_wk.T,
        grad_wv.T,
        grad_bv,
        grad_th.T,
        grad_tv.T,
        grad_wo,
        shared[0],
        shared[1],
        shared[2],
        grad_up,
        grad_bu,
        grad_down,
        shared[3],
    )


def solution(mesh):
    rows = P(("dp", "mp"), None)
    columns = P(None, "mp")
    split = P("mp")
    placed = (
        rows, rows, P(), P(), columns, split, columns, columns, split, columns, columns,
        P("mp", None), P(), P(), P(), columns, split, P("mp", None), P(),
        P("dp", None), P("dp", None), P("dp", None, None), P("dp", None, None),
    )
    given = (
        rows, rows, P(), P(), columns, split, columns, columns, split, columns, columns,
        P("mp", None), P(), P(), P(), columns, split, P("mp", None), P(),
    )
    return jax.shard_map(
        functools.partial(on_device, mesh.shape["dp"], mesh.shape["mp"]),
        mesh=mesh,
        in_specs=placed,
        out_specs=given,
        check_vma=False,
    )
```

```python
import functools

import jax
import jax.numpy as jnp
from jax import lax
from jax.experimental import pallas as pl
from jax.experimental.pallas import tpu as pltpu
from jax.sharding import PartitionSpec as P

EPSILON = 1e-05
NEGATIVE = -1e30
HEAD = 64
EXTRA = 16
F32 = jnp.float32
BF16 = jnp.bfloat16
LIMIT = 16 * 1024 * 1024
SCALE = 30

NN = (((1,), (0,)), ((), ()))
NT = (((1,), (1,)), ((), ()))
TN = (((0,), (0,)), ((), ()))


def mm(left, right, dims=NN):
    return lax.dot_general(left, right, dims, preferred_element_type=F32)


def struct(shape, dtype):
    return jax.ShapeDtypeStruct(shape, dtype)


class Own:
    def __init__(self, value, cuts=()):
        self.value = value
        self.cuts = cuts


class Loaded:
    def __init__(self, source, scratch, sems, cuts):
        self.scratch = scratch
        self.shape = scratch.shape
        edges = [0, *cuts, scratch.shape[0]]
        self.parts = []
        for n, (low, high) in enumerate(zip(edges, edges[1:])):
            here = pl.ds(low, high - low)
            copy = pltpu.make_async_copy(source.at[here], scratch.at[here], sems[n])
            copy.start()
            self.parts.append((low, high, copy))

    def wait(self, low, high):
        for part in list(self.parts):
            if part[0] < high and low < part[1]:
                part[2].wait()
                self.parts.remove(part)

    def __getitem__(self, at):
        first = at[0] if isinstance(at, tuple) else at
        if isinstance(first, slice):
            self.wait(first.start or 0, self.shape[0] if first.stop is None else first.stop)
        else:
            self.wait(0, self.shape[0])
        return self.scratch[at]


class Stored:
    def __init__(self, target, scratch, sem):
        self.copy = pltpu.make_async_copy(scratch, target, sem)
        self.scratch = scratch
        self.shape = scratch.shape
        self.dtype = scratch.dtype
        self.sent = False

    def __getitem__(self, at):
        return self.scratch[at]

    def __setitem__(self, at, value):
        self.scratch[at] = value

    def flush(self):
        self.copy.start()
        self.sent = True


def flush(ref):
    if isinstance(ref, Stored):
        ref.flush()


def call(body, outs, name, flops=0, transcendentals=0, scalar=False, scratch=(), alias=None, limit=LIMIT):
    def run(*args, hold=()):
        own_in = [isinstance(a, Own) for a in args]
        own_out = [isinstance(o, Own) for o in outs]
        ins = [a.value if own else a for a, own in zip(args, own_in)]
        shapes = [o.value if own else o for o, own in zip(outs, own_out)]
        moved = sum(a.size * a.dtype.itemsize for a in ins + shapes)
        count, held = len(ins), len(hold)
        total = sum(1 + len(v.cuts) for v in [*args, *outs] if isinstance(v, Own))
        copied = [v for v, own in zip(ins + shapes, own_in + own_out) if own]

        def inner(*refs):
            given, results = refs[:count], refs[count + held:count + held + len(shapes)]
            spare = refs[count + held + len(shapes):]
            slots, rest = iter(spare[:len(copied)]), spare[len(copied):]
            sems = iter(range(total))
            loaded = [
                Loaded(
                    ref, next(slots), [rest[-1].at[next(sems)] for _ in (0, *arg.cuts)], arg.cuts
                )
                if isinstance(arg, Own)
                else ref
                for ref, arg in zip(given, args)
            ]
            stored = [
                Stored(ref, next(slots), rest[-1].at[next(sems)]) if own else ref
                for ref, own in zip(results, own_out)
            ]
            body(*loaded, *stored, *(rest[:-1] if copied else rest))
            for ref in loaded:
                if isinstance(ref, Loaded):
                    ref.wait(0, ref.shape[0])
            for ref in stored:
                if isinstance(ref, Stored):
                    if not ref.sent:
                        ref.flush()
                    ref.copy.wait()

        buffers = [pltpu.VMEM(v.shape, v.dtype) for v in copied] + list(scratch)
        if copied:
            buffers.append(pltpu.SemaphoreType.DMA((total,)))
        kept = pl.BlockSpec(memory_space=pl.ANY)
        inside = pl.BlockSpec(memory_space=pltpu.VMEM)
        in_specs = [kept if own else inside for own in own_in]
        if scalar:
            in_specs[0] = pl.BlockSpec(memory_space=pltpu.SMEM)
        return pl.pallas_call(
            inner,
            out_shape=[
                (pltpu.HBM if own else pltpu.VMEM)(o.shape, o.dtype) for o, own in zip(shapes, own_out)
            ],
            in_specs=in_specs + [kept] * held,
            out_specs=[kept if own else inside for own in own_out],
            scratch_shapes=buffers,
            input_output_aliases=alias or {},
            compiler_params=pltpu.CompilerParams(vmem_limit_bytes=limit),
            cost_estimate=pl.CostEstimate(
                flops=int(flops * SCALE),
                bytes_accessed=int(moved * SCALE),
                transcendentals=int(transcendentals),
            ),
            name=name,
        )(
            *[
                v
                if scalar and n == 0
                else pltpu.with_memory_space_constraint(v, pltpu.HBM if own else pltpu.VMEM)
                for n, (v, own) in enumerate(zip(ins, own_in))
            ],
            *hold,
        )

    return run


def line(ref):
    value = ref[...]
    return value if value.ndim == 2 else value.reshape(1, value.shape[0])


def halves(values):
    high = values.astype(BF16)
    return high, (values - high.astype(F32)).astype(BF16)


def pack_attn_body(place_ref, wq_ref, wk_ref, wv_ref, wo_ref, th_ref, tv_ref, bq_ref, bv_ref,
                   all_ref, send_ref):
    local = wq_ref.shape[0]
    heads = th_ref.shape[0]
    piece = 2 * local + EXTRA
    th, tv = th_ref[...], tv_ref[...]
    parts = []
    for m in range(heads):
        parts += [th[m:m + 1], tv[m:m + 1]]
    high, low = halves(jnp.concatenate(parts + [line(bq_ref), line(bv_ref)], axis=1))
    which = lax.broadcasted_iota(jnp.int32, (EXTRA, high.shape[1]), 0)
    extra = jnp.where(which == 0, high.astype(F32), jnp.where(which == 1, low.astype(F32), 0.0))
    extra = extra.astype(BF16)
    side = place_ref[0, 0]
    for n, (one_ref, two_ref) in enumerate(((wq_ref, wv_ref), (wk_ref, wo_ref))):
        one, two = one_ref[...], two_ref[...]
        all_ref[n * local:(n + 1) * local, :] = one
        all_ref[piece + n * local:piece + (n + 1) * local, :] = two
        send_ref[n * local:(n + 1) * local, :] = jnp.where(side == 0, one, two)
    all_ref[2 * local:piece, :] = extra
    all_ref[piece + 2 * local:, :] = extra
    send_ref[2 * local:, :] = extra


def pack_mlp_body(place_ref, up_ref, bias_ref, down_ref, all_ref, up_send_ref, down_send_ref):
    half = down_ref.shape[0] // 2
    piece = 2 * half + EXTRA
    own = place_ref[0, 0] == 0
    bias = line(bias_ref)
    which = lax.broadcasted_iota(jnp.int32, (EXTRA, half), 0) == 0
    for n in (0, 1):
        one, two = pl.ds(n * half, half), pl.ds((1 - n) * half, half)
        at = n * piece
        left = jnp.where(own, up_ref[0:half, one], up_ref[0:half, two])
        right = jnp.where(own, up_ref[half:, one], up_ref[half:, two])
        high, low = halves(jnp.where(own, bias[:, n * half:(n + 1) * half], bias[:, (1 - n) * half:(2 - n) * half]))
        high = jnp.where(which, high.astype(F32), 0.0).astype(BF16)
        low = jnp.where(which, low.astype(F32), 0.0).astype(BF16)
        all_ref[at:at + half, 0:half] = left
        all_ref[at:at + half, half:] = right
        all_ref[at + half:at + half + EXTRA, 0:half] = high
        all_ref[at + half:at + half + EXTRA, half:] = low
        down = jnp.where(own, down_ref[one, :], down_ref[two, :])
        all_ref[at + half + EXTRA:at + piece, :] = down
        if n == 0:
            up_send_ref[0:half, 0:half] = left
            up_send_ref[0:half, half:] = right
            up_send_ref[half:, 0:half] = high
            up_send_ref[half:, half:] = low
            flush(up_send_ref)
            down_send_ref[...] = down
            flush(down_send_ref)


def start_body(place_ref, x_ref, gain_ref, shift_ref, seg_ref, valid_ref, bh_ref, bv_ref,
               xn_ref, mt_ref, neg_ref, ih_ref, iv_ref):
    x = x_ref[...].astype(F32)
    mean = jnp.mean(x, axis=1, keepdims=True)
    cen = x - mean
    var = jnp.mean(cen * cen, axis=1, keepdims=True)
    xn_ref[...] = (cen * lax.rsqrt(var + EPSILON) * line(gain_ref) + line(shift_ref)).astype(BF16)
    segs = mt_ref.shape[0]
    seq = x.shape[0]
    rows = lax.broadcasted_iota(jnp.int32, (segs, seq), 0)
    top = lax.broadcasted_iota(jnp.int32, (EXTRA, seq), 0) == 0
    for p in (0, 1):
        page = place_ref[0, 1 + p]
        here = pl.ds(p * seq, seq)
        member = jnp.where(rows == seg_ref[pl.ds(page, 1), :], 1.0, 0.0).astype(BF16)
        mt_ref[:, here] = member
        masked = jnp.where(valid_ref[pl.ds(page, 1), :] > 0, 0.0, NEGATIVE)
        neg_ref[:, here] = jnp.where(top, masked, 0.0).astype(BF16)
        bh, bv = bh_ref[page].astype(F32).astype(BF16), bv_ref[page].astype(F32).astype(BF16)
        ih_ref[:, here] = mm(bh, member, TN).astype(jnp.int32)
        iv_ref[:, here] = mm(bv, member, TN).astype(jnp.int32) + segs


def lookup(table, index):
    rows, seq = index.shape
    spread = jnp.broadcast_to(table, (rows, 128))
    parts = [
        jnp.take_along_axis(
            spread, index[:, at:at + 128], axis=1, mode="promise_in_bounds"
        )
        for at in range(0, seq, 128)
    ]
    return jnp.concatenate(parts, axis=1)


def attn_body(first, *refs):
    if first:
        w_ref, ih_ref, iv_ref, mt_ref, neg_ref = refs[2:7]
        given = (None, None)
        qkv_ref, ctx_ref, lse_ref, bias_ref, *outs = refs[7:]
    else:
        place_ref, own_ref, other_ref = refs[0], refs[3], refs[4]
        ih_ref, iv_ref, mt_ref, neg_ref = refs[5:9]
        given = refs[9:11]
        qkv_ref, ctx_ref, lse_ref, bias_ref, *outs, w_ref = refs[11:]
        refs = refs[1:]
        low = place_ref[0, 0] == 0
        own, other = own_ref[...], other_ref[...]
        size = own.shape[0]
        w_ref[0:size, :] = jnp.where(low, own, other)
        w_ref[size:, :] = jnp.where(low, other, own)
        flush(w_ref)
    width = ctx_ref.shape[0]
    heads = width // HEAD
    segs = mt_ref.shape[0]
    seq = refs[0].shape[0]
    second = 2 * width + EXTRA
    extra = w_ref[2 * width:second, :]
    pick = jnp.where(lax.broadcasted_iota(jnp.int32, (EXTRA, seq), 0) < 2, 1.0, 0.0).astype(BF16)
    bias = mm(extra[:, heads * 128:heads * 128 + 2 * width], pick, TN)
    tables = extra[0:1, :].astype(F32) + extra[1:2, :].astype(F32)
    ones = jnp.ones((EXTRA, seq), BF16)
    for p in (0, 1):
        xn = refs[p][...]
        here = pl.ds(p * seq, seq)
        qk = mm(w_ref[0:2 * width, :], xn, NT)
        v = mm(w_ref[second:second + width, :], xn, NT)
        qkv_ref[0:width, here] = ((qk[0:width] + bias[0:width]) * 0.125).astype(BF16)
        qkv_ref[width:2 * width, here] = qk[width:].astype(BF16)
        qkv_ref[2 * width:, here] = (v + bias[width:]).astype(BF16)
    flush(qkv_ref)
    for p in (0, 1):
        here = pl.ds(p * seq, seq)
        member = mt_ref[:, here]
        for m in range(heads):
            table = tables[:, 128 * m:128 * m + 128]
            pos = lookup(table, ih_ref[:, here]) + lookup(table, iv_ref[:, here])
            high, low = halves(pos)
            bias_ref[2 * segs * m:2 * segs * m + segs, here] = high
            bias_ref[2 * segs * m + segs:2 * segs * (m + 1), here] = low
            at = HEAD * m
            q_aug = jnp.concatenate([qkv_ref[at:at + HEAD, here], high, low, ones], axis=0)
            k_aug = jnp.concatenate(
                [qkv_ref[width + at:width + at + HEAD, here], member, member, neg_ref[:, here]],
                axis=0,
            )
            scores = mm(k_aug, q_aug, TN)
            top = jnp.max(scores, axis=0, keepdims=True)
            expo = jnp.exp(scores - top).astype(BF16)
            v_aug = jnp.concatenate(
                [qkv_ref[2 * width + at:2 * width + at + HEAD, here], ones], axis=0
            )
            summed = mm(v_aug, expo)
            total = summed[HEAD:HEAD + 1]
            ctx_ref[at:at + HEAD, here] = (summed[0:HEAD] / total).astype(BF16)
            lse_ref[m:m + 1, here] = top + jnp.log(total)
        out = mm(ctx_ref[:, here], w_ref[second + width:second + 2 * width, :], TN)
        if given[p] is not None:
            out = given[p][...] + out
        outs[p][...] = out.astype(outs[p].dtype)
    lse_ref[heads:, :] = jnp.zeros((lse_ref.shape[0] - heads, 2 * seq), F32)


def middle_body(x_ref, acc_ref, got_ref, bias_ref, gain_ref, shift_ref, mid_ref, nm_ref):
    mid = x_ref[...].astype(F32) + (acc_ref[...] + got_ref[...].astype(F32)) + line(bias_ref)
    mid_ref[...] = mid
    mean = jnp.mean(mid, axis=1, keepdims=True)
    cen = mid - mean
    var = jnp.mean(cen * cen, axis=1, keepdims=True)
    nm_ref[...] = (cen * lax.rsqrt(var + EPSILON) * line(gain_ref) + line(shift_ref)).astype(BF16)


def mlp_body(first, layout, *refs):
    nm_refs, cot_refs = refs[0:2], refs[2:4]
    weights = refs[4:7]
    given = (None,) * 4 if first else refs[7:11]
    outs = refs[7 if first else 11:]
    accs, grads, db_ref = outs[0:4], outs[4:8], outs[8]
    half = grads[0].shape[0]
    for n, (up_in, up_at, down_in, down_at) in enumerate(layout):
        u_ref, d_ref = weights[up_in], weights[down_in]
        extra = u_ref[up_at + half:up_at + half + EXTRA, :].astype(F32)
        bias = extra[0:1, 0:half] + extra[0:1, half:]
        up_left = u_ref[up_at:up_at + half, 0:half]
        up_right = u_ref[up_at:up_at + half, half:]
        down = d_ref[down_at:down_at + half, :]
        total = None
        for p in (0, 1):
            nm_left, nm_right = nm_refs[p][:, 0:half], nm_refs[p][:, half:]
            cot = cot_refs[p][...]
            upper = mm(nm_left, up_left) + mm(nm_right, up_right) + bias
            cdf = 0.5 + 0.5 * lax.erf(upper * 0.7071067811865476)
            pdf = jnp.exp(upper * upper * -0.5) * 0.3989422804014327
            hidden = (upper * cdf).astype(BF16)
            grad_hidden = mm(cot, down, NT)
            grad_upper = (grad_hidden * (cdf + upper * pdf)).astype(BF16)
            sums_now = (
                mm(nm_left, grad_upper, TN),
                mm(nm_right, grad_upper, TN),
                mm(hidden, cot, TN),
                jnp.sum(grad_upper.astype(F32), axis=0, keepdims=True),
            )
            total = sums_now if total is None else [a + b for a, b in zip(total, sums_now)]
            down_ref, back_ref = accs[p], accs[2 + p]
            base_down, base_back = (given[p], given[2 + p]) if n == 0 else (down_ref, back_ref)
            down_out = mm(hidden, down)
            back_left = mm(grad_upper, up_left, NT)
            back_right = mm(grad_upper, up_right, NT)
            if base_down is not None:
                down_out = base_down[...].astype(F32) + down_out
                back_left = base_back[:, 0:half].astype(F32) + back_left
                back_right = base_back[:, half:].astype(F32) + back_right
            down_ref[...] = down_out.astype(down_ref.dtype)
            back_ref[:, 0:half] = back_left.astype(back_ref.dtype)
            back_ref[:, half:] = back_right.astype(back_ref.dtype)
        up_ref, dn_ref = grads[2 * n:2 * n + 2]
        up_ref[:, 0:half] = total[0].astype(BF16)
        up_ref[:, half:] = total[1].astype(BF16)
        flush(up_ref)
        dn_ref[...] = total[2].astype(BF16)
        flush(dn_ref)
        db_ref[0:1, n * half:(n + 1) * half] = total[3]
    db_ref[1:, :] = jnp.zeros((db_ref.shape[0] - 1, 2 * half), F32)


def turn_body(mid_ref, down_ref, down_got_ref, bias_ref, back_ref, back_got_ref, cot_ref, gain_ref,
              res_ref, gmid_ref, ga_ref, rows_ref):
    mid = mid_ref[...]
    down = down_ref[...] + down_got_ref[...].astype(F32)
    res_ref[...] = (mid + down + line(bias_ref)).astype(BF16)
    mean = jnp.mean(mid, axis=1, keepdims=True)
    cen = mid - mean
    var = jnp.mean(cen * cen, axis=1, keepdims=True)
    rstd = lax.rsqrt(var + EPSILON)
    n = cen * rstd
    back = back_ref[...] + back_got_ref[...].astype(F32)
    q = back * line(gain_ref)
    cot = cot_ref[...].astype(F32)
    mean_q = jnp.mean(q, axis=1, keepdims=True)
    mean_qn = jnp.mean(q * n, axis=1, keepdims=True)
    grad = cot + rstd * (q - mean_q - n * mean_qn)
    gmid_ref[...] = grad
    ga_ref[...] = grad.astype(BF16)
    rows_ref[0:1, :] = jnp.sum(grad, axis=0, keepdims=True)
    rows_ref[1:2, :] = jnp.sum(back * n, axis=0, keepdims=True)
    rows_ref[2:3, :] = jnp.sum(back, axis=0, keepdims=True)
    rows_ref[3:4, :] = jnp.sum(cot, axis=0, keepdims=True)
    rows_ref[4:, :] = jnp.zeros((rows_ref.shape[0] - 4, rows_ref.shape[1]), F32)


def attn_back_body(first, *refs):
    place_ref, xn_refs, ga_refs = refs[0], refs[1:3], refs[3:5]
    w_ref, qkv_ref, ctx_ref, lse_ref, bias_ref, mt_ref, neg_ref = refs[5:12]
    given = (None, None) if first else refs[12:14]
    *backs, kept_ref, other_ref, sums_ref, seg_ref, dqkv_ref = refs[12 if first else 14:]
    width = ctx_ref.shape[0]
    heads = width // HEAD
    seq = xn_refs[0].shape[0]
    segs = mt_ref.shape[0]
    second = 2 * width + EXTRA
    ones = jnp.ones((EXTRA, seq), BF16)
    grad_out = None
    for p in (0, 1):
        here = pl.ds(p * seq, seq)
        ga = ga_refs[p][...]
        member = mt_ref[:, here]
        grad_ctx = mm(w_ref[second + width:second + 2 * width, :], ga, NT).astype(BF16)
        part = mm(ctx_ref[:, here], ga)
        grad_out = part if p == 0 else grad_out + part
        for m in range(heads):
            at = HEAD * m
            q = qkv_ref[at:at + HEAD, here]
            k = qkv_ref[width + at:width + at + HEAD, here]
            v = qkv_ref[2 * width + at:2 * width + at + HEAD, here]
            g = grad_ctx[at:at + HEAD]
            q_aug = jnp.concatenate(
                [q, bias_ref[2 * segs * m:2 * segs * (m + 1), here], ones], axis=0
            )
            k_aug = jnp.concatenate([k, member, member, neg_ref[:, here]], axis=0)
            scores = mm(k_aug, q_aug, TN)
            probs = jnp.exp(scores - lse_ref[m:m + 1, here])
            grad_probs = mm(v, g, TN)
            delta = jnp.sum(probs * grad_probs, axis=0, keepdims=True)
            grad_scores = (probs * (grad_probs - delta)).astype(BF16)
            grad_v = mm(g, probs.astype(BF16), NT)
            dqkv_ref[2 * width + at:2 * width + at + HEAD, here] = grad_v.astype(BF16)
            dqkv_ref[width + at:width + at + HEAD, here] = mm(q, grad_scores, NT).astype(BF16)
            both = mm(jnp.concatenate([k, member], axis=0), grad_scores)
            dqkv_ref[at:at + HEAD, here] = both[0:HEAD].astype(BF16) * jnp.asarray(0.125, BF16)
            high, low = halves(both[HEAD:])
            seg_ref[p * heads + m] = mm(member, high, NT) + mm(member, low, NT)
    grads = mm(dqkv_ref[:, 0:seq], xn_refs[0][...]) + mm(dqkv_ref[:, seq:], xn_refs[1][...])
    grads = jnp.concatenate([grads, grad_out], axis=0).astype(BF16)
    low = place_ref[0, 0] == 0
    kept_ref[...] = jnp.where(low, grads[0:2 * width], grads[2 * width:])
    flush(kept_ref)
    other_ref[...] = jnp.where(low, grads[2 * width:], grads[0:2 * width])
    flush(other_ref)
    for p in (0, 1):
        here = pl.ds(p * seq, seq)
        back = mm(dqkv_ref[0:2 * width, here], w_ref[0:2 * width, :], TN)
        back = back + mm(dqkv_ref[2 * width:, here], w_ref[second:second + width, :], TN)
        if given[p] is not None:
            back = given[p][...] + back
        backs[p][...] = back.astype(backs[p].dtype)
    sums_ref[...] = mm(jnp.ones((8, 2 * seq), BF16), dqkv_ref[...], NT)


def sum_body(counts, *refs):
    total = sum(counts)
    outs = refs[total:]
    at = 0
    for count, out in zip(counts, outs):
        value = refs[at][...].astype(F32)
        for ref in refs[at + 1:at + count]:
            value = value + ref[...].astype(F32)
        out[...] = value.astype(out.dtype)
        at += count


def sums(name, *groups, hold=()):
    outs = [struct(group[0].shape, group[0].dtype) for group in groups]
    body = functools.partial(sum_body, [len(group) for group in groups])
    flat = [value for group in groups for value in group]
    return call(body, outs, name)(*flat, hold=hold)


def split_body(which, groups, place_ref, *refs):
    *parts, keep_ref, give_ref = refs
    low = place_ref[0, which] == 0
    size = keep_ref.shape[0] // groups
    count = len(parts) // groups
    for n in range(groups):
        value = parts[n * count][...].astype(F32)
        for ref in parts[n * count + 1:(n + 1) * count]:
            value = value + ref[...].astype(F32)
        one, two = value[0:size], value[size:]
        here = pl.ds(n * size, size)
        keep_ref[here, :] = jnp.where(low, one, two).astype(BF16)
        give_ref[here, :] = jnp.where(low, two, one).astype(BF16)


def resplit_body(which, groups, place_ref, own_ref, got_ref, keep_ref, give_ref):
    low = place_ref[0, which] == 0
    size = keep_ref.shape[0] // groups
    value = own_ref[...].astype(F32) + got_ref[...].astype(F32)
    for n in range(groups):
        at = 2 * n * size
        one, two = value[at:at + size], value[at + size:at + 2 * size]
        here = pl.ds(n * size, size)
        keep_ref[here, :] = jnp.where(low, one, two).astype(BF16)
        give_ref[here, :] = jnp.where(low, two, one).astype(BF16)


def join_body(which, groups, place_ref, own_ref, other_ref, out_ref):
    size = own_ref.shape[0] // groups
    low = place_ref[0, which] == 0
    own, other = own_ref[...], other_ref[...]
    for n in range(groups):
        part = slice(n * size, (n + 1) * size)
        out_ref[2 * n * size:(2 * n + 1) * size, :] = jnp.where(low, own[part], other[part])
        out_ref[(2 * n + 1) * size:(2 * n + 2) * size, :] = jnp.where(low, other[part], own[part])


def corner_body(y_ref, z_ref, low_ref, high_ref):
    size = low_ref.shape[0]
    low_ref[...] = z_ref[0:size, :]
    high_ref[...] = y_ref[size:, :]


def end_body(x_ref, back_ref, got_ref, gmid_ref, gain_ref, gx_ref, rows_ref):
    x = x_ref[...].astype(F32)
    mean = jnp.mean(x, axis=1, keepdims=True)
    cen = x - mean
    var = jnp.mean(cen * cen, axis=1, keepdims=True)
    rstd = lax.rsqrt(var + EPSILON)
    n = cen * rstd
    back = back_ref[...] + got_ref[...].astype(F32)
    q = back * line(gain_ref)
    mean_q = jnp.mean(q, axis=1, keepdims=True)
    mean_qn = jnp.mean(q * n, axis=1, keepdims=True)
    gx_ref[...] = (gmid_ref[...] + rstd * (q - mean_q - n * mean_qn)).astype(BF16)
    rows_ref[0:1, :] = jnp.sum(back * n, axis=0, keepdims=True)
    rows_ref[1:2, :] = jnp.sum(back, axis=0, keepdims=True)
    rows_ref[2:, :] = jnp.zeros((rows_ref.shape[0] - 2, rows_ref.shape[1]), F32)


def small_body(place_ref, ups_0_ref, ups_1_ref, sums_near_ref, sums_far_ref, seg_near_ref,
               seg_far_ref, bh_ref, bv_ref, turn_ref, end_ref, out_ref):
    count, segs, _ = seg_near_ref.shape
    heads = count // 2
    bins = lax.broadcasted_iota(jnp.int32, (segs, segs), 0)
    total = jnp.zeros((2 * EXTRA, 2 * segs), F32)
    for p in (0, 1):
        page = place_ref[0, 1 + p]
        bh, bv = bh_ref[page], bv_ref[page]
        own = pl.ds(p * heads, heads)
        for s in range(segs):
            both = jnp.concatenate(
                [
                    seg_near_ref[own, s, :],
                    seg_far_ref[own, s, :],
                    jnp.zeros((EXTRA - 2 * heads, segs), F32),
                ],
                axis=0,
            )
            hot = jnp.concatenate(
                [
                    jnp.where(bins == bh[s:s + 1, :], 1.0, 0.0),
                    jnp.where(bins == bv[s:s + 1, :], 1.0, 0.0),
                ],
                axis=0,
            ).astype(BF16)
            total = total + mm(jnp.concatenate(halves(both), axis=0), hot, NT)
    tables = total[0:EXTRA] + total[EXTRA:]
    low = place_ref[0, 0] == 0
    out_ref[...] = jnp.zeros(out_ref.shape, F32)
    width = sums_near_ref.shape[1] // 3
    half = ups_0_ref.shape[1] // 2
    ups_0, ups_1 = ups_0_ref[0:1, :], ups_1_ref[0:1, :]
    near = (ups_1[:, half:], ups_0[:, half:], sums_near_ref)
    far = (ups_0[:, 0:half], ups_1[:, 0:half], sums_far_ref)
    for k, (one, two, sums_in) in enumerate((near, far)):
        out_ref[2 * k:2 * k + 1, 0:half] = jnp.where(low, one, two)
        out_ref[2 * k:2 * k + 1, half:] = jnp.where(low, two, one)
        parts = [sums_in[0:1, 0:width], sums_in[0:1, 2 * width:]]
        parts += [tables[k * heads + m:k * heads + m + 1] for m in range(heads)]
        out_ref[2 * k + 1:2 * k + 2, :] = jnp.concatenate(parts, axis=1)
    out_ref[4:8, :] = turn_ref[0:4, :]
    out_ref[8:10, :] = end_ref[0:2, :]


def small_end_body(place_ref, all_ref, rows_ref, th_ref, tv_ref):
    shard = place_ref[0, 1]
    own = all_ref[shard, 0:2, :] + all_ref[shard ^ 2, 2:4, :]
    every = all_ref[0, 4:10, :]
    for n in range(1, all_ref.shape[0]):
        every = every + all_ref[n, 4:10, :]
    rows_ref[0:2, :] = own
    rows_ref[2:8, :] = every
    heads, bins = th_ref.shape
    for m in range(heads):
        at = own.shape[1] - 2 * bins * (heads - m)
        th_ref[m:m + 1, :] = own[1:2, at:at + bins]
        tv_ref[m:m + 1, :] = own[1:2, at + bins:at + 2 * bins]


def square(place_ref, own, beside, along, corner):
    side, low = place_ref[0, 0] == 0, place_ref[0, 3] == 0
    own_half = (jnp.where(low, own, along), jnp.where(low, along, own))
    other_half = (jnp.where(low, beside, corner), jnp.where(low, corner, beside))
    first = [jnp.where(side, a, b).astype(F32) for a, b in zip(own_half, other_half)]
    second = [jnp.where(side, b, a).astype(F32) for a, b in zip(own_half, other_half)]
    return first + second


def unpack_mlp_body(place_ref, own_ref, y_ref, z_ref, low_ref, high_ref, up_ref, down_ref):
    size = low_ref.shape[0]
    half = 2 * size
    ups = square(
        place_ref, own_ref[0:size, :], y_ref[0:size, :], z_ref[0:size, :], low_ref[...]
    )
    for n, part in enumerate(ups):
        here = pl.ds((n // 2) * half, half)
        at = (n % 2) * size
        up_ref[at:at + size, here] = part[:, 0:half]
        up_ref[half + at:half + at + size, here] = part[:, half:]
    flush(up_ref)
    downs = square(
        place_ref, own_ref[size:, :], y_ref[size:, :], z_ref[size:, :], high_ref[...]
    )
    for n, part in enumerate(downs):
        down_ref[n * size:(n + 1) * size, :] = part


def unpack_attn_body(place_ref, own_ref, y_ref, z_ref, low_ref, high_ref,
                     q_ref, k_ref, v_ref, o_ref):
    corner = jnp.concatenate([low_ref[...], high_ref[...]], axis=0)
    parts = square(place_ref, own_ref[...], y_ref[...], z_ref[...], corner)
    for ref, part in zip((q_ref, k_ref, v_ref, o_ref), parts):
        ref[...] = part
        flush(ref)


def order_body(*refs):
    pass


def gate(inside, outside, *others):
    spec = pl.BlockSpec(memory_space=pl.ANY)
    spaces = [pltpu.VMEM] * len(inside) + [pltpu.HBM] * len(outside)
    values = [*inside, *outside]
    return pl.pallas_call(
        order_body,
        out_shape=[space(v.shape, v.dtype) for space, v in zip(spaces, values)],
        in_specs=[spec] * (len(values) + len(others)),
        out_specs=[spec] * len(values),
        input_output_aliases={n: n for n in range(len(values))},
        compiler_params=pltpu.CompilerParams(vmem_limit_bytes=2**20),
        name="order",
    )(
        *[pltpu.with_memory_space_constraint(v, space) for space, v in zip(spaces, values)],
        *others,
    )


def on_device(
    dp_count,
    mp_count,
    inputs,
    cotangent,
    gain_attn,
    shift_attn,
    weight_query,
    bias_query,
    weight_key,
    weight_value,
    bias_value,
    table_horizontal,
    table_vertical,
    weight_out,
    bias_out,
    gain_mlp,
    shift_mlp,
    weight_up,
    bias_up,
    weight_down,
    bias_down,
    segment,
    valid,
    bucket_horizontal,
    bucket_vertical,
):
    seq, width = inputs.shape
    local = weight_query.shape[1]
    heads = table_horizontal.shape[1]
    hidden = weight_up.shape[1]
    half = hidden // 2
    segs = bucket_horizontal.shape[1]
    bins = table_horizontal.shape[0]
    shard = lax.axis_index("mp")
    pages = lax.axis_index("dp")
    bits = [1 << b for b in range(1, dp_count.bit_length() - 1)]
    place = jnp.stack([pages % 2, shard, shard ^ 1] + [(pages // bit) % 2 for bit in bits])
    place = place.astype(jnp.int32).reshape(1, -1)
    scalar = functools.partial(call, scalar=True)

    def swap(value, axis, bit):
        count = dp_count if axis == "dp" else mp_count
        return lax.ppermute(value, axis, [(i, i ^ bit) for i in range(count)])

    def core(value):
        return swap(value, "mp", 1)

    def across(value):
        return swap(value, "mp", 2)

    def beside(value):
        return swap(value, "dp", 1)

    piece = struct((2 * local + EXTRA, width), BF16)
    both = struct((4 * local + 2 * EXTRA, width), BF16)
    near_w, attn_send = scalar(pack_attn_body, [both, piece], "pack_attn")(
        place, Own(weight_query.T), Own(weight_key.T), Own(weight_value.T), Own(weight_out),
        Own(table_horizontal.T), Own(table_vertical.T), bias_query, bias_value,
    )
    x_attn = across(attn_send)
    cot_got = core(cotangent)
    mlp_w, up_send, down_send = scalar(
        pack_mlp_body,
        [
            struct((2 * (2 * half + EXTRA), width), BF16),
            Own(struct((half + EXTRA, width), BF16)),
            Own(struct((half, width), BF16)),
        ],
        "pack_mlp",
    )(place, Own(weight_up), bias_up, Own(weight_down))

    attn_flops = 2 * (2 * seq * width * 4 * local + heads * seq * seq * 256 * 2 * 2)
    page = struct((seq, width), F32)
    page_low = struct((seq, width), BF16)

    def owned(*values):
        return [Own(value) for value in values]

    saved = [
        struct((3 * local, 2 * seq), BF16),
        struct((local, 2 * seq), BF16),
        struct((8, 2 * seq), F32),
        struct((2 * segs * heads, 2 * seq), BF16),
    ]

    def mlp(weights, layout, acc, name, hold=()):
        first = acc is None
        ins = [*nms, cotangent, cot_got, *weights]
        outs = call(
            functools.partial(mlp_body, first, layout),
            [page, page_low, page, page_low]
            + [struct((half, width), BF16)] * 4
            + [struct((8, hidden), F32)],
            name,
            flops=2 * 2 * 6 * seq * width * hidden,
            alias=None if first else {len(ins) + n: n for n in range(4)},
        )(*ins, *(acc or ()), hold=hold)
        return list(outs[0:4]), outs[4:8], outs[8]

    xn, member, negative, index_h, index_v = scalar(
        start_body,
        [
            struct((seq, width), BF16),
            struct((segs, 2 * seq), BF16),
            struct((EXTRA, 2 * seq), BF16),
            struct((segs, 2 * seq), jnp.int32),
            struct((segs, 2 * seq), jnp.int32),
        ],
        "first_norm",
    )(
        place, Own(inputs), gain_attn, shift_attn,
        Own(segment), Own(valid), Own(bucket_horizontal), Own(bucket_vertical)
    )
    x_attn, xn, up_send, down_send = gate([x_attn, xn], [up_send, down_send])
    y_attn = beside(x_attn)
    x_up = across(up_send)
    xns = [xn, core(xn)]
    *kept_near, acc_0, acc_1 = call(
        functools.partial(attn_body, True), [*saved, page, page_low], "attn_near", flops=attn_flops
    )(*xns, near_w, index_h, index_v, member, negative)
    acc_0, acc_1, x_attn, y_attn, x_up, down_send = gate(
        [acc_0, acc_1, x_attn, y_attn, x_up], [down_send]
    )
    y_up = beside(x_up)
    x_down = across(down_send)
    *kept_far, acc_0, acc_1, far_w = scalar(
        functools.partial(attn_body, False),
        [*saved, page, page_low, both],
        "attn_far",
        flops=attn_flops,
        alias={9: 4, 10: 5},
    )(
        place, *xns, x_attn, y_attn, index_h, index_v, member, negative, acc_0, acc_1
    )
    acc_0, acc_1, x_up, y_up, x_down = gate([acc_0, acc_1, x_up, y_up, x_down], [])
    middle, normed_mlp = call(middle_body, [page, page_low], "second_norm")(
        Own(inputs), acc_0, core(acc_1), bias_out, gain_mlp, shift_mlp
    )
    nms = [normed_mlp, core(normed_mlp)]
    y_down = beside(x_down)
    up_rows, all_rows = half + EXTRA, 2 * half + EXTRA
    mlp_acc, grads, ups_0 = mlp(
        [x_up, x_down, mlp_w], [(0, 0, 1, 0), (2, all_rows, 2, all_rows + up_rows)], None, "mlp_0"
    )
    far_up_0, far_down_0, near_up_1, near_down_1 = grads
    *mlp_acc, y_down, near_up_1, far_down_0 = gate(
        [*mlp_acc, y_down, near_up_1, far_down_0], []
    )
    near_y_up = beside(near_up_1)
    x_far_down_0 = across(far_down_0)
    mlp_acc, grads, ups_1 = mlp(
        [y_up, y_down, mlp_w], [(0, 0, 1, 0), (2, 0, 2, up_rows)], mlp_acc, "mlp_1"
    )
    far_up_1, far_down_1, near_up_0, near_down_0 = grads
    *mlp_acc, near_y_up, x_far_down_0, far_up_1, far_down_1 = gate(
        [*mlp_acc, near_y_up, x_far_down_0, far_up_1, far_down_1], []
    )
    y_far_up = beside(far_up_1)
    x_far_down_1 = across(far_down_1)
    result, grad_middle, grad_attn, turn_rows = call(
        turn_body,
        [Own(page_low), page, page_low, struct((8, width), F32)],
        "turn",
    )(
        middle, mlp_acc[0], core(mlp_acc[1]), bias_down, mlp_acc[2], core(mlp_acc[3]),
        Own(cotangent), gain_mlp,
    )
    grad_attn, y_far_up, x_far_down_1 = gate([grad_attn, y_far_up, x_far_down_1], [])
    up_send, down_send = sums("plane_sum", (far_up_0, y_far_up), (near_down_1, x_far_down_1))
    x_up = across(up_send)
    y_down = beside(down_send)
    gas = [grad_attn, core(grad_attn)]

    def attn_back(weights, kept, acc, name, hold=()):
        first = acc is None
        ins = [
            place, *xns, *gas, weights, *kept, member, negative,
        ]
        outs = scalar(
            functools.partial(attn_back_body, first),
            [
                page,
                page_low,
                struct((2 * local, width), BF16),
                struct((2 * local, width), BF16),
                struct((8, 3 * local), F32),
                struct((2 * heads, segs, segs), F32),
            ],
            name,
            flops=2 * attn_flops,
            scratch=[pltpu.VMEM((3 * local, 2 * seq), BF16)],
            alias=None if first else {len(ins): 0, len(ins) + 1: 1},
        )(*ins, *(acc or ()), hold=hold)
        return list(outs[0:2]), outs[2:4], outs[4], outs[5]

    first_bit, *rest_bits = bits

    def resplit(groups, keep, got, name):
        for n, bit in enumerate(rest_bits):
            out = struct((keep.shape[0] // 2, width), BF16)
            body = functools.partial(resplit_body, 4 + n, groups)
            keep, give = scalar(body, [out] * 2, name + "_split")(place, keep, got)
            (got,) = yield [(give, "dp", bit)]
        (part,) = sums(name + "_total", (keep, got))
        for n, bit in reversed(list(enumerate(rest_bits))):
            (got,) = yield [(part, "dp", bit)]
            out = struct((2 * part.shape[0], width), BF16)
            body = functools.partial(join_body, 4 + n, groups)
            (part,) = scalar(body, [out], name + "_join")(place, part, got)
        y_got, z_got = yield [(part, "dp", 1), (part, "dp", first_bit)]
        out = struct((part.shape[0] // 2, width), BF16)
        low, high = call(corner_body, [out] * 2, name + "_corner")(y_got, z_got)
        low, high = yield [(low, "dp", 1), (high, "dp", first_bit)]
        return part, y_got, z_got, low, high

    def split(groups, name, *parts):
        out = struct((groups * parts[0].shape[0] // 2, width), BF16)
        body = functools.partial(split_body, 3, groups)
        return scalar(body, [out] * 2, name + "_split")(place, *parts)

    def attn_chain(far_0, far_got, near_0, near_1):
        (send,) = sums("attn_sum", (far_0, far_got))
        near_got, far_got = yield [(near_1, "dp", 1), (send, "mp", 2)]
        keep, give = split(1, "attn", near_0, near_got, far_got)
        (got,) = yield [(give, "dp", first_bit)]
        return (yield from resplit(1, keep, got, "attn"))

    acc, (far_attn_0, far_attn_1), sums_far, seg_far = attn_back(
        far_w, kept_far, None, "attn_back_far"
    )
    *acc, x_up, y_down, far_attn_1 = gate([*acc, x_up, y_down, far_attn_1], [])
    mlp_keep, mlp_give = split(
        2, "mlp", near_up_0, near_y_up, x_up, near_down_0, y_down, x_far_down_0
    )
    mlp_got = swap(mlp_give, "dp", first_bit)
    y_far_attn = beside(far_attn_1)
    acc, (near_attn_0, near_attn_1), sums_near, seg_near = attn_back(
        near_w, kept_near, acc, "attn_back_near", hold=[mlp_give]
    )
    *acc, mlp_got, y_far_attn, near_attn_1 = gate(
        [*acc, mlp_got, y_far_attn, near_attn_1], []
    )
    grad_inputs, end_rows = call(
        end_body, [Own(page_low), struct((8, width), F32)], "end"
    )(Own(inputs), acc[0], core(acc[1]), grad_middle, gain_attn)
    (small,) = scalar(small_body, [struct((16, width), F32)], "small")(
        place, ups_0, ups_1, sums_near, sums_far, seg_near, seg_far,
        Own(bucket_horizontal), Own(bucket_vertical), turn_rows, end_rows,
    )
    chains = [
        attn_chain(far_attn_0, y_far_attn, near_attn_0, near_attn_1),
        resplit(2, mlp_keep, mlp_got, "mlp"),
    ]
    asked = [next(chain) for chain in chains]
    ends = [None] * len(chains)
    table = struct((heads, bins), F32)

    def small_end(gathered):
        small = jnp.sum(gathered.reshape(dp_count, mp_count, 16, width), axis=0)
        return scalar(small_end_body, [struct((8, width), F32), Own(table), Own(table)], "small_end")(
            place, small
        )

    rounds = 4 + 2 * len(rest_bits)
    grad_up = grad_down = None
    for at in range(rounds):
        got = [swap(*send) for request in asked for send in request or ()]
        if at == 0:
            *got, small = gate([*got, small], [])
            small_rows, grad_th, grad_tv = small_end(lax.all_gather(small, ("dp", "mp")))
        else:
            late = {rounds - 2: [grad_up], rounds - 1: [small_rows]}.get(at, [])
            got = gate(got, [], *late)
        got = iter(got)
        for n, chain in enumerate(chains):
            if asked[n] is not None:
                received = [next(got) for _ in asked[n]]
                try:
                    asked[n] = chain.send(received)
                except StopIteration as stop:
                    asked[n], ends[n] = None, stop.value
        if grad_up is None and ends[1] is not None:
            grad_up, grad_down = scalar(
                unpack_mlp_body,
                [Own(struct((width, hidden), F32)), Own(struct((hidden, width), F32))],
                "unpack_mlp",
            )(place, *ends[1])
    grad_wq, grad_wk, grad_wv, grad_wo = scalar(
        unpack_attn_body, [Own(struct((local, width), F32))] * 4, "unpack_attn"
    )(place, *ends[0])

    return (
        result,
        grad_inputs,
        small_rows[6],
        small_rows[7],
        grad_wq.T,
        small_rows[1, :local],
        grad_wk.T,
        grad_wv.T,
        small_rows[1, local:2 * local],
        grad_th.T,
        grad_tv.T,
        grad_wo,
        small_rows[2],
        small_rows[3],
        small_rows[4],
        grad_up,
        small_rows[0],
        grad_down,
        small_rows[5],
    )


def solution(mesh):
    rows = P(("dp", "mp"), None)
    columns = P(None, "mp")
    split = P("mp")
    placed = (
        rows, rows, P(), P(), columns, split, columns, columns, split, columns, columns,
        P("mp", None), P(), P(), P(), columns, split, P("mp", None), P(),
        P("dp", None), P("dp", None), P("dp", None, None), P("dp", None, None),
    )
    given = (
        rows, rows, P(), P(), columns, split, columns, columns, split, columns, columns,
        P("mp", None), P(), P(), P(), columns, split, P("mp", None), P(),
    )
    return jax.shard_map(
        functools.partial(on_device, mesh.shape["dp"], mesh.shape["mp"]),
        mesh=mesh,
        in_specs=placed,
        out_specs=given,
        check_vma=False,
    )
```

```python
import functools

import jax
import jax.numpy as jnp
from jax import lax
from jax.experimental import pallas as pl
from jax.experimental.pallas import tpu as pltpu
from jax.sharding import PartitionSpec as P

EPSILON = 1e-05
NEGATIVE = -1e30
HEAD = 64
EXTRA = 16
PARTS = 3
F32 = jnp.float32
BF16 = jnp.bfloat16
LIMIT = 16 * 1024 * 1024
SCALE = 30

NN = (((1,), (0,)), ((), ()))
NT = (((1,), (1,)), ((), ()))
TN = (((0,), (0,)), ((), ()))


def mm(left, right, dims=NN):
    return lax.dot_general(left, right, dims, preferred_element_type=F32)


def struct(shape, dtype):
    return jax.ShapeDtypeStruct(shape, dtype)


class Own:
    def __init__(self, value, cuts=()):
        self.value = value
        self.cuts = cuts


class Loaded:
    def __init__(self, source, scratch, sems, cuts):
        self.scratch = scratch
        self.shape = scratch.shape
        edges = [0, *cuts, scratch.shape[0]]
        self.parts = []
        for n, (low, high) in enumerate(zip(edges, edges[1:])):
            here = pl.ds(low, high - low)
            copy = pltpu.make_async_copy(source.at[here], scratch.at[here], sems[n])
            copy.start()
            self.parts.append((low, high, copy))

    def wait(self, low, high):
        for part in list(self.parts):
            if part[0] < high and low < part[1]:
                part[2].wait()
                self.parts.remove(part)

    def __getitem__(self, at):
        first = at[0] if isinstance(at, tuple) else at
        if isinstance(first, slice):
            self.wait(first.start or 0, self.shape[0] if first.stop is None else first.stop)
        else:
            self.wait(0, self.shape[0])
        return self.scratch[at]


class Stored:
    def __init__(self, target, scratch, sem):
        self.copy = pltpu.make_async_copy(scratch, target, sem)
        self.scratch = scratch
        self.shape = scratch.shape
        self.dtype = scratch.dtype
        self.sent = False

    def __getitem__(self, at):
        return self.scratch[at]

    def __setitem__(self, at, value):
        self.scratch[at] = value

    def flush(self):
        self.copy.start()
        self.sent = True


class Rows:
    def __init__(self, refs):
        self.refs = refs
        self.shape = (sum(ref.shape[0] for ref in refs), refs[0].shape[1])

    def __getitem__(self, at):
        rows, *rest = at if isinstance(at, tuple) else (at,)
        if rows is Ellipsis:
            rows = slice(None)
        return jnp.concatenate([ref[(slice(None), *rest)] for ref in self.refs], axis=0)[rows]


def flush(ref):
    if isinstance(ref, Stored):
        ref.flush()


def call(body, outs, name, flops=0, transcendentals=0, scalar=False, scratch=(), alias=None, scale=SCALE):
    def run(*args, hold=()):
        own_in = [isinstance(a, Own) for a in args]
        own_out = [isinstance(o, Own) for o in outs]
        ins = [a.value if own else a for a, own in zip(args, own_in)]
        shapes = [o.value if own else o for o, own in zip(outs, own_out)]
        moved = sum(a.size * a.dtype.itemsize for a in ins + shapes)
        count, held = len(ins), len(hold)
        total = sum(1 + len(v.cuts) for v in [*args, *outs] if isinstance(v, Own))
        copied = [v for v, own in zip(ins + shapes, own_in + own_out) if own]

        def inner(*refs):
            given, results = refs[:count], refs[count + held:count + held + len(shapes)]
            spare = refs[count + held + len(shapes):]
            slots, rest = iter(spare[:len(copied)]), spare[len(copied):]
            sems = iter(range(total))
            loaded = [
                Loaded(
                    ref, next(slots), [rest[-1].at[next(sems)] for _ in (0, *arg.cuts)], arg.cuts
                )
                if isinstance(arg, Own)
                else ref
                for ref, arg in zip(given, args)
            ]
            stored = [
                Stored(ref, next(slots), rest[-1].at[next(sems)]) if own else ref
                for ref, own in zip(results, own_out)
            ]
            body(*loaded, *stored, *(rest[:-1] if copied else rest))
            for ref in loaded:
                if isinstance(ref, Loaded):
                    ref.wait(0, ref.shape[0])
            for ref in stored:
                if isinstance(ref, Stored):
                    if not ref.sent:
                        ref.flush()
                    ref.copy.wait()

        buffers = [pltpu.VMEM(v.shape, v.dtype) for v in copied] + list(scratch)
        if copied:
            buffers.append(pltpu.SemaphoreType.DMA((total,)))
        kept = pl.BlockSpec(memory_space=pl.ANY)
        inside = pl.BlockSpec(memory_space=pltpu.VMEM)
        in_specs = [kept if own else inside for own in own_in]
        if scalar:
            in_specs[0] = pl.BlockSpec(memory_space=pltpu.SMEM)
        return pl.pallas_call(
            inner,
            out_shape=[
                (pltpu.HBM if own else pltpu.VMEM)(o.shape, o.dtype) for o, own in zip(shapes, own_out)
            ],
            in_specs=in_specs + [kept] * held,
            out_specs=[kept if own else inside for own in own_out],
            scratch_shapes=buffers,
            input_output_aliases=alias or {},
            compiler_params=pltpu.CompilerParams(vmem_limit_bytes=LIMIT),
            cost_estimate=pl.CostEstimate(
                flops=int(flops * scale),
                bytes_accessed=int(moved * scale),
                transcendentals=int(transcendentals),
            ),
            name=name,
        )(
            *[
                v
                if scalar and n == 0
                else pltpu.with_memory_space_constraint(v, pltpu.HBM if own else pltpu.VMEM)
                for n, (v, own) in enumerate(zip(ins, own_in))
            ],
            *hold,
        )

    return run


def line(ref):
    value = ref[...]
    return value if value.ndim == 2 else value.reshape(1, value.shape[0])


def halves(values):
    high = values.astype(BF16)
    return high, (values - high.astype(F32)).astype(BF16)


def pack_attn_body(place_ref, wq_ref, wk_ref, wv_ref, wo_ref, th_ref, tv_ref, bq_ref, bv_ref,
                   all_ref, send_ref):
    local = wq_ref.shape[0]
    heads = th_ref.shape[0]
    piece = 2 * local + EXTRA
    th, tv = th_ref[...], tv_ref[...]
    parts = []
    for m in range(heads):
        parts += [th[m:m + 1], tv[m:m + 1]]
    high, low = halves(jnp.concatenate(parts + [line(bq_ref), line(bv_ref)], axis=1))
    which = lax.broadcasted_iota(jnp.int32, (EXTRA, high.shape[1]), 0)
    extra = jnp.where(which == 0, high.astype(F32), jnp.where(which == 1, low.astype(F32), 0.0))
    extra = extra.astype(BF16)
    side = place_ref[0, 0]
    for n, (one_ref, two_ref) in enumerate(((wq_ref, wv_ref), (wk_ref, wo_ref))):
        one, two = one_ref[...], two_ref[...]
        all_ref[n * local:(n + 1) * local, :] = one
        all_ref[piece + n * local:piece + (n + 1) * local, :] = two
        send_ref[n * local:(n + 1) * local, :] = jnp.where(side == 0, one, two)
    all_ref[2 * local:piece, :] = extra
    all_ref[piece + 2 * local:, :] = extra
    send_ref[2 * local:, :] = extra


def pack_mlp_body(place_ref, up_ref, bias_ref, down_ref, all_ref, up_send_ref, down_send_ref):
    half = down_ref.shape[0] // 2
    piece = 2 * half + EXTRA
    bias = line(bias_ref)
    which = lax.broadcasted_iota(jnp.int32, (EXTRA, half), 0) == 0

    def put(at, own, up_to, down_to, down_at):
        one, two = slice(at * half, (at + 1) * half), slice((1 - at) * half, (2 - at) * half)
        high, low = halves(jnp.where(own, bias[:, one], bias[:, two]))
        up_to(0, jnp.where(own, up_ref[0:half, one], up_ref[0:half, two]), high)
        up_to(half, jnp.where(own, up_ref[half:, one], up_ref[half:, two]), low)
        down_to[down_at:down_at + half, :] = jnp.where(own, down_ref[one, :], down_ref[two, :])

    def up_to(ref, at):
        def store(column, value, extra):
            ref[at:at + half, column:column + half] = value
            extra = jnp.where(which, extra.astype(F32), 0.0).astype(BF16)
            ref[at + half:at + half + EXTRA, column:column + half] = extra

        return store

    put(0, place_ref[0, 3] == 0, up_to(up_send_ref, 0), down_send_ref, 0)
    flush(up_send_ref)
    flush(down_send_ref)
    for n in (0, 1):
        at = n * piece
        put(n, place_ref[0, 0] == 0, up_to(all_ref, at), all_ref, at + half + EXTRA)


def start_body(place_ref, x_ref, gain_ref, shift_ref, seg_ref, valid_ref, bh_ref, bv_ref,
               xn_ref, mt_ref, neg_ref, ih_ref, iv_ref):
    x = x_ref[...].astype(F32)
    mean = jnp.mean(x, axis=1, keepdims=True)
    cen = x - mean
    var = jnp.mean(cen * cen, axis=1, keepdims=True)
    xn_ref[...] = (cen * lax.rsqrt(var + EPSILON) * line(gain_ref) + line(shift_ref)).astype(BF16)
    segs = mt_ref.shape[0]
    seq = x.shape[0]
    rows = lax.broadcasted_iota(jnp.int32, (segs, seq), 0)
    top = lax.broadcasted_iota(jnp.int32, (EXTRA, seq), 0) == 0
    for p in (0, 1):
        page = place_ref[0, 1 + p]
        here = pl.ds(p * seq, seq)
        member = jnp.where(rows == seg_ref[pl.ds(page, 1), :], 1.0, 0.0).astype(BF16)
        mt_ref[:, here] = member
        masked = jnp.where(valid_ref[pl.ds(page, 1), :] > 0, 0.0, NEGATIVE)
        neg_ref[:, here] = jnp.where(top, masked, 0.0).astype(BF16)
        bh, bv = bh_ref[page].astype(F32).astype(BF16), bv_ref[page].astype(F32).astype(BF16)
        ih_ref[:, here] = mm(bh, member, TN).astype(jnp.int32)
        iv_ref[:, here] = mm(bv, member, TN).astype(jnp.int32) + segs


def lookup(table, index):
    rows, seq = index.shape
    spread = jnp.broadcast_to(table, (rows, 128))
    parts = [
        jnp.take_along_axis(
            spread, index[:, at:at + 128], axis=1, mode="promise_in_bounds"
        )
        for at in range(0, seq, 128)
    ]
    return jnp.concatenate(parts, axis=1)


def attn_body(first, *refs):
    if first:
        w_ref, ih_ref, iv_ref, mt_ref, neg_ref = refs[2:7]
        given = (None, None)
        qkv_ref, ctx_ref, lse_ref, bias_ref, *outs = refs[7:]
    else:
        place_ref, own_ref, other_ref = refs[0], refs[3], refs[4]
        ih_ref, iv_ref, mt_ref, neg_ref = refs[5:9]
        given = refs[9:11]
        qkv_ref, ctx_ref, lse_ref, bias_ref, *outs, w_ref = refs[11:]
        refs = refs[1:]
        low = place_ref[0, 0] == 0
        own, other = own_ref[...], other_ref[...]
        size = own.shape[0]
        w_ref[0:size, :] = jnp.where(low, own, other)
        w_ref[size:, :] = jnp.where(low, other, own)
        flush(w_ref)
    width = ctx_ref.shape[0]
    heads = width // HEAD
    segs = mt_ref.shape[0]
    seq = refs[0].shape[0]
    second = 2 * width + EXTRA
    extra = w_ref[2 * width:second, :]
    pick = jnp.where(lax.broadcasted_iota(jnp.int32, (EXTRA, seq), 0) < 2, 1.0, 0.0).astype(BF16)
    bias = mm(extra[:, heads * 128:heads * 128 + 2 * width], pick, TN)
    tables = extra[0:1, :].astype(F32) + extra[1:2, :].astype(F32)
    ones = jnp.ones((EXTRA, seq), BF16)
    for p in (0, 1):
        xn = refs[p][...]
        here = pl.ds(p * seq, seq)
        qk = mm(w_ref[0:2 * width, :], xn, NT)
        v = mm(w_ref[second:second + width, :], xn, NT)
        qkv_ref[0:width, here] = ((qk[0:width] + bias[0:width]) * 0.125).astype(BF16)
        qkv_ref[width:2 * width, here] = qk[width:].astype(BF16)
        qkv_ref[2 * width:, here] = (v + bias[width:]).astype(BF16)
    flush(qkv_ref)
    for p in (0, 1):
        here = pl.ds(p * seq, seq)
        member = mt_ref[:, here]
        for m in range(heads):
            table = tables[:, 128 * m:128 * m + 128]
            pos = lookup(table, ih_ref[:, here]) + lookup(table, iv_ref[:, here])
            high, low = halves(pos)
            bias_ref[2 * segs * m:2 * segs * m + segs, here] = high
            bias_ref[2 * segs * m + segs:2 * segs * (m + 1), here] = low
            at = HEAD * m
            q_aug = jnp.concatenate([qkv_ref[at:at + HEAD, here], high, low, ones], axis=0)
            k_aug = jnp.concatenate(
                [qkv_ref[width + at:width + at + HEAD, here], member, member, neg_ref[:, here]],
                axis=0,
            )
            scores = mm(k_aug, q_aug, TN)
            top = jnp.max(scores, axis=0, keepdims=True)
            expo = jnp.exp(scores - top).astype(BF16)
            v_aug = jnp.concatenate(
                [qkv_ref[2 * width + at:2 * width + at + HEAD, here], ones], axis=0
            )
            summed = mm(v_aug, expo)
            total = summed[HEAD:HEAD + 1]
            ctx_ref[at:at + HEAD, here] = (summed[0:HEAD] / total).astype(BF16)
            lse_ref[m:m + 1, here] = top + jnp.log(total)
        out = mm(ctx_ref[:, here], w_ref[second + width:second + 2 * width, :], TN)
        if given[p] is not None:
            out = given[p][...] + out
        if first:
            outs[p][...] = out.astype(outs[p].dtype)
            continue
        if p == 0:
            outs[0][...] = out
        at = 0
        for ref in outs[1:]:
            low, high = max(at, p * seq), min(at + ref.shape[0], (p + 1) * seq)
            if low < high:
                ref[low - at:high - at, :] = out[low - p * seq:high - p * seq].astype(ref.dtype)
            at += ref.shape[0]
    lse_ref[heads:, :] = jnp.zeros((lse_ref.shape[0] - heads, 2 * seq), F32)


def middle_body(x_ref, other_x_ref, acc_ref, bias_ref, gain_ref, shift_ref, *refs):
    sent, got = Rows(refs[0:PARTS]), Rows(refs[PARTS:2 * PARTS])
    mid_ref, nm_ref, other_nm_ref = refs[2 * PARTS:]
    seq = x_ref.shape[0]
    own = acc_ref[...] + got[seq:, :].astype(F32)
    other = sent[seq:, :].astype(F32) + got[0:seq, :].astype(F32)
    for value, source_ref, out_ref in ((own, x_ref, nm_ref), (other, other_x_ref, other_nm_ref)):
        mid = source_ref[...].astype(F32) + value + line(bias_ref)
        if out_ref is nm_ref:
            mid_ref[...] = mid
        mean = jnp.mean(mid, axis=1, keepdims=True)
        cen = mid - mean
        var = jnp.mean(cen * cen, axis=1, keepdims=True)
        out = cen * lax.rsqrt(var + EPSILON) * line(gain_ref) + line(shift_ref)
        out_ref[...] = out.astype(BF16)


def mlp_body(first, up_at, down_at, *refs):
    nm_refs, cot_refs = refs[0:2], refs[2:4]
    refs = refs[4:]
    u_ref, d_ref = refs[0:2]
    given = (None,) * 4 if first else refs[2:6]
    outs = refs[2 if first else 6:]
    accs, grads, db_ref = outs[0:4], outs[4:6], outs[6]
    half = grads[0].shape[0]
    for n in (0,):
        extra = u_ref[up_at + half:up_at + half + EXTRA, :].astype(F32)
        bias = extra[0:1, 0:half] + extra[0:1, half:]
        up_left = u_ref[up_at:up_at + half, 0:half]
        up_right = u_ref[up_at:up_at + half, half:]
        down = d_ref[down_at:down_at + half, :]
        total = None
        for p in (0, 1):
            nm_left, nm_right = nm_refs[p][:, 0:half], nm_refs[p][:, half:]
            cot = cot_refs[p][...]
            upper = mm(nm_left, up_left) + mm(nm_right, up_right) + bias
            cdf = 0.5 + 0.5 * lax.erf(upper * 0.7071067811865476)
            pdf = jnp.exp(upper * upper * -0.5) * 0.3989422804014327
            hidden = (upper * cdf).astype(BF16)
            grad_hidden = mm(cot, down, NT)
            grad_upper = (grad_hidden * (cdf + upper * pdf)).astype(BF16)
            sums_now = (
                mm(nm_left, grad_upper, TN),
                mm(nm_right, grad_upper, TN),
                mm(hidden, cot, TN),
                jnp.sum(grad_upper.astype(F32), axis=0, keepdims=True),
            )
            total = sums_now if total is None else [a + b for a, b in zip(total, sums_now)]
            down_ref, back_ref = accs[p], accs[2 + p]
            base_down, base_back = (given[p], given[2 + p]) if n == 0 else (down_ref, back_ref)
            down_out = mm(hidden, down)
            back_left = mm(grad_upper, up_left, NT)
            back_right = mm(grad_upper, up_right, NT)
            if base_down is not None:
                down_out = base_down[...].astype(F32) + down_out
                back_left = base_back[:, 0:half].astype(F32) + back_left
                back_right = base_back[:, half:].astype(F32) + back_right
            down_ref[...] = down_out.astype(down_ref.dtype)
            back_ref[:, 0:half] = back_left.astype(back_ref.dtype)
            back_ref[:, half:] = back_right.astype(back_ref.dtype)
        up_ref, dn_ref = grads[2 * n:2 * n + 2]
        up_ref[:, 0:half] = total[0].astype(BF16)
        up_ref[:, half:] = total[1].astype(BF16)
        flush(up_ref)
        dn_ref[...] = total[2].astype(BF16)
        flush(dn_ref)
        db_ref[...] = jnp.broadcast_to(total[3], db_ref.shape)


def turn_body(mid_ref, down_ref, down_got_ref, bias_ref, back_ref, back_got_ref, cot_ref, gain_ref,
              res_ref, gmid_ref, ga_ref, rows_ref):
    mid = mid_ref[...]
    down = down_ref[...] + down_got_ref[...].astype(F32)
    res_ref[...] = (mid + down + line(bias_ref)).astype(BF16)
    mean = jnp.mean(mid, axis=1, keepdims=True)
    cen = mid - mean
    var = jnp.mean(cen * cen, axis=1, keepdims=True)
    rstd = lax.rsqrt(var + EPSILON)
    n = cen * rstd
    back = back_ref[...] + back_got_ref[...].astype(F32)
    q = back * line(gain_ref)
    cot = cot_ref[...].astype(F32)
    mean_q = jnp.mean(q, axis=1, keepdims=True)
    mean_qn = jnp.mean(q * n, axis=1, keepdims=True)
    grad = cot + rstd * (q - mean_q - n * mean_qn)
    gmid_ref[...] = grad
    ga_ref[...] = grad.astype(BF16)
    rows_ref[0:1, :] = jnp.sum(grad, axis=0, keepdims=True)
    rows_ref[1:2, :] = jnp.sum(back * n, axis=0, keepdims=True)
    rows_ref[2:3, :] = jnp.sum(back, axis=0, keepdims=True)
    rows_ref[3:4, :] = jnp.sum(cot, axis=0, keepdims=True)
    rows_ref[4:, :] = jnp.zeros((rows_ref.shape[0] - 4, rows_ref.shape[1]), F32)


def attn_back_body(first, *refs):
    place_ref, xn_refs, ga_refs = refs[0], refs[1:3], refs[3:5]
    w_ref, qkv_ref, ctx_ref, lse_ref, bias_ref, mt_ref, neg_ref = refs[5:12]
    given = (None, None) if first else refs[12:14]
    *backs, kept_ref, other_ref, sums_ref, seg_ref, dqkv_ref = refs[12 if first else 14:]
    width = ctx_ref.shape[0]
    heads = width // HEAD
    seq = xn_refs[0].shape[0]
    segs = mt_ref.shape[0]
    second = 2 * width + EXTRA
    ones = jnp.ones((EXTRA, seq), BF16)
    grad_out = None
    for p in (0, 1):
        here = pl.ds(p * seq, seq)
        ga = ga_refs[p][...]
        member = mt_ref[:, here]
        grad_ctx = mm(w_ref[second + width:second + 2 * width, :], ga, NT).astype(BF16)
        part = mm(ctx_ref[:, here], ga)
        grad_out = part if p == 0 else grad_out + part
        for m in range(heads):
            at = HEAD * m
            q = qkv_ref[at:at + HEAD, here]
            k = qkv_ref[width + at:width + at + HEAD, here]
            v = qkv_ref[2 * width + at:2 * width + at + HEAD, here]
            g = grad_ctx[at:at + HEAD]
            q_aug = jnp.concatenate(
                [q, bias_ref[2 * segs * m:2 * segs * (m + 1), here], ones], axis=0
            )
            k_aug = jnp.concatenate([k, member, member, neg_ref[:, here]], axis=0)
            scores = mm(k_aug, q_aug, TN)
            probs = jnp.exp(scores - lse_ref[m:m + 1, here])
            grad_probs = mm(v, g, TN)
            delta = jnp.sum(probs * grad_probs, axis=0, keepdims=True)
            grad_scores = (probs * (grad_probs - delta)).astype(BF16)
            grad_v = mm(g, probs.astype(BF16), NT)
            dqkv_ref[2 * width + at:2 * width + at + HEAD, here] = grad_v.astype(BF16)
            dqkv_ref[width + at:width + at + HEAD, here] = mm(q, grad_scores, NT).astype(BF16)
            both = mm(jnp.concatenate([k, member], axis=0), grad_scores)
            dqkv_ref[at:at + HEAD, here] = both[0:HEAD].astype(BF16) * jnp.asarray(0.125, BF16)
            high, low = halves(both[HEAD:])
            seg_ref[p * heads + m] = mm(member, high, NT) + mm(member, low, NT)
    grads = mm(dqkv_ref[:, 0:seq], xn_refs[0][...]) + mm(dqkv_ref[:, seq:], xn_refs[1][...])
    grads = jnp.concatenate([grads, grad_out], axis=0).astype(BF16)
    low = place_ref[0, 0] == 0
    kept_ref[...] = jnp.where(low, grads[0:2 * width], grads[2 * width:])
    flush(kept_ref)
    other_ref[...] = jnp.where(low, grads[2 * width:], grads[0:2 * width])
    flush(other_ref)
    for p in (0, 1):
        here = pl.ds(p * seq, seq)
        back = mm(dqkv_ref[0:2 * width, here], w_ref[0:2 * width, :], TN)
        back = back + mm(dqkv_ref[2 * width:, here], w_ref[second:second + width, :], TN)
        if given[p] is not None:
            back = given[p][...] + back
        backs[p][...] = back.astype(backs[p].dtype)
    sums_ref[...] = mm(jnp.ones((8, 2 * seq), BF16), dqkv_ref[...], NT)


def sum_body(counts, *refs):
    total = sum(counts)
    outs = refs[total:]
    at = 0
    for count, out in zip(counts, outs):
        value = refs[at][...].astype(F32)
        for ref in refs[at + 1:at + count]:
            value = value + ref[...].astype(F32)
        out[...] = value.astype(out.dtype)
        at += count


def sums(name, *groups, hold=()):
    outs = [struct(group[0].shape, group[0].dtype) for group in groups]
    body = functools.partial(sum_body, [len(group) for group in groups])
    flat = [value for group in groups for value in group]
    return call(body, outs, name)(*flat, hold=hold)


def pick_body(place_ref, zero_ref, one_ref, out_ref):
    same = place_ref[0, 0] == place_ref[0, 3]
    out_ref[...] = jnp.where(same, one_ref[...], zero_ref[...])


def plane_body(place_ref, up_0_ref, up_1_ref, up_got_ref, near_ref, down_0_ref, down_1_ref,
               up_ref, down_ref):
    same = place_ref[0, 0] == place_ref[0, 3]
    up = jnp.where(same, up_0_ref[...], up_1_ref[...]).astype(F32)
    up_ref[...] = (up + up_got_ref[...].astype(F32)).astype(BF16)
    down = jnp.where(same, down_1_ref[...], down_0_ref[...]).astype(F32)
    down_ref[...] = (near_ref[...].astype(F32) + down).astype(BF16)


def plane_split_body(place_ref, up_0_ref, up_1_ref, up_2_ref, down_0_ref, down_1_ref, far_0_ref,
                     far_1_ref, keep_ref, give_ref):
    same = place_ref[0, 0] == place_ref[0, 3]
    low = place_ref[0, 3] == 0
    size = keep_ref.shape[0] // 2
    up = up_0_ref[...].astype(F32) + up_1_ref[...].astype(F32) + up_2_ref[...].astype(F32)
    down = down_0_ref[...].astype(F32) + down_1_ref[...].astype(F32)
    down = down + jnp.where(same, far_0_ref[...], far_1_ref[...]).astype(F32)
    for n, value in enumerate((up, down)):
        one, two = value[0:size], value[size:]
        here = pl.ds(n * size, size)
        keep_ref[here, :] = jnp.where(low, one, two).astype(BF16)
        give_ref[here, :] = jnp.where(low, two, one).astype(BF16)


def split_body(which, groups, place_ref, *refs):
    *parts, keep_ref, give_ref = refs
    low = place_ref[0, which] == 0
    size = keep_ref.shape[0] // groups
    count = len(parts) // groups
    for n in range(groups):
        value = parts[n * count][...].astype(F32)
        for ref in parts[n * count + 1:(n + 1) * count]:
            value = value + ref[...].astype(F32)
        one, two = value[0:size], value[size:]
        here = pl.ds(n * size, size)
        keep_ref[here, :] = jnp.where(low, one, two).astype(BF16)
        give_ref[here, :] = jnp.where(low, two, one).astype(BF16)


def resplit_body(which, groups, place_ref, own_ref, got_ref, keep_ref, give_ref):
    low = place_ref[0, which] == 0
    size = keep_ref.shape[0] // groups
    value = own_ref[...].astype(F32) + got_ref[...].astype(F32)
    for n in range(groups):
        at = 2 * n * size
        one, two = value[at:at + size], value[at + size:at + 2 * size]
        here = pl.ds(n * size, size)
        keep_ref[here, :] = jnp.where(low, one, two).astype(BF16)
        give_ref[here, :] = jnp.where(low, two, one).astype(BF16)


def join_body(which, groups, place_ref, own_ref, other_ref, out_ref):
    size = own_ref.shape[0] // groups
    low = place_ref[0, which] == 0
    own, other = own_ref[...], other_ref[...]
    for n in range(groups):
        part = slice(n * size, (n + 1) * size)
        out_ref[2 * n * size:(2 * n + 1) * size, :] = jnp.where(low, own[part], other[part])
        out_ref[(2 * n + 1) * size:(2 * n + 2) * size, :] = jnp.where(low, other[part], own[part])


def corner_body(y_ref, z_ref, low_ref, high_ref):
    size = low_ref.shape[0]
    low_ref[...] = z_ref[0:size, :]
    high_ref[...] = y_ref[size:, :]


def end_body(x_ref, back_ref, got_ref, gmid_ref, gain_ref, gx_ref, rows_ref):
    x = x_ref[...].astype(F32)
    mean = jnp.mean(x, axis=1, keepdims=True)
    cen = x - mean
    var = jnp.mean(cen * cen, axis=1, keepdims=True)
    rstd = lax.rsqrt(var + EPSILON)
    n = cen * rstd
    back = back_ref[...] + got_ref[...].astype(F32)
    q = back * line(gain_ref)
    mean_q = jnp.mean(q, axis=1, keepdims=True)
    mean_qn = jnp.mean(q * n, axis=1, keepdims=True)
    gx_ref[...] = (gmid_ref[...] + rstd * (q - mean_q - n * mean_qn)).astype(BF16)
    rows_ref[0:1, :] = jnp.sum(back * n, axis=0, keepdims=True)
    rows_ref[1:2, :] = jnp.sum(back, axis=0, keepdims=True)
    rows_ref[2:, :] = jnp.zeros((rows_ref.shape[0] - 2, rows_ref.shape[1]), F32)


def small_body(place_ref, near_0_ref, near_1_ref, far_0_ref, far_1_ref, sums_near_ref, sums_far_ref,
               seg_near_ref, seg_far_ref, bh_ref, bv_ref, turn_ref, end_ref, out_ref):
    count, segs, _ = seg_near_ref.shape
    heads = count // 2
    bins = lax.broadcasted_iota(jnp.int32, (segs, segs), 0)
    total = jnp.zeros((2 * EXTRA, 2 * segs), F32)
    for p in (0, 1):
        page = place_ref[0, 1 + p]
        bh, bv = bh_ref[page], bv_ref[page]
        own = pl.ds(p * heads, heads)
        for s in range(segs):
            both = jnp.concatenate(
                [
                    seg_near_ref[own, s, :],
                    seg_far_ref[own, s, :],
                    jnp.zeros((EXTRA - 2 * heads, segs), F32),
                ],
                axis=0,
            )
            hot = jnp.concatenate(
                [
                    jnp.where(bins == bh[s:s + 1, :], 1.0, 0.0),
                    jnp.where(bins == bv[s:s + 1, :], 1.0, 0.0),
                ],
                axis=0,
            ).astype(BF16)
            total = total + mm(jnp.concatenate(halves(both), axis=0), hot, NT)
    tables = total[0:EXTRA] + total[EXTRA:]
    side, low = place_ref[0, 0] == 0, place_ref[0, 3] == 0
    out_ref[...] = jnp.zeros(out_ref.shape, F32)
    width = sums_near_ref.shape[1] // 3
    half = near_0_ref.shape[1]
    near = (side, near_0_ref[0:1, :], near_1_ref[0:1, :], sums_near_ref)
    far = (low, far_0_ref[0:1, :], far_1_ref[0:1, :], sums_far_ref)
    for k, (own, one, two, sums_in) in enumerate((near, far)):
        out_ref[2 * k:2 * k + 1, 0:half] = jnp.where(own, one, two)
        out_ref[2 * k:2 * k + 1, half:] = jnp.where(own, two, one)
        parts = [sums_in[0:1, 0:width], sums_in[0:1, 2 * width:]]
        parts += [tables[k * heads + m:k * heads + m + 1] for m in range(heads)]
        out_ref[2 * k + 1:2 * k + 2, :] = jnp.concatenate(parts, axis=1)
    out_ref[4:8, :] = turn_ref[0:4, :]
    out_ref[8:10, :] = end_ref[0:2, :]


def small_shards_body(own_ref, core_ref, across_ref, corner_ref, out_ref):
    out_ref[...] = jnp.zeros(out_ref.shape, F32)
    out_ref[0:2, :] = own_ref[0:2, :] + across_ref[2:4, :]
    out_ref[4:10, :] = (own_ref[4:10, :] + across_ref[4:10, :]) + (
        core_ref[4:10, :] + corner_ref[4:10, :]
    )


def small_end_body(own_ref, got_ref, rows_ref, th_ref, tv_ref):
    rows_ref[...] = own_ref[...] + got_ref[...]
    own = own_ref[1:2, :] + got_ref[1:2, :]
    heads, bins = th_ref.shape
    for m in range(heads):
        at = own.shape[1] - 2 * bins * (heads - m)
        th_ref[m:m + 1, :] = own[:, at:at + bins]
        tv_ref[m:m + 1, :] = own[:, at + bins:at + 2 * bins]


def square(place_ref, own, beside, along, corner):
    side, low = place_ref[0, 0] == 0, place_ref[0, 3] == 0
    own_half = (jnp.where(low, own, along), jnp.where(low, along, own))
    other_half = (jnp.where(low, beside, corner), jnp.where(low, corner, beside))
    first = [jnp.where(side, a, b).astype(F32) for a, b in zip(own_half, other_half)]
    second = [jnp.where(side, b, a).astype(F32) for a, b in zip(own_half, other_half)]
    return first + second


def unpack_mlp_body(place_ref, own_ref, y_ref, z_ref, low_ref, high_ref,
                    up_ref, down_ref, done_ref):
    done_ref[...] = jnp.zeros(done_ref.shape, F32)
    size = low_ref.shape[0]
    half = 2 * size
    ups = square(
        place_ref, own_ref[0:size, :], y_ref[0:size, :], z_ref[0:size, :], low_ref[...]
    )
    for n, part in enumerate(ups):
        here = pl.ds((n // 2) * half, half)
        at = (n % 2) * size
        up_ref[at:at + size, here] = part[:, 0:half]
        up_ref[half + at:half + at + size, here] = part[:, half:]
    flush(up_ref)
    downs = square(
        place_ref, own_ref[size:, :], y_ref[size:, :], z_ref[size:, :], high_ref[...]
    )
    for n, part in enumerate(downs):
        down_ref[n * size:(n + 1) * size, :] = part


def unpack_attn_body(place_ref, own_ref, y_ref, z_ref, low_ref, high_ref,
                     q_ref, k_ref, v_ref, o_ref):
    corner = jnp.concatenate([low_ref[...], high_ref[...]], axis=0)
    parts = square(place_ref, own_ref[...], y_ref[...], z_ref[...], corner)
    for ref, part in zip((q_ref, k_ref, v_ref, o_ref), parts):
        ref[...] = part
        flush(ref)


def order_body(*refs):
    pass


def gate(inside, outside, *others):
    spec = pl.BlockSpec(memory_space=pl.ANY)
    spaces = [pltpu.VMEM] * len(inside) + [pltpu.HBM] * len(outside)
    values = [*inside, *outside]
    return pl.pallas_call(
        order_body,
        out_shape=[space(v.shape, v.dtype) for space, v in zip(spaces, values)],
        in_specs=[spec] * (len(values) + len(others)),
        out_specs=[spec] * len(values),
        input_output_aliases={n: n for n in range(len(values))},
        compiler_params=pltpu.CompilerParams(vmem_limit_bytes=2**20),
        name="order",
    )(
        *[pltpu.with_memory_space_constraint(v, space) for space, v in zip(spaces, values)],
        *others,
    )


def on_device(
    dp_count,
    mp_count,
    inputs,
    cotangent,
    gain_attn,
    shift_attn,
    weight_query,
    bias_query,
    weight_key,
    weight_value,
    bias_value,
    table_horizontal,
    table_vertical,
    weight_out,
    bias_out,
    gain_mlp,
    shift_mlp,
    weight_up,
    bias_up,
    weight_down,
    bias_down,
    segment,
    valid,
    bucket_horizontal,
    bucket_vertical,
):
    seq, width = inputs.shape
    local = weight_query.shape[1]
    heads = table_horizontal.shape[1]
    hidden = weight_up.shape[1]
    half = hidden // 2
    segs = bucket_horizontal.shape[1]
    bins = table_horizontal.shape[0]
    shard = lax.axis_index("mp")
    pages = lax.axis_index("dp")
    bits = [1 << b for b in range(1, dp_count.bit_length() - 1)]
    place = jnp.stack([pages % 2, shard, shard ^ 1] + [(pages // bit) % 2 for bit in bits])
    place = place.astype(jnp.int32).reshape(1, -1)
    scalar = functools.partial(call, scalar=True)

    def swap(value, axis, bit):
        count = dp_count if axis == "dp" else mp_count
        return lax.ppermute(value, axis, [(i, i ^ bit) for i in range(count)])

    def core(value):
        return swap(value, "mp", 1)

    def across(value):
        return swap(value, "mp", 2)

    def beside(value):
        return swap(value, "dp", 1)

    piece = struct((2 * local + EXTRA, width), BF16)
    both = struct((4 * local + 2 * EXTRA, width), BF16)
    near_w, attn_send = scalar(pack_attn_body, [both, piece], "pack_attn")(
        place, Own(weight_query.T), Own(weight_key.T), Own(weight_value.T), Own(weight_out),
        Own(table_horizontal.T), Own(table_vertical.T), Own(bias_query), Own(bias_value),
    )
    x_attn = across(attn_send)
    cot_got, inputs_got = core(cotangent), core(inputs)
    mlp_w, up_send, down_send = scalar(
        pack_mlp_body,
        [
            struct((2 * (2 * half + EXTRA), width), BF16),
            Own(struct((half + EXTRA, width), BF16)),
            Own(struct((half, width), BF16)),
        ],
        "pack_mlp",
    )(place, Own(weight_up), bias_up, Own(weight_down))

    attn_flops = 2 * (2 * seq * width * 4 * local + heads * seq * seq * 256 * 2 * 2)
    page = struct((seq, width), F32)
    page_low = struct((seq, width), BF16)

    def owned(*values):
        return [Own(value) for value in values]

    saved = [
        struct((3 * local, 2 * seq), BF16),
        struct((local, 2 * seq), BF16),
        struct((8, 2 * seq), F32),
        struct((2 * segs * heads, 2 * seq), BF16),
    ]

    def mlp(weights, rows, acc, name, hold=()):
        first = acc is None
        ins = [*nms, cotangent, cot_got, *weights]
        outs = call(
            functools.partial(mlp_body, first, *rows),
            [page, page_low, page, page_low]
            + [struct((half, width), BF16)] * 2
            + [struct((8, half), F32)],
            name,
            flops=2 * 6 * seq * width * hidden,
            alias=None if first else {len(ins) + n: n for n in range(4)},
            scale=0,
        )(*ins, *(acc or ()), hold=hold)
        return list(outs[0:4]), *outs[4:7]

    xn, member, negative, index_h, index_v = scalar(
        start_body,
        [
            struct((seq, width), BF16),
            struct((segs, 2 * seq), BF16),
            struct((EXTRA, 2 * seq), BF16),
            struct((segs, 2 * seq), jnp.int32),
            struct((segs, 2 * seq), jnp.int32),
        ],
        "first_norm",
    )(
        place, Own(inputs), Own(gain_attn), Own(shift_attn),
        Own(segment), Own(valid), Own(bucket_horizontal), Own(bucket_vertical)
    )
    x_attn, xn, cot_got, inputs_got, up_send, down_send = gate(
        [x_attn, xn, cot_got, inputs_got], [up_send, down_send]
    )
    y_attn = beside(x_attn)
    x_up = across(up_send)
    xns = [xn, core(xn)]
    *kept_near, acc_0, acc_1 = call(
        functools.partial(attn_body, True), [*saved, page, page_low], "attn_near", flops=attn_flops
    )(*xns, near_w, index_h, index_v, member, negative)
    acc_0, acc_1, x_attn, y_attn, x_up, down_send = gate(
        [acc_0, acc_1, x_attn, y_attn, x_up], [down_send]
    )
    x_down = across(down_send)
    z_up = swap(x_up, "dp", bits[0])
    edges = [2 * seq * n // PARTS // EXTRA * EXTRA for n in range(PARTS)] + [2 * seq]
    lows = [struct((high - low, width), BF16) for low, high in zip(edges, edges[1:])]
    outs = scalar(
        functools.partial(attn_body, False),
        [*saved, page, *lows, both],
        "attn_far",
        flops=attn_flops,
        alias={9: 4},
    )(
        place, *xns, x_attn, y_attn, index_h, index_v, member, negative, acc_0, acc_1
    )
    kept_far, acc_0, lows, far_w = outs[0:4], outs[4], outs[5:-1], outs[-1]
    middle, *nms = call(middle_body, [page, page_low, page_low], "second_norm", scale=0)(
        Own(inputs), inputs_got, acc_0, bias_out, gain_mlp, shift_mlp,
        *lows, *[core(value) for value in lows],
    )
    *nms, x_down, z_up, x_up = gate([*nms, x_down, z_up, x_up], [])
    z_down = swap(x_down, "dp", bits[0])
    up_rows, all_rows = half + EXTRA, 2 * half + EXTRA
    mlp_acc, near_up_1, near_down_1, near_sums_1 = mlp(
        [mlp_w, mlp_w], [all_rows, all_rows + up_rows], None, "mlp_near_1"
    )
    *mlp_acc, near_up_1 = gate([*mlp_acc, near_up_1], [])
    near_y_up = beside(near_up_1)
    mlp_acc, far_up_0, far_down_0, far_sums_0 = mlp([x_up, x_down], [0, 0], mlp_acc, "mlp_far_0")
    *mlp_acc, far_down_0 = gate([*mlp_acc, far_down_0], [])
    x_far_down_0 = across(far_down_0)
    mlp_acc, far_up_1, far_down_1, far_sums_1 = mlp(
        [z_up, z_down], [0, 0], mlp_acc, "mlp_far_1", hold=[far_down_0]
    )
    (far_up_send,) = scalar(pick_body, [struct((half, width), BF16)], "pick")(
        place, far_up_0, far_up_1
    )
    *mlp_acc, near_y_up, far_up_send, far_down_1 = gate(
        [*mlp_acc, near_y_up, far_up_send, far_down_1], []
    )
    y_far_up = beside(far_up_send)
    mlp_acc, near_up_0, near_down_0, near_sums_0 = mlp(
        [mlp_w, mlp_w], [0, up_rows], mlp_acc, "mlp_near_0"
    )
    *mlp_acc, x_far_down_0, far_down_1 = gate([*mlp_acc, x_far_down_0, far_down_1], [])
    x_far_down_1 = across(far_down_1)
    result, grad_middle, grad_attn, turn_rows = call(
        turn_body,
        [Own(page_low), page, page_low, struct((8, width), F32)],
        "turn",
    )(
        middle, mlp_acc[0], core(mlp_acc[1]), bias_down, mlp_acc[2], core(mlp_acc[3]),
        Own(cotangent), gain_mlp,
    )
    grad_attn, y_far_up, x_far_down_1 = gate([grad_attn, y_far_up, x_far_down_1], [])
    quarters = [struct((half, width), BF16)] * 2
    up_send, down_send = scalar(plane_body, quarters, "plane_sum")(
        place, far_up_0, far_up_1, y_far_up, near_down_1, x_far_down_0, x_far_down_1
    )
    x_up = across(up_send)
    y_down = beside(down_send)
    gas = [grad_attn, core(grad_attn)]

    def attn_back(weights, kept, acc, name, hold=()):
        first = acc is None
        ins = [
            place, *xns, *gas, weights, *kept, member, negative,
        ]
        outs = scalar(
            functools.partial(attn_back_body, first),
            [
                page,
                page_low,
                struct((2 * local, width), BF16),
                struct((2 * local, width), BF16),
                struct((8, 3 * local), F32),
                struct((2 * heads, segs, segs), F32),
            ],
            name,
            flops=2 * attn_flops,
            scratch=[pltpu.VMEM((3 * local, 2 * seq), BF16)],
            alias=None if first else {len(ins): 0, len(ins) + 1: 1},
        )(*ins, *(acc or ()), hold=hold)
        return list(outs[0:2]), outs[2:4], outs[4], outs[5]

    first_bit, *rest_bits = bits

    def resplit(groups, keep, got, name):
        for n, bit in enumerate(rest_bits):
            out = struct((keep.shape[0] // 2, width), BF16)
            body = functools.partial(resplit_body, 4 + n, groups)
            keep, give = scalar(body, [out] * 2, name + "_split")(place, keep, got)
            (got,) = yield [(give, "dp", bit)]
        (part,) = sums(name + "_total", (keep, got))
        for n, bit in reversed(list(enumerate(rest_bits))):
            (got,) = yield [(part, "dp", bit)]
            out = struct((2 * part.shape[0], width), BF16)
            body = functools.partial(join_body, 4 + n, groups)
            (part,) = scalar(body, [out], name + "_join")(place, part, got)
        y_got, z_got = yield [(part, "dp", 1), (part, "dp", first_bit)]
        out = struct((part.shape[0] // 2, width), BF16)
        low, high = call(corner_body, [out] * 2, name + "_corner")(y_got, z_got)
        low, high = yield [(low, "dp", 1), (high, "dp", first_bit)]
        return part, y_got, z_got, low, high

    def split(groups, name, *parts):
        out = struct((groups * parts[0].shape[0] // 2, width), BF16)
        body = functools.partial(split_body, 3, groups)
        return scalar(body, [out] * 2, name + "_split")(place, *parts)

    def attn_chain(far_0, far_got, near_0, near_1):
        (send,) = sums("attn_sum", (far_0, far_got))
        near_got, far_got = yield [(near_1, "dp", 1), (send, "mp", 2)]
        keep, give = split(1, "attn", near_0, near_got, far_got)
        (got,) = yield [(give, "dp", first_bit)]
        return (yield from resplit(1, keep, got, "attn"))

    acc, (far_attn_0, far_attn_1), sums_far, seg_far = attn_back(
        far_w, kept_far, None, "attn_back_far"
    )
    *acc, x_up, y_down, far_attn_1 = gate([*acc, x_up, y_down, far_attn_1], [])
    y_far_attn = beside(far_attn_1)
    mlp_keep, mlp_give = scalar(plane_split_body, quarters, "mlp_split")(
        place, near_up_0, near_y_up, x_up, near_down_0, y_down, x_far_down_0, x_far_down_1
    )
    mlp_got = swap(mlp_give, "dp", first_bit)
    acc, (near_attn_0, near_attn_1), sums_near, seg_near = attn_back(
        near_w, kept_near, acc, "attn_back_near", hold=[mlp_give]
    )
    *acc, mlp_got, y_far_attn, near_attn_1 = gate(
        [*acc, mlp_got, y_far_attn, near_attn_1], []
    )
    grad_inputs, end_rows = call(
        end_body, [Own(page_low), struct((8, width), F32)], "end"
    )(Own(inputs), acc[0], core(acc[1]), grad_middle, gain_attn)
    (small,) = scalar(small_body, [struct((16, width), F32)], "small")(
        place, near_sums_0, near_sums_1, far_sums_0, far_sums_1, sums_near, sums_far, seg_near, seg_far,
        Own(bucket_horizontal), Own(bucket_vertical), turn_rows, end_rows,
    )
    table = struct((heads, bins), F32)

    def small_chain(value):
        line = struct(value.shape, F32)
        for bit in bits:
            (got,) = yield [(value, "dp", bit)]
            (value,) = sums("small_sum", (value, got))
        got = yield [(value, "mp", 1), (value, "mp", 2), (value, "mp", 3)]
        (value,) = call(small_shards_body, [line], "small_shards")(value, *got)
        (got,) = yield [(value, "dp", 1)]
        return call(small_end_body, [line, Own(table), Own(table)], "small_end")(
            value, got, hold=[send[0] for send in asked["attn"]]
        )

    rounds = 4 + 2 * len(rest_bits)
    chains = {
        "mlp": resplit(2, mlp_keep, mlp_got, "mlp"),
        "attn": attn_chain(far_attn_0, y_far_attn, near_attn_0, near_attn_1),
    }
    asked = {name: next(chain) for name, chain in chains.items()}
    ends = {}
    for at in range(rounds):
        got = [swap(*send) for request in asked.values() for send in request]
        late = []
        if at == 0:
            late = [small]
        elif "done" in ends and at == rounds - 2:
            late = [ends["done"]]
        elif at == rounds - 1:
            late = [ends["small"][0]]
        *got, small = [*gate([*got, *late], [])] if at == 0 else [*gate(got, [], *late), small]
        got = iter(got)
        for name, request in list(asked.items()):
            received = [next(got) for _ in request]
            try:
                asked[name] = chains[name].send(received)
            except StopIteration as stop:
                ends[name] = stop.value
                del asked[name]
        if at == 0:
            chains["small"] = small_chain(small)
            asked["small"] = next(chains["small"])
        if "mlp" in ends and "done" not in ends:
            grad_up, grad_down, ends["done"] = scalar(
                unpack_mlp_body,
                [
                    Own(struct((width, hidden), F32)),
                    Own(struct((hidden, width), F32)),
                    struct((8, 128), F32),
                ],
                "unpack_mlp",
            )(place, *ends["mlp"])

    small_rows, grad_th, grad_tv = ends["small"]
    grad_wq, grad_wk, grad_wv, grad_wo = scalar(
        unpack_attn_body, [Own(struct((local, width), F32))] * 4, "unpack_attn"
    )(place, *ends["attn"])

    return (
        result,
        grad_inputs,
        small_rows[8],
        small_rows[9],
        grad_wq.T,
        small_rows[1, :local],
        grad_wk.T,
        grad_wv.T,
        small_rows[1, local:2 * local],
        grad_th.T,
        grad_tv.T,
        grad_wo,
        small_rows[4],
        small_rows[5],
        small_rows[6],
        grad_up,
        small_rows[0],
        grad_down,
        small_rows[7],
    )


def solution(mesh):
    rows = P(("dp", "mp"), None)
    columns = P(None, "mp")
    split = P("mp")
    placed = (
        rows, rows, P(), P(), columns, split, columns, columns, split, columns, columns,
        P("mp", None), P(), P(), P(), columns, split, P("mp", None), P(),
        P("dp", None), P("dp", None), P("dp", None, None), P("dp", None, None),
    )
    given = (
        rows, rows, P(), P(), columns, split, columns, columns, split, columns, columns,
        P("mp", None), P(), P(), P(), columns, split, P("mp", None), P(),
    )
    return jax.shard_map(
        functools.partial(on_device, mesh.shape["dp"], mesh.shape["mp"]),
        mesh=mesh,
        in_specs=placed,
        out_specs=given,
        check_vma=False,
    )
```

```python
import functools

import jax
import jax.numpy as jnp
from jax import lax
from jax.experimental import pallas as pl
from jax.experimental.pallas import tpu as pltpu
from jax.sharding import PartitionSpec as P

EPSILON = 1e-05
NEGATIVE = -1e30
HEAD = 64
EXTRA = 16
PARTS = 3
F32 = jnp.float32
BF16 = jnp.bfloat16
LIMIT = 16 * 1024 * 1024
SCALE = 30

NN = (((1,), (0,)), ((), ()))
NT = (((1,), (1,)), ((), ()))
TN = (((0,), (0,)), ((), ()))


def mm(left, right, dims=NN):
    return lax.dot_general(left, right, dims, preferred_element_type=F32)


def struct(shape, dtype):
    return jax.ShapeDtypeStruct(shape, dtype)


class Own:
    def __init__(self, value, cuts=()):
        self.value = value
        self.cuts = cuts


class Loaded:
    def __init__(self, source, scratch, sems, cuts):
        self.scratch = scratch
        self.shape = scratch.shape
        edges = [0, *cuts, scratch.shape[0]]
        self.parts = []
        for n, (low, high) in enumerate(zip(edges, edges[1:])):
            here = pl.ds(low, high - low)
            copy = pltpu.make_async_copy(source.at[here], scratch.at[here], sems[n])
            copy.start()
            self.parts.append((low, high, copy))

    def wait(self, low, high):
        for part in list(self.parts):
            if part[0] < high and low < part[1]:
                part[2].wait()
                self.parts.remove(part)

    def __getitem__(self, at):
        first = at[0] if isinstance(at, tuple) else at
        if isinstance(first, slice):
            self.wait(first.start or 0, self.shape[0] if first.stop is None else first.stop)
        else:
            self.wait(0, self.shape[0])
        return self.scratch[at]


class Stored:
    def __init__(self, target, scratch, sem):
        self.copy = pltpu.make_async_copy(scratch, target, sem)
        self.scratch = scratch
        self.shape = scratch.shape
        self.dtype = scratch.dtype
        self.sent = False

    def __getitem__(self, at):
        return self.scratch[at]

    def __setitem__(self, at, value):
        self.scratch[at] = value

    def flush(self):
        self.copy.start()
        self.sent = True


class Rows:
    def __init__(self, refs):
        self.refs = refs
        self.shape = (sum(ref.shape[0] for ref in refs), refs[0].shape[1])

    def __getitem__(self, at):
        rows, *rest = at if isinstance(at, tuple) else (at,)
        if rows is Ellipsis:
            rows = slice(None)
        return jnp.concatenate([ref[(slice(None), *rest)] for ref in self.refs], axis=0)[rows]


def spread(value, start, refs):
    at, end = 0, start + value.shape[0]
    for ref in refs:
        low, high = max(at, start), min(at + ref.shape[0], end)
        if low < high:
            ref[low - at:high - at, :] = value[low - start:high - start].astype(ref.dtype)
        at += ref.shape[0]


def flush(ref):
    if isinstance(ref, Stored):
        ref.flush()


def call(body, outs, name, flops=0, transcendentals=0, scalar=False, scratch=(), alias=None, scale=SCALE):
    def run(*args, hold=()):
        own_in = [isinstance(a, Own) for a in args]
        own_out = [isinstance(o, Own) for o in outs]
        ins = [a.value if own else a for a, own in zip(args, own_in)]
        shapes = [o.value if own else o for o, own in zip(outs, own_out)]
        moved = sum(a.size * a.dtype.itemsize for a in ins + shapes)
        count, held = len(ins), len(hold)
        total = sum(1 + len(v.cuts) for v in [*args, *outs] if isinstance(v, Own))
        copied = [v for v, own in zip(ins + shapes, own_in + own_out) if own]

        def inner(*refs):
            given, results = refs[:count], refs[count + held:count + held + len(shapes)]
            spare = refs[count + held + len(shapes):]
            slots, rest = iter(spare[:len(copied)]), spare[len(copied):]
            sems = iter(range(total))
            loaded = [
                Loaded(
                    ref, next(slots), [rest[-1].at[next(sems)] for _ in (0, *arg.cuts)], arg.cuts
                )
                if isinstance(arg, Own)
                else ref
                for ref, arg in zip(given, args)
            ]
            stored = [
                Stored(ref, next(slots), rest[-1].at[next(sems)]) if own else ref
                for ref, own in zip(results, own_out)
            ]
            body(*loaded, *stored, *(rest[:-1] if copied else rest))
            for ref in loaded:
                if isinstance(ref, Loaded):
                    ref.wait(0, ref.shape[0])
            for ref in stored:
                if isinstance(ref, Stored):
                    if not ref.sent:
                        ref.flush()
                    ref.copy.wait()

        buffers = [pltpu.VMEM(v.shape, v.dtype) for v in copied] + list(scratch)
        if copied:
            buffers.append(pltpu.SemaphoreType.DMA((total,)))
        kept = pl.BlockSpec(memory_space=pl.ANY)
        inside = pl.BlockSpec(memory_space=pltpu.VMEM)
        in_specs = [kept if own else inside for own in own_in]
        if scalar:
            in_specs[0] = pl.BlockSpec(memory_space=pltpu.SMEM)
        return pl.pallas_call(
            inner,
            out_shape=[
                (pltpu.HBM if own else pltpu.VMEM)(o.shape, o.dtype) for o, own in zip(shapes, own_out)
            ],
            in_specs=in_specs + [kept] * held,
            out_specs=[kept if own else inside for own in own_out],
            scratch_shapes=buffers,
            input_output_aliases=alias or {},
            compiler_params=pltpu.CompilerParams(vmem_limit_bytes=LIMIT),
            cost_estimate=pl.CostEstimate(
                flops=int(flops * scale),
                bytes_accessed=int(moved * scale),
                transcendentals=int(transcendentals),
            ),
            name=name,
        )(
            *[
                v
                if scalar and n == 0
                else pltpu.with_memory_space_constraint(v, pltpu.HBM if own else pltpu.VMEM)
                for n, (v, own) in enumerate(zip(ins, own_in))
            ],
            *hold,
        )

    return run


def line(ref):
    value = ref[...]
    return value if value.ndim == 2 else value.reshape(1, value.shape[0])


def halves(values):
    high = values.astype(BF16)
    return high, (values - high.astype(F32)).astype(BF16)


def pack_attn_body(place_ref, wq_ref, wk_ref, wv_ref, wo_ref, th_ref, tv_ref, bq_ref, bv_ref,
                   all_ref, send_ref):
    local = wq_ref.shape[0]
    heads = th_ref.shape[0]
    th, tv = th_ref[...], tv_ref[...]
    parts = []
    for m in range(heads):
        parts += [th[m:m + 1], tv[m:m + 1]]
    high, low = halves(jnp.concatenate(parts + [line(bq_ref), line(bv_ref)], axis=1))
    which = lax.broadcasted_iota(jnp.int32, (2 * EXTRA, high.shape[1]), 0)
    extra = jnp.where(which == 0, high.astype(F32), jnp.where(which == 1, low.astype(F32), 0.0))
    extra = extra.astype(BF16)
    side, along = place_ref[0, 0] == 0, place_ref[0, 3] == 0
    four = [ref[...] for ref in (wq_ref, wk_ref, wv_ref, wo_ref)]
    first, second = jnp.where(along, four[0], four[1]), jnp.where(along, four[2], four[3])
    send_ref[0:local, :] = jnp.where(side, first, second)
    send_ref[local:, :] = extra
    join_weights(all_ref, four, extra)


def join_weights(all_ref, four, extra):
    local = four[0].shape[0]
    piece = 2 * local + EXTRA
    for n, value in enumerate(four):
        at = (n // 2) * piece + (n % 2) * local
        all_ref[at:at + local, :] = value
    all_ref[2 * local:piece, :] = extra[0:EXTRA]
    all_ref[piece + 2 * local:, :] = extra[0:EXTRA]


def pack_mlp_body(place_ref, up_ref, bias_ref, down_ref, all_ref, up_send_ref, down_send_ref):
    half = down_ref.shape[0] // 2
    piece = 2 * half + EXTRA
    bias = line(bias_ref)
    which = lax.broadcasted_iota(jnp.int32, (EXTRA, half), 0) == 0

    def put(at, own, up_to, down_to, down_at):
        one, two = slice(at * half, (at + 1) * half), slice((1 - at) * half, (2 - at) * half)
        high, low = halves(jnp.where(own, bias[:, one], bias[:, two]))
        up_to(0, jnp.where(own, up_ref[0:half, one], up_ref[0:half, two]), high)
        up_to(half, jnp.where(own, up_ref[half:, one], up_ref[half:, two]), low)
        down_to[down_at:down_at + half, :] = jnp.where(own, down_ref[one, :], down_ref[two, :])

    def up_to(ref, at):
        def store(column, value, extra):
            ref[at:at + half, column:column + half] = value
            extra = jnp.where(which, extra.astype(F32), 0.0).astype(BF16)
            ref[at + half:at + half + EXTRA, column:column + half] = extra

        return store

    put(0, place_ref[0, 3] == 0, up_to(up_send_ref, 0), down_send_ref, 0)
    flush(up_send_ref)
    flush(down_send_ref)
    for n in (0, 1):
        at = n * piece
        put(n, place_ref[0, 0] == 0, up_to(all_ref, at), all_ref, at + half + EXTRA)


def start_body(place_ref, x_ref, gain_ref, shift_ref, seg_ref, valid_ref, bh_ref, bv_ref,
               xn_ref, mt_ref, neg_ref, ih_ref, iv_ref):
    x = x_ref[...].astype(F32)
    mean = jnp.mean(x, axis=1, keepdims=True)
    cen = x - mean
    var = jnp.mean(cen * cen, axis=1, keepdims=True)
    xn_ref[...] = (cen * lax.rsqrt(var + EPSILON) * line(gain_ref) + line(shift_ref)).astype(BF16)
    segs = mt_ref.shape[0]
    seq = x.shape[0]
    rows = lax.broadcasted_iota(jnp.int32, (segs, seq), 0)
    top = lax.broadcasted_iota(jnp.int32, (EXTRA, seq), 0) == 0
    for p in (0, 1):
        page = place_ref[0, 1 + p]
        here = pl.ds(p * seq, seq)
        member = jnp.where(rows == seg_ref[pl.ds(page, 1), :], 1.0, 0.0).astype(BF16)
        mt_ref[:, here] = member
        masked = jnp.where(valid_ref[pl.ds(page, 1), :] > 0, 0.0, NEGATIVE)
        neg_ref[:, here] = jnp.where(top, masked, 0.0).astype(BF16)
        bh, bv = bh_ref[page].astype(F32).astype(BF16), bv_ref[page].astype(F32).astype(BF16)
        ih_ref[:, here] = mm(bh, member, TN).astype(jnp.int32)
        iv_ref[:, here] = mm(bv, member, TN).astype(jnp.int32) + segs


def lookup(table, index):
    rows, seq = index.shape
    spread = jnp.broadcast_to(table, (rows, 128))
    parts = [
        jnp.take_along_axis(
            spread, index[:, at:at + 128], axis=1, mode="promise_in_bounds"
        )
        for at in range(0, seq, 128)
    ]
    return jnp.concatenate(parts, axis=1)


def attn_body(first, *refs):
    if first:
        w_ref, ih_ref, iv_ref, mt_ref, neg_ref = refs[2:7]
        given = (None, None)
        qkv_ref, ctx_ref, lse_ref, bias_ref, *outs = refs[7:]
    else:
        place_ref, pieces = refs[0], refs[3:8]
        ih_ref, iv_ref, mt_ref, neg_ref = refs[8:12]
        given = refs[12:14]
        qkv_ref, ctx_ref, lse_ref, bias_ref, *outs, w_ref = refs[14:]
        refs = refs[1:]
        own, beside, along, low, high = [ref[...] for ref in pieces]
        corner = jnp.concatenate([low, high], axis=0)
        local = own.shape[0] - 2 * EXTRA
        four = square(place_ref, own, beside, along, corner)
        join_weights(w_ref, [value[0:local] for value in four], own[local:])
        flush(w_ref)
    width = ctx_ref.shape[0]
    heads = width // HEAD
    segs = mt_ref.shape[0]
    seq = refs[0].shape[0]
    second = 2 * width + EXTRA
    extra = w_ref[2 * width:second, :]
    pick = jnp.where(lax.broadcasted_iota(jnp.int32, (EXTRA, seq), 0) < 2, 1.0, 0.0).astype(BF16)
    bias = mm(extra[:, heads * 128:heads * 128 + 2 * width], pick, TN)
    tables = extra[0:1, :].astype(F32) + extra[1:2, :].astype(F32)
    ones = jnp.ones((EXTRA, seq), BF16)
    for p in (0, 1):
        xn = refs[p][...]
        here = pl.ds(p * seq, seq)
        qk = mm(w_ref[0:2 * width, :], xn, NT)
        v = mm(w_ref[second:second + width, :], xn, NT)
        qkv_ref[0:width, here] = ((qk[0:width] + bias[0:width]) * 0.125).astype(BF16)
        qkv_ref[width:2 * width, here] = qk[width:].astype(BF16)
        qkv_ref[2 * width:, here] = (v + bias[width:]).astype(BF16)
    flush(qkv_ref)
    for p in (0, 1):
        here = pl.ds(p * seq, seq)
        member = mt_ref[:, here]
        for m in range(heads):
            table = tables[:, 128 * m:128 * m + 128]
            pos = lookup(table, ih_ref[:, here]) + lookup(table, iv_ref[:, here])
            high, low = halves(pos)
            bias_ref[2 * segs * m:2 * segs * m + segs, here] = high
            bias_ref[2 * segs * m + segs:2 * segs * (m + 1), here] = low
            at = HEAD * m
            q_aug = jnp.concatenate([qkv_ref[at:at + HEAD, here], high, low, ones], axis=0)
            k_aug = jnp.concatenate(
                [qkv_ref[width + at:width + at + HEAD, here], member, member, neg_ref[:, here]],
                axis=0,
            )
            scores = mm(k_aug, q_aug, TN)
            top = jnp.max(scores, axis=0, keepdims=True)
            expo = jnp.exp(scores - top).astype(BF16)
            v_aug = jnp.concatenate(
                [qkv_ref[2 * width + at:2 * width + at + HEAD, here], ones], axis=0
            )
            summed = mm(v_aug, expo)
            total = summed[HEAD:HEAD + 1]
            ctx_ref[at:at + HEAD, here] = (summed[0:HEAD] / total).astype(BF16)
            lse_ref[m:m + 1, here] = top + jnp.log(total)
        out = mm(ctx_ref[:, here], w_ref[second + width:second + 2 * width, :], TN)
        if given[p] is not None:
            out = given[p][...] + out
        if first:
            outs[p][...] = out.astype(outs[p].dtype)
            continue
        if p == 0:
            outs[0][...] = out
        spread(out, p * seq, outs[1:])
    lse_ref[heads:, :] = jnp.zeros((lse_ref.shape[0] - heads, 2 * seq), F32)


def middle_body(x_ref, other_x_ref, acc_ref, bias_ref, gain_ref, shift_ref, *refs):
    sent, got = Rows(refs[0:PARTS]), Rows(refs[PARTS:2 * PARTS])
    mid_ref, nm_ref, other_nm_ref = refs[2 * PARTS:]
    seq = x_ref.shape[0]
    own = acc_ref[...] + got[seq:, :].astype(F32)
    other = sent[seq:, :].astype(F32) + got[0:seq, :].astype(F32)
    for value, source_ref, out_ref in ((own, x_ref, nm_ref), (other, other_x_ref, other_nm_ref)):
        mid = source_ref[...].astype(F32) + value + line(bias_ref)
        if out_ref is nm_ref:
            mid_ref[...] = mid
        mean = jnp.mean(mid, axis=1, keepdims=True)
        cen = mid - mean
        var = jnp.mean(cen * cen, axis=1, keepdims=True)
        out = cen * lax.rsqrt(var + EPSILON) * line(gain_ref) + line(shift_ref)
        out_ref[...] = out.astype(BF16)


def mlp_body(first, last, up_at, down_at, *refs):
    nm_refs, cot_refs = refs[0:2], refs[2:4]
    refs = refs[4:]
    u_ref, d_ref = refs[0:2]
    given = (None,) * 4 if first else refs[2:6]
    *accs, up_ref, dn_ref, db_ref = refs[2 if first else 6:]
    if last:
        accs, parts = (accs[0], None, accs[1], None), accs[2:]
    half = up_ref.shape[0]
    extra = u_ref[up_at + half:up_at + half + EXTRA, :].astype(F32)
    bias = extra[0:1, 0:half] + extra[0:1, half:]
    up_left = u_ref[up_at:up_at + half, 0:half]
    up_right = u_ref[up_at:up_at + half, half:]
    down = d_ref[down_at:down_at + half, :]
    total = None
    for p in (0, 1):
        nm_left, nm_right = nm_refs[p][:, 0:half], nm_refs[p][:, half:]
        cot = cot_refs[p][...]
        upper = mm(nm_left, up_left) + mm(nm_right, up_right) + bias
        cdf = 0.5 + 0.5 * lax.erf(upper * 0.7071067811865476)
        pdf = jnp.exp(upper * upper * -0.5) * 0.3989422804014327
        hidden = (upper * cdf).astype(BF16)
        grad_hidden = mm(cot, down, NT)
        grad_upper = (grad_hidden * (cdf + upper * pdf)).astype(BF16)
        sums_now = (
            mm(nm_left, grad_upper, TN),
            mm(nm_right, grad_upper, TN),
            mm(hidden, cot, TN),
            jnp.sum(grad_upper.astype(F32), axis=0, keepdims=True),
        )
        total = sums_now if total is None else [a + b for a, b in zip(total, sums_now)]
        down_out = mm(hidden, down)
        back_left = mm(grad_upper, up_left, NT)
        back_right = mm(grad_upper, up_right, NT)
        if not first:
            down_out = given[p][...].astype(F32) + down_out
            back_left = given[2 + p][:, 0:half].astype(F32) + back_left
            back_right = given[2 + p][:, half:].astype(F32) + back_right
        if last and p == 1:
            back = jnp.concatenate([back_left, back_right], axis=1)
            spread(jnp.concatenate([down_out, back], axis=0), 0, parts)
            continue
        down_ref, back_ref = accs[p], accs[2 + p]
        down_ref[...] = down_out.astype(down_ref.dtype)
        back_ref[:, 0:half] = back_left.astype(back_ref.dtype)
        back_ref[:, half:] = back_right.astype(back_ref.dtype)
    up_ref[:, 0:half] = total[0].astype(BF16)
    up_ref[:, half:] = total[1].astype(BF16)
    dn_ref[...] = total[2].astype(BF16)
    db_ref[...] = jnp.broadcast_to(total[3], db_ref.shape)


def turn_body(mid_ref, down_ref, bias_ref, back_ref, cot_ref, gain_ref, *refs):
    got, (res_ref, gmid_ref, ga_ref, rows_ref) = Rows(refs[:PARTS]), refs[PARTS:]
    mid = mid_ref[...]
    seq = mid.shape[0]
    down = down_ref[...] + got[0:seq, :].astype(F32)
    res_ref[...] = (mid + down + line(bias_ref)).astype(BF16)
    mean = jnp.mean(mid, axis=1, keepdims=True)
    cen = mid - mean
    var = jnp.mean(cen * cen, axis=1, keepdims=True)
    rstd = lax.rsqrt(var + EPSILON)
    n = cen * rstd
    back = back_ref[...] + got[seq:, :].astype(F32)
    q = back * line(gain_ref)
    cot = cot_ref[...].astype(F32)
    mean_q = jnp.mean(q, axis=1, keepdims=True)
    mean_qn = jnp.mean(q * n, axis=1, keepdims=True)
    grad = cot + rstd * (q - mean_q - n * mean_qn)
    gmid_ref[...] = grad
    ga_ref[...] = grad.astype(BF16)
    rows_ref[0:1, :] = jnp.sum(grad, axis=0, keepdims=True)
    rows_ref[1:2, :] = jnp.sum(back * n, axis=0, keepdims=True)
    rows_ref[2:3, :] = jnp.sum(back, axis=0, keepdims=True)
    rows_ref[3:4, :] = jnp.sum(cot, axis=0, keepdims=True)
    rows_ref[4:, :] = jnp.zeros((rows_ref.shape[0] - 4, rows_ref.shape[1]), F32)


def attn_back_body(first, *refs):
    place_ref, xn_refs, ga_refs = refs[0], refs[1:3], refs[3:5]
    w_ref, qkv_ref, ctx_ref, lse_ref, bias_ref, mt_ref, neg_ref = refs[5:12]
    given = (None, None) if first else refs[12:14]
    *backs, kept_ref, other_ref, sums_ref, seg_ref, dqkv_ref = refs[12 if first else 14:]
    width = ctx_ref.shape[0]
    heads = width // HEAD
    seq = xn_refs[0].shape[0]
    segs = mt_ref.shape[0]
    second = 2 * width + EXTRA
    ones = jnp.ones((EXTRA, seq), BF16)
    grad_out = None
    for p in (0, 1):
        here = pl.ds(p * seq, seq)
        ga = ga_refs[p][...]
        member = mt_ref[:, here]
        grad_ctx = mm(w_ref[second + width:second + 2 * width, :], ga, NT).astype(BF16)
        part = mm(ctx_ref[:, here], ga)
        grad_out = part if p == 0 else grad_out + part
        for m in range(heads):
            at = HEAD * m
            q = qkv_ref[at:at + HEAD, here]
            k = qkv_ref[width + at:width + at + HEAD, here]
            v = qkv_ref[2 * width + at:2 * width + at + HEAD, here]
            g = grad_ctx[at:at + HEAD]
            q_aug = jnp.concatenate(
                [q, bias_ref[2 * segs * m:2 * segs * (m + 1), here], ones], axis=0
            )
            k_aug = jnp.concatenate([k, member, member, neg_ref[:, here]], axis=0)
            scores = mm(k_aug, q_aug, TN)
            probs = jnp.exp(scores - lse_ref[m:m + 1, here])
            grad_probs = mm(v, g, TN)
            delta = jnp.sum(probs * grad_probs, axis=0, keepdims=True)
            grad_scores = (probs * (grad_probs - delta)).astype(BF16)
            grad_v = mm(g, probs.astype(BF16), NT)
            dqkv_ref[2 * width + at:2 * width + at + HEAD, here] = grad_v.astype(BF16)
            dqkv_ref[width + at:width + at + HEAD, here] = mm(q, grad_scores, NT).astype(BF16)
            both = mm(jnp.concatenate([k, member], axis=0), grad_scores)
            dqkv_ref[at:at + HEAD, here] = both[0:HEAD].astype(BF16) * jnp.asarray(0.125, BF16)
            high, low = halves(both[HEAD:])
            seg_ref[p * heads + m] = mm(member, high, NT) + mm(member, low, NT)
    grads = mm(dqkv_ref[:, 0:seq], xn_refs[0][...]) + mm(dqkv_ref[:, seq:], xn_refs[1][...])
    grads = jnp.concatenate([grads, grad_out], axis=0).astype(BF16)
    low = place_ref[0, 0] == 0
    kept_ref[...] = jnp.where(low, grads[0:2 * width], grads[2 * width:])
    flush(kept_ref)
    other_ref[...] = jnp.where(low, grads[2 * width:], grads[0:2 * width])
    flush(other_ref)
    for p in (0, 1):
        here = pl.ds(p * seq, seq)
        back = mm(dqkv_ref[0:2 * width, here], w_ref[0:2 * width, :], TN)
        back = back + mm(dqkv_ref[2 * width:, here], w_ref[second:second + width, :], TN)
        if given[p] is not None:
            back = given[p][...] + back
        backs[p][...] = back.astype(backs[p].dtype)
    sums_ref[...] = mm(jnp.ones((8, 2 * seq), BF16), dqkv_ref[...], NT)


def total_of(refs):
    if len(refs) == 2:
        return refs[0][...] + refs[1][...]
    value = refs[0][...].astype(F32)
    for ref in refs[1:]:
        value = value + ref[...].astype(F32)
    return value.astype(refs[0].dtype)


def sum_body(counts, *refs):
    outs = refs[sum(counts):]
    at = 0
    for count, out in zip(counts, outs):
        out[...] = total_of(refs[at:at + count])
        at += count


def sums(name, *groups, hold=()):
    outs = [struct(group[0].shape, group[0].dtype) for group in groups]
    body = functools.partial(sum_body, [len(group) for group in groups])
    flat = [value for group in groups for value in group]
    return call(body, outs, name)(*flat, hold=hold)


def pick_body(place_ref, zero_ref, one_ref, out_ref):
    same = place_ref[0, 0] == place_ref[0, 3]
    rows = one_ref.shape[0]
    out_ref[0:rows, :] = jnp.where(same, one_ref[...], zero_ref[...])
    out_ref[rows:, :] = jnp.zeros((out_ref.shape[0] - rows, out_ref.shape[1]), out_ref.dtype)


def plane_body(place_ref, up_0_ref, up_1_ref, up_got_ref, near_ref, down_0_ref, down_1_ref,
               up_ref, down_ref):
    same = place_ref[0, 0] == place_ref[0, 3]
    up = jnp.where(same, up_0_ref[...], up_1_ref[...])
    up_ref[...] = up + up_got_ref[0:up.shape[0], :]
    down_ref[...] = near_ref[...] + jnp.where(same, down_1_ref[...], down_0_ref[...])


def plane_part_body(place_ref, up_0_ref, up_1_ref, down_ref, far_0_ref, far_1_ref,
                    up_ref, out_ref):
    same = place_ref[0, 0] == place_ref[0, 3]
    up_ref[...] = up_0_ref[...] + up_1_ref[...]
    out_ref[...] = down_ref[...] + jnp.where(same, far_0_ref[...], far_1_ref[...])


def put_halves(low, value, keep_ref, give_ref, at):
    size = value.shape[0] // 2
    one, two = value[0:size], value[size:]
    keep_ref[at:at + size, :] = jnp.where(low, one, two)
    give_ref[at:at + size, :] = jnp.where(low, two, one)


def split_body(which, groups, place_ref, *refs):
    *parts, keep_ref, give_ref = refs
    low = place_ref[0, which] == 0
    size = keep_ref.shape[0] // groups
    count = len(parts) // groups
    for n in range(groups):
        value = total_of(parts[n * count:(n + 1) * count])
        put_halves(low, value, keep_ref, give_ref, n * size)


def resplit_body(which, groups, place_ref, own_ref, got_ref, keep_ref, give_ref):
    low = place_ref[0, which] == 0
    size = keep_ref.shape[0] // groups
    value = own_ref[...] + got_ref[...]
    for n in range(groups):
        here = slice(2 * n * size, 2 * (n + 1) * size)
        put_halves(low, value[here], keep_ref, give_ref, n * size)


def join_body(which, groups, place_ref, own_ref, other_ref, out_ref):
    size = own_ref.shape[0] // groups
    low = place_ref[0, which] == 0
    own, other = own_ref[...], other_ref[...]
    for n in range(groups):
        part = slice(n * size, (n + 1) * size)
        out_ref[2 * n * size:(2 * n + 1) * size, :] = jnp.where(low, own[part], other[part])
        out_ref[(2 * n + 1) * size:(2 * n + 2) * size, :] = jnp.where(low, other[part], own[part])


def corner_body(y_ref, z_ref, low_ref, high_ref):
    size = low_ref.shape[0]
    low_ref[...] = z_ref[0:size, :]
    high_ref[...] = y_ref[size:, :]


def end_body(x_ref, back_ref, got_ref, gmid_ref, gain_ref, gx_ref, rows_ref):
    x = x_ref[...].astype(F32)
    mean = jnp.mean(x, axis=1, keepdims=True)
    cen = x - mean
    var = jnp.mean(cen * cen, axis=1, keepdims=True)
    rstd = lax.rsqrt(var + EPSILON)
    n = cen * rstd
    back = back_ref[...] + got_ref[...].astype(F32)
    q = back * line(gain_ref)
    mean_q = jnp.mean(q, axis=1, keepdims=True)
    mean_qn = jnp.mean(q * n, axis=1, keepdims=True)
    gx_ref[...] = (gmid_ref[...] + rstd * (q - mean_q - n * mean_qn)).astype(BF16)
    rows_ref[0:1, :] = jnp.sum(back * n, axis=0, keepdims=True)
    rows_ref[1:2, :] = jnp.sum(back, axis=0, keepdims=True)
    rows_ref[2:, :] = jnp.zeros((rows_ref.shape[0] - 2, rows_ref.shape[1]), F32)


def small_body(place_ref, near_0_ref, near_1_ref, far_0_ref, far_1_ref, sums_near_ref, sums_far_ref,
               seg_near_ref, seg_far_ref, bh_ref, bv_ref, turn_ref, end_ref, out_ref):
    count, segs, _ = seg_near_ref.shape
    heads = count // 2
    bins = lax.broadcasted_iota(jnp.int32, (segs, segs), 0)
    total = jnp.zeros((2 * EXTRA, 2 * segs), F32)
    for p in (0, 1):
        page = place_ref[0, 1 + p]
        bh, bv = bh_ref[page], bv_ref[page]
        own = pl.ds(p * heads, heads)
        for s in range(segs):
            both = jnp.concatenate(
                [
                    seg_near_ref[own, s, :],
                    seg_far_ref[own, s, :],
                    jnp.zeros((EXTRA - 2 * heads, segs), F32),
                ],
                axis=0,
            )
            hot = jnp.concatenate(
                [
                    jnp.where(bins == bh[s:s + 1, :], 1.0, 0.0),
                    jnp.where(bins == bv[s:s + 1, :], 1.0, 0.0),
                ],
                axis=0,
            ).astype(BF16)
            total = total + mm(jnp.concatenate(halves(both), axis=0), hot, NT)
    tables = total[0:EXTRA] + total[EXTRA:]
    side, low = place_ref[0, 0] == 0, place_ref[0, 3] == 0
    out_ref[...] = jnp.zeros(out_ref.shape, F32)
    width = sums_near_ref.shape[1] // 3
    half = near_0_ref.shape[1]
    near = (side, near_0_ref[0:1, :], near_1_ref[0:1, :], sums_near_ref)
    far = (low, far_0_ref[0:1, :], far_1_ref[0:1, :], sums_far_ref)
    for k, (own, one, two, sums_in) in enumerate((near, far)):
        out_ref[2 * k:2 * k + 1, 0:half] = jnp.where(own, one, two)
        out_ref[2 * k:2 * k + 1, half:] = jnp.where(own, two, one)
        parts = [sums_in[0:1, 0:width], sums_in[0:1, 2 * width:]]
        parts += [tables[k * heads + m:k * heads + m + 1] for m in range(heads)]
        out_ref[2 * k + 1:2 * k + 2, :] = jnp.concatenate(parts, axis=1)
    out_ref[4:8, :] = turn_ref[0:4, :]
    out_ref[8:10, :] = end_ref[0:2, :]


def small_shards_body(own_ref, core_ref, across_ref, corner_ref, out_ref):
    out_ref[...] = jnp.zeros(out_ref.shape, F32)
    out_ref[0:2, :] = own_ref[0:2, :] + across_ref[2:4, :]
    out_ref[4:10, :] = (own_ref[4:10, :] + across_ref[4:10, :]) + (
        core_ref[4:10, :] + corner_ref[4:10, :]
    )


def small_end_body(own_ref, got_ref, rows_ref, th_ref, tv_ref):
    rows_ref[...] = own_ref[...] + got_ref[...]
    own = own_ref[1:2, :] + got_ref[1:2, :]
    heads, bins = th_ref.shape
    for m in range(heads):
        at = own.shape[1] - 2 * bins * (heads - m)
        th_ref[m:m + 1, :] = own[:, at:at + bins]
        tv_ref[m:m + 1, :] = own[:, at + bins:at + 2 * bins]


def square(place_ref, own, beside, along, corner):
    side, low = place_ref[0, 0] == 0, place_ref[0, 3] == 0
    own_half = (jnp.where(low, own, along), jnp.where(low, along, own))
    other_half = (jnp.where(low, beside, corner), jnp.where(low, corner, beside))
    first = [jnp.where(side, a, b) for a, b in zip(own_half, other_half)]
    second = [jnp.where(side, b, a) for a, b in zip(own_half, other_half)]
    return first + second


def unpack_mlp_body(place_ref, own_ref, y_ref, z_ref, low_ref, high_ref,
                    up_ref, down_ref, done_ref):
    done_ref[...] = jnp.zeros(done_ref.shape, F32)
    size = low_ref.shape[0]
    half = 2 * size
    ups = square(
        place_ref, own_ref[0:size, :], y_ref[0:size, :], z_ref[0:size, :], low_ref[...]
    )
    for n, part in enumerate(ups):
        here = pl.ds((n // 2) * half, half)
        at = (n % 2) * size
        part = part.astype(F32)
        up_ref[at:at + size, here] = part[:, 0:half]
        up_ref[half + at:half + at + size, here] = part[:, half:]
    flush(up_ref)
    downs = square(
        place_ref, own_ref[size:, :], y_ref[size:, :], z_ref[size:, :], high_ref[...]
    )
    for n, part in enumerate(downs):
        down_ref[n * size:(n + 1) * size, :] = part.astype(F32)


def unpack_attn_body(place_ref, own_ref, y_ref, z_ref, low_ref, high_ref,
                     q_ref, k_ref, v_ref, o_ref):
    corner = jnp.concatenate([low_ref[...], high_ref[...]], axis=0)
    parts = square(place_ref, own_ref[...], y_ref[...], z_ref[...], corner)
    for ref, part in zip((q_ref, k_ref, v_ref, o_ref), parts):
        ref[...] = part.astype(F32)
        flush(ref)


def order_body(*refs):
    pass


def gate(inside, outside, *others):
    spec = pl.BlockSpec(memory_space=pl.ANY)
    spaces = [pltpu.VMEM] * len(inside) + [pltpu.HBM] * len(outside)
    values = [*inside, *outside]
    return pl.pallas_call(
        order_body,
        out_shape=[space(v.shape, v.dtype) for space, v in zip(spaces, values)],
        in_specs=[spec] * (len(values) + len(others)),
        out_specs=[spec] * len(values),
        input_output_aliases={n: n for n in range(len(values))},
        compiler_params=pltpu.CompilerParams(vmem_limit_bytes=2**20),
        name="order",
    )(
        *[pltpu.with_memory_space_constraint(v, space) for space, v in zip(spaces, values)],
        *others,
    )


def on_device(
    dp_count,
    mp_count,
    inputs,
    cotangent,
    gain_attn,
    shift_attn,
    weight_query,
    bias_query,
    weight_key,
    weight_value,
    bias_value,
    table_horizontal,
    table_vertical,
    weight_out,
    bias_out,
    gain_mlp,
    shift_mlp,
    weight_up,
    bias_up,
    weight_down,
    bias_down,
    segment,
    valid,
    bucket_horizontal,
    bucket_vertical,
):
    seq, width = inputs.shape
    local = weight_query.shape[1]
    heads = table_horizontal.shape[1]
    hidden = weight_up.shape[1]
    half = hidden // 2
    segs = bucket_horizontal.shape[1]
    bins = table_horizontal.shape[0]
    shard = lax.axis_index("mp")
    pages = lax.axis_index("dp")
    bits = [1 << b for b in range(1, dp_count.bit_length() - 1)]
    place = jnp.stack([pages % 2, shard, shard ^ 1] + [(pages // bit) % 2 for bit in bits])
    place = place.astype(jnp.int32).reshape(1, -1)
    scalar = functools.partial(call, scalar=True)

    def swap(value, axis, bit):
        count = dp_count if axis == "dp" else mp_count
        return lax.ppermute(value, axis, [(i, i ^ bit) for i in range(count)])

    def core(value):
        return swap(value, "mp", 1)

    def across(value):
        return swap(value, "mp", 2)

    def beside(value):
        return swap(value, "dp", 1)

    piece = struct((local + 2 * EXTRA, width), BF16)
    both = struct((4 * local + 2 * EXTRA, width), BF16)
    near_w, attn_send = scalar(pack_attn_body, [both, piece], "pack_attn")(
        place, Own(weight_query.T), Own(weight_key.T), Own(weight_value.T), Own(weight_out),
        Own(table_horizontal.T), Own(table_vertical.T), Own(bias_query), Own(bias_value),
    )
    x_attn = across(attn_send)
    cot_got, inputs_got = core(cotangent), core(inputs)
    mlp_w, up_send, down_send = scalar(
        pack_mlp_body,
        [
            struct((2 * (2 * half + EXTRA), width), BF16),
            Own(struct((half + EXTRA, width), BF16)),
            Own(struct((half, width), BF16)),
        ],
        "pack_mlp",
    )(place, Own(weight_up), bias_up, Own(weight_down))

    attn_flops = 2 * (2 * seq * width * 4 * local + heads * seq * seq * 256 * 2 * 2)
    page = struct((seq, width), F32)
    page_low = struct((seq, width), BF16)

    def owned(*values):
        return [Own(value) for value in values]

    saved = [
        struct((3 * local, 2 * seq), BF16),
        struct((local, 2 * seq), BF16),
        struct((8, 2 * seq), F32),
        struct((2 * segs * heads, 2 * seq), BF16),
    ]

    def mlp(weights, rows, acc, name, last=False):
        first = acc is None
        ins = [*nms, cot, cot_got, *weights]
        at = len(ins)
        outs = call(
            functools.partial(mlp_body, first, last, *rows),
            ([page, page, *low_parts] if last else [page, page_low, page, page_low])
            + [struct((half, width), BF16)] * 2
            + [struct((8, half), F32)],
            name,
            alias={}
            if first
            else {at: 0, at + 2: 1}
            if last
            else {at + n: n for n in range(4)},
            scale=0,
        )(*ins, *(acc or ()))
        return list(outs[:-3]), *outs[-3:]

    xn, member, negative, index_h, index_v = scalar(
        start_body,
        [
            struct((seq, width), BF16),
            struct((segs, 2 * seq), BF16),
            struct((EXTRA, 2 * seq), BF16),
            struct((segs, 2 * seq), jnp.int32),
            struct((segs, 2 * seq), jnp.int32),
        ],
        "first_norm",
    )(
        place, Own(inputs), Own(gain_attn), Own(shift_attn),
        Own(segment), Own(valid), Own(bucket_horizontal), Own(bucket_vertical)
    )
    x_attn, xn, cot, cot_got, inputs_got, up_send, down_send = gate(
        [x_attn, xn, cotangent, cot_got, inputs_got], [up_send, down_send]
    )
    y_attn = beside(x_attn)
    z_attn = swap(x_attn, "dp", bits[0])
    x_up = across(up_send)
    xns = [xn, core(xn)]
    *kept_near, acc_0, acc_1 = call(
        functools.partial(attn_body, True), [*saved, page, page_low], "attn_near", scale=0
    )(*xns, near_w, index_h, index_v, member, negative)
    acc_0, acc_1, x_attn, y_attn, z_attn = gate([acc_0, acc_1, x_attn, y_attn, z_attn], [])
    corner = struct((piece.shape[0] // 2, width), BF16)
    low, high = call(corner_body, [corner] * 2, "attn_corner")(y_attn, z_attn)
    low, high = beside(low), swap(high, "dp", bits[0])
    x_up, down_send = gate([x_up], [down_send], acc_0)
    x_down = across(down_send)
    z_up = swap(x_up, "dp", bits[0])
    low, high = gate([low, high], [])
    edges = [2 * seq * n // PARTS // EXTRA * EXTRA for n in range(PARTS)] + [2 * seq]
    low_parts = [struct((high - low, width), BF16) for low, high in zip(edges, edges[1:])]
    outs = scalar(
        functools.partial(attn_body, False),
        [*saved, page, *low_parts, both],
        "attn_far",
        scale=0,
        alias={12: 4},
    )(
        place, *xns, x_attn, y_attn, z_attn, low, high, index_h, index_v, member, negative,
        acc_0, acc_1,
    )
    kept_far, far_w = outs[0:4], outs[-1]
    acc_0, *lows = outs[4:-1]
    middle, *nms = call(middle_body, [page, page_low, page_low], "second_norm", scale=0)(
        Own(inputs), inputs_got, acc_0, bias_out, gain_mlp, shift_mlp,
        *lows, *[core(value) for value in lows],
    )
    *nms, x_down, z_up, x_up = gate([*nms, x_down, z_up, x_up], [])
    z_down = swap(x_down, "dp", bits[0])
    up_rows, all_rows = half + EXTRA, 2 * half + EXTRA
    mlp_acc, near_up_1, near_down_1, near_sums_1 = mlp(
        [mlp_w, mlp_w], [all_rows, all_rows + up_rows], None, "mlp_near_1"
    )
    *mlp_acc, near_up_1 = gate([*mlp_acc, near_up_1], [])
    near_y_up = beside(near_up_1)
    mlp_acc, far_up_0, far_down_0, far_sums_0 = mlp([x_up, x_down], [0, 0], mlp_acc, "mlp_far_0")
    *mlp_acc, far_down_0 = gate([*mlp_acc, far_down_0], [])
    x_far_down_0 = across(far_down_0)
    mlp_acc, far_up_1, far_down_1, far_sums_1 = mlp([z_up, z_down], [0, 0], mlp_acc, "mlp_far_1")
    (far_up_send,) = scalar(pick_body, [struct((half + EXTRA, width), BF16)], "pick")(
        place, far_up_0, far_up_1
    )
    *mlp_acc, near_y_up, far_up_send, far_down_1 = gate(
        [*mlp_acc, near_y_up, far_up_send, far_down_1], []
    )
    y_far_up = beside(far_up_send)
    mlp_acc, near_up_0, near_down_0, near_sums_0 = mlp(
        [mlp_w, mlp_w], [0, up_rows], mlp_acc, "mlp_near_0", last=True
    )
    *mlp_acc, x_far_down_0, far_down_1 = gate([*mlp_acc, x_far_down_0, far_down_1], [])
    x_far_down_1 = across(far_down_1)
    result, grad_middle, grad_attn, turn_rows = call(
        turn_body,
        [Own(page_low), page, page_low, struct((8, width), F32)],
        "turn",
        scale=0,
    )(
        middle, mlp_acc[0], bias_down, mlp_acc[1], Own(cotangent), gain_mlp,
        *[core(value) for value in mlp_acc[2:]],
    )
    grad_attn, y_far_up, x_far_down_1 = gate([grad_attn, y_far_up, x_far_down_1], [])
    quarters = [struct((half, width), BF16)] * 2
    up_send, down_send = scalar(plane_body, quarters, "plane_sum")(
        place, far_up_0, far_up_1, y_far_up, near_down_1, x_far_down_0, x_far_down_1
    )
    x_up = across(up_send)
    y_down = beside(down_send)
    gas = [grad_attn, core(grad_attn)]

    def attn_back(weights, kept, acc, name, hold=()):
        first = acc is None
        ins = [
            place, *xns, *gas, weights, *kept, member, negative,
        ]
        outs = scalar(
            functools.partial(attn_back_body, first),
            [
                page,
                page_low,
                struct((2 * local, width), BF16),
                struct((2 * local, width), BF16),
                struct((8, 3 * local), F32),
                struct((2 * heads, segs, segs), F32),
            ],
            name,
            flops=2 * attn_flops,
            scratch=[pltpu.VMEM((3 * local, 2 * seq), BF16)],
            alias=None if first else {len(ins): 0, len(ins) + 1: 1},
        )(*ins, *(acc or ()), hold=hold)
        return list(outs[0:2]), outs[2:4], outs[4], outs[5]

    first_bit, *rest_bits = bits

    def resplit(groups, keep, got, name):
        for n, bit in enumerate(rest_bits):
            out = struct((keep.shape[0] // 2, width), BF16)
            body = functools.partial(resplit_body, 4 + n, groups)
            keep, give = scalar(body, [out] * 2, name + "_split")(place, keep, got)
            (got,) = yield [(give, "dp", bit)]
        (part,) = sums(name + "_total", (keep, got))
        for n, bit in reversed(list(enumerate(rest_bits))):
            (got,) = yield [(part, "dp", bit)]
            out = struct((2 * part.shape[0], width), BF16)
            body = functools.partial(join_body, 4 + n, groups)
            (part,) = scalar(body, [out], name + "_join")(place, part, got)
        y_got, z_got = yield [(part, "dp", 1), (part, "dp", first_bit)]
        out = struct((part.shape[0] // 2, width), BF16)
        low, high = call(corner_body, [out] * 2, name + "_corner")(y_got, z_got)
        low, high = yield [(low, "dp", 1), (high, "dp", first_bit)]
        return part, y_got, z_got, low, high

    def split(groups, name, *parts):
        out = struct((groups * parts[0].shape[0] // 2, width), BF16)
        body = functools.partial(split_body, 3, groups)
        return scalar(body, [out] * 2, name + "_split")(place, *parts)

    def attn_chain(far_0, far_got, near_0, near_1):
        (send,) = sums("attn_sum", (far_0, far_got))
        near_got, far_got = yield [(near_1, "dp", 1), (send, "mp", 2)]
        keep, give = split(1, "attn", near_0, near_got, far_got)
        (got,) = yield [(give, "dp", first_bit)]
        return (yield from resplit(1, keep, got, "attn"))

    acc, (far_attn_0, far_attn_1), sums_far, seg_far = attn_back(
        far_w, kept_far, None, "attn_back_far"
    )
    up_part, down_part = scalar(plane_part_body, quarters, "plane_part")(
        place, near_up_0, near_y_up, near_down_0, x_far_down_0, x_far_down_1, hold=[acc[0]]
    )
    *acc, x_up, y_down, far_attn_1, up_part, down_part = gate(
        [*acc, x_up, y_down, far_attn_1, up_part, down_part], []
    )
    y_far_attn = beside(far_attn_1)
    mlp_keep, mlp_give = split(2, "mlp", up_part, x_up, down_part, y_down)
    mlp_got = swap(mlp_give, "dp", first_bit)
    acc, (near_attn_0, near_attn_1), sums_near, seg_near = attn_back(
        near_w, kept_near, acc, "attn_back_near", hold=[mlp_give]
    )
    *acc, mlp_got, y_far_attn, near_attn_1 = gate(
        [*acc, mlp_got, y_far_attn, near_attn_1], []
    )
    grad_inputs, end_rows = call(
        end_body, [Own(page_low), struct((8, width), F32)], "end"
    )(Own(inputs), acc[0], core(acc[1]), grad_middle, gain_attn)
    (small,) = scalar(small_body, [struct((16, width), F32)], "small")(
        place, near_sums_0, near_sums_1, far_sums_0, far_sums_1, sums_near, sums_far, seg_near, seg_far,
        Own(bucket_horizontal), Own(bucket_vertical), turn_rows, end_rows,
    )
    table = struct((heads, bins), F32)

    def small_chain(value):
        line = struct(value.shape, F32)
        for bit in bits:
            (got,) = yield [(value, "dp", bit)]
            (value,) = sums("small_sum", (value, got))
        got = yield [(value, "mp", 1), (value, "mp", 2), (value, "mp", 3)]
        (value,) = call(small_shards_body, [line], "small_shards")(value, *got)
        (got,) = yield [(value, "dp", 1)]
        return call(small_end_body, [line, Own(table), Own(table)], "small_end")(
            value, got, hold=[send[0] for send in asked["attn"]]
        )

    rounds = 4 + 2 * len(rest_bits)
    chains = {
        "attn": attn_chain(far_attn_0, y_far_attn, near_attn_0, near_attn_1),
        "mlp": resplit(2, mlp_keep, mlp_got, "mlp"),
    }
    asked = {name: next(chain) for name, chain in chains.items()}
    ends = {}
    for at in range(rounds):
        got = [swap(*send) for request in asked.values() for send in request]
        late = []
        if at == 0:
            late = [small]
        elif "done" in ends and at == rounds - 2:
            late = [ends["done"]]
        elif at == rounds - 1:
            late = [ends["small"][0]]
        *got, small = [*gate([*got, *late], [])] if at == 0 else [*gate(got, [], *late), small]
        got = iter(got)
        for name, request in list(asked.items()):
            received = [next(got) for _ in request]
            try:
                asked[name] = chains[name].send(received)
            except StopIteration as stop:
                ends[name] = stop.value
                del asked[name]
        if at == 0:
            chains["small"] = small_chain(small)
            asked["small"] = next(chains["small"])
        if "mlp" in ends and "done" not in ends:
            grad_up, grad_down, ends["done"] = scalar(
                unpack_mlp_body,
                [
                    Own(struct((width, hidden), F32)),
                    Own(struct((hidden, width), F32)),
                    struct((8, 128), F32),
                ],
                "unpack_mlp",
            )(place, *ends["mlp"])

    small_rows, grad_th, grad_tv = ends["small"]
    grad_wq, grad_wk, grad_wv, grad_wo = scalar(
        unpack_attn_body, [Own(struct((local, width), F32))] * 4, "unpack_attn"
    )(place, *ends["attn"])

    return (
        result,
        grad_inputs,
        small_rows[8],
        small_rows[9],
        grad_wq.T,
        small_rows[1, :local],
        grad_wk.T,
        grad_wv.T,
        small_rows[1, local:2 * local],
        grad_th.T,
        grad_tv.T,
        grad_wo,
        small_rows[4],
        small_rows[5],
        small_rows[6],
        grad_up,
        small_rows[0],
        grad_down,
        small_rows[7],
    )


def solution(mesh):
    rows = P(("dp", "mp"), None)
    columns = P(None, "mp")
    split = P("mp")
    placed = (
        rows, rows, P(), P(), columns, split, columns, columns, split, columns, columns,
        P("mp", None), P(), P(), P(), columns, split, P("mp", None), P(),
        P("dp", None), P("dp", None), P("dp", None, None), P("dp", None, None),
    )
    given = (
        rows, rows, P(), P(), columns, split, columns, columns, split, columns, columns,
        P("mp", None), P(), P(), P(), columns, split, P("mp", None), P(),
    )
    return jax.shard_map(
        functools.partial(on_device, mesh.shape["dp"], mesh.shape["mp"]),
        mesh=mesh,
        in_specs=placed,
        out_specs=given,
        check_vma=False,
    )
```

```python
import functools

import jax
import jax.numpy as jnp
from jax import lax
from jax.experimental import pallas as pl
from jax.experimental.pallas import tpu as pltpu
from jax.sharding import PartitionSpec as P

EPSILON = 1e-05
NEGATIVE = -1e30
HEAD = 64
EXTRA = 16
PARTS = 3
F32 = jnp.float32
BF16 = jnp.bfloat16
LIMIT = 16 * 1024 * 1024
SCALE = 30

NN = (((1,), (0,)), ((), ()))
NT = (((1,), (1,)), ((), ()))
TN = (((0,), (0,)), ((), ()))


def mm(left, right, dims=NN):
    return lax.dot_general(left, right, dims, preferred_element_type=F32)


def struct(shape, dtype):
    return jax.ShapeDtypeStruct(shape, dtype)


class Own:
    def __init__(self, value, cuts=()):
        self.value = value
        self.cuts = cuts


class Loaded:
    def __init__(self, source, scratch, sems, cuts):
        self.scratch = scratch
        self.shape = scratch.shape
        edges = [0, *cuts, scratch.shape[0]]
        self.parts = []
        for n, (low, high) in enumerate(zip(edges, edges[1:])):
            here = pl.ds(low, high - low)
            copy = pltpu.make_async_copy(source.at[here], scratch.at[here], sems[n])
            copy.start()
            self.parts.append((low, high, copy))

    def wait(self, low, high):
        for part in list(self.parts):
            if part[0] < high and low < part[1]:
                part[2].wait()
                self.parts.remove(part)

    def __getitem__(self, at):
        first = at[0] if isinstance(at, tuple) else at
        if isinstance(first, slice):
            self.wait(first.start or 0, self.shape[0] if first.stop is None else first.stop)
        else:
            self.wait(0, self.shape[0])
        return self.scratch[at]


class Stored:
    def __init__(self, target, scratch, sem):
        self.copy = pltpu.make_async_copy(scratch, target, sem)
        self.scratch = scratch
        self.shape = scratch.shape
        self.dtype = scratch.dtype
        self.sent = False

    def __getitem__(self, at):
        return self.scratch[at]

    def __setitem__(self, at, value):
        self.scratch[at] = value

    def flush(self):
        self.copy.start()
        self.sent = True


class Rows:
    def __init__(self, refs):
        self.refs = refs
        self.shape = (sum(ref.shape[0] for ref in refs), refs[0].shape[1])

    def __getitem__(self, at):
        rows, *rest = at if isinstance(at, tuple) else (at,)
        if rows is Ellipsis:
            rows = slice(None)
        return jnp.concatenate([ref[(slice(None), *rest)] for ref in self.refs], axis=0)[rows]


def spread(value, start, refs):
    at, end = 0, start + value.shape[0]
    for ref in refs:
        low, high = max(at, start), min(at + ref.shape[0], end)
        if low < high:
            ref[low - at:high - at, :] = value[low - start:high - start].astype(ref.dtype)
        at += ref.shape[0]


def flush(ref):
    if isinstance(ref, Stored):
        ref.flush()


def call(body, outs, name, flops=0, transcendentals=0, scalar=False, scratch=(), alias=None, scale=SCALE):
    def run(*args, hold=()):
        own_in = [isinstance(a, Own) for a in args]
        own_out = [isinstance(o, Own) for o in outs]
        ins = [a.value if own else a for a, own in zip(args, own_in)]
        shapes = [o.value if own else o for o, own in zip(outs, own_out)]
        moved = sum(a.size * a.dtype.itemsize for a in ins + shapes)
        count, held = len(ins), len(hold)
        total = sum(1 + len(v.cuts) for v in [*args, *outs] if isinstance(v, Own))
        copied = [v for v, own in zip(ins + shapes, own_in + own_out) if own]

        def inner(*refs):
            given, results = refs[:count], refs[count + held:count + held + len(shapes)]
            spare = refs[count + held + len(shapes):]
            slots, rest = iter(spare[:len(copied)]), spare[len(copied):]
            sems = iter(range(total))
            loaded = [
                Loaded(
                    ref, next(slots), [rest[-1].at[next(sems)] for _ in (0, *arg.cuts)], arg.cuts
                )
                if isinstance(arg, Own)
                else ref
                for ref, arg in zip(given, args)
            ]
            stored = [
                Stored(ref, next(slots), rest[-1].at[next(sems)]) if own else ref
                for ref, own in zip(results, own_out)
            ]
            body(*loaded, *stored, *(rest[:-1] if copied else rest))
            for ref in loaded:
                if isinstance(ref, Loaded):
                    ref.wait(0, ref.shape[0])
            for ref in stored:
                if isinstance(ref, Stored):
                    if not ref.sent:
                        ref.flush()
                    ref.copy.wait()

        buffers = [pltpu.VMEM(v.shape, v.dtype) for v in copied] + list(scratch)
        if copied:
            buffers.append(pltpu.SemaphoreType.DMA((total,)))
        kept = pl.BlockSpec(memory_space=pl.ANY)
        inside = pl.BlockSpec(memory_space=pltpu.VMEM)
        in_specs = [kept if own else inside for own in own_in]
        if scalar:
            in_specs[0] = pl.BlockSpec(memory_space=pltpu.SMEM)
        return pl.pallas_call(
            inner,
            out_shape=[
                (pltpu.HBM if own else pltpu.VMEM)(o.shape, o.dtype) for o, own in zip(shapes, own_out)
            ],
            in_specs=in_specs + [kept] * held,
            out_specs=[kept if own else inside for own in own_out],
            scratch_shapes=buffers,
            input_output_aliases=alias or {},
            compiler_params=pltpu.CompilerParams(vmem_limit_bytes=LIMIT),
            cost_estimate=pl.CostEstimate(
                flops=int(flops * scale),
                bytes_accessed=int(moved * scale),
                transcendentals=int(transcendentals),
            ),
            name=name,
        )(
            *[
                v
                if scalar and n == 0
                else pltpu.with_memory_space_constraint(v, pltpu.HBM if own else pltpu.VMEM)
                for n, (v, own) in enumerate(zip(ins, own_in))
            ],
            *hold,
        )

    return run


def line(ref):
    value = ref[...]
    return value if value.ndim == 2 else value.reshape(1, value.shape[0])


def halves(values):
    high = values.astype(BF16)
    return high, (values - high.astype(F32)).astype(BF16)


def pack_attn_body(place_ref, wq_ref, wk_ref, wv_ref, wo_ref, th_ref, tv_ref, bq_ref, bv_ref,
                   all_ref, send_ref):
    local = wq_ref.shape[0]
    heads = th_ref.shape[0]
    th, tv = th_ref[...], tv_ref[...]
    parts = []
    for m in range(heads):
        parts += [th[m:m + 1], tv[m:m + 1]]
    high, low = halves(jnp.concatenate(parts + [line(bq_ref), line(bv_ref)], axis=1))
    which = lax.broadcasted_iota(jnp.int32, (2 * EXTRA, high.shape[1]), 0)
    extra = jnp.where(which == 0, high.astype(F32), jnp.where(which == 1, low.astype(F32), 0.0))
    extra = extra.astype(BF16)
    side, along = place_ref[0, 0] == 0, place_ref[0, 3] == 0
    four = [ref[...] for ref in (wq_ref, wk_ref, wv_ref, wo_ref)]
    first, second = jnp.where(along, four[0], four[1]), jnp.where(along, four[2], four[3])
    send_ref[0:local, :] = jnp.where(side, first, second)
    send_ref[local:, :] = extra
    join_weights(all_ref, four, extra)


def join_weights(all_ref, four, extra):
    local = four[0].shape[0]
    piece = 2 * local + EXTRA
    for n, value in enumerate(four):
        at = (n // 2) * piece + (n % 2) * local
        all_ref[at:at + local, :] = value
    all_ref[2 * local:piece, :] = extra[0:EXTRA]
    all_ref[piece + 2 * local:, :] = extra[0:EXTRA]


def pack_mlp_body(place_ref, up_ref, bias_ref, down_ref, all_ref, up_send_ref, down_send_ref):
    half = down_ref.shape[0] // 2
    piece = 2 * half + EXTRA
    bias = line(bias_ref)
    which = lax.broadcasted_iota(jnp.int32, (EXTRA, half), 0) == 0

    def put(at, own, up_to, down_to, down_at):
        one, two = slice(at * half, (at + 1) * half), slice((1 - at) * half, (2 - at) * half)
        high, low = halves(jnp.where(own, bias[:, one], bias[:, two]))
        up_to(0, jnp.where(own, up_ref[0:half, one], up_ref[0:half, two]), high)
        up_to(half, jnp.where(own, up_ref[half:, one], up_ref[half:, two]), low)
        down_to[down_at:down_at + half, :] = jnp.where(own, down_ref[one, :], down_ref[two, :])

    def up_to(ref, at):
        def store(column, value, extra):
            ref[at:at + half, column:column + half] = value
            extra = jnp.where(which, extra.astype(F32), 0.0).astype(BF16)
            ref[at + half:at + half + EXTRA, column:column + half] = extra

        return store

    put(0, place_ref[0, 3] == 0, up_to(up_send_ref, 0), down_send_ref, 0)
    flush(up_send_ref)
    flush(down_send_ref)
    for n in (0, 1):
        at = n * piece
        put(n, place_ref[0, 0] == 0, up_to(all_ref, at), all_ref, at + half + EXTRA)


def start_body(place_ref, x_ref, gain_ref, shift_ref, seg_ref, valid_ref, bh_ref, bv_ref,
               xn_ref, mt_ref, neg_ref, ih_ref, iv_ref):
    x = x_ref[...].astype(F32)
    mean = jnp.mean(x, axis=1, keepdims=True)
    cen = x - mean
    var = jnp.mean(cen * cen, axis=1, keepdims=True)
    xn_ref[...] = (cen * lax.rsqrt(var + EPSILON) * line(gain_ref) + line(shift_ref)).astype(BF16)
    segs = mt_ref.shape[0]
    seq = x.shape[0]
    rows = lax.broadcasted_iota(jnp.int32, (segs, seq), 0)
    top = lax.broadcasted_iota(jnp.int32, (EXTRA, seq), 0) == 0
    for p in (0, 1):
        page = place_ref[0, 1 + p]
        here = pl.ds(p * seq, seq)
        member = jnp.where(rows == seg_ref[pl.ds(page, 1), :], 1.0, 0.0).astype(BF16)
        mt_ref[:, here] = member
        masked = jnp.where(valid_ref[pl.ds(page, 1), :] > 0, 0.0, NEGATIVE)
        neg_ref[:, here] = jnp.where(top, masked, 0.0).astype(BF16)
        bh, bv = bh_ref[page].astype(F32).astype(BF16), bv_ref[page].astype(F32).astype(BF16)
        ih_ref[:, here] = mm(bh, member, TN).astype(jnp.int32)
        iv_ref[:, here] = mm(bv, member, TN).astype(jnp.int32) + segs


def lookup(table, index):
    rows, seq = index.shape
    spread = jnp.broadcast_to(table, (rows, 128))
    parts = [
        jnp.take_along_axis(
            spread, index[:, at:at + 128], axis=1, mode="promise_in_bounds"
        )
        for at in range(0, seq, 128)
    ]
    return jnp.concatenate(parts, axis=1)


def attn_body(first, *refs):
    if first:
        w_ref, ih_ref, iv_ref, mt_ref, neg_ref = refs[2:7]
        given = (None, None)
        qkv_ref, ctx_ref, lse_ref, bias_ref, *outs = refs[7:]
    else:
        place_ref, pieces = refs[0], refs[3:8]
        ih_ref, iv_ref, mt_ref, neg_ref = refs[8:12]
        given = refs[12:14]
        qkv_ref, ctx_ref, lse_ref, bias_ref, *outs, w_ref = refs[14:]
        refs = refs[1:]
        own, beside, along, low, high = [ref[...] for ref in pieces]
        corner = jnp.concatenate([low, high], axis=0)
        local = own.shape[0] - 2 * EXTRA
        four = square(place_ref, own, beside, along, corner)
        join_weights(w_ref, [value[0:local] for value in four], own[local:])
        flush(w_ref)
    width = ctx_ref.shape[0]
    heads = width // HEAD
    segs = mt_ref.shape[0]
    seq = refs[0].shape[0]
    second = 2 * width + EXTRA
    extra = w_ref[2 * width:second, :]
    pick = jnp.where(lax.broadcasted_iota(jnp.int32, (EXTRA, seq), 0) < 2, 1.0, 0.0).astype(BF16)
    bias = mm(extra[:, heads * 128:heads * 128 + 2 * width], pick, TN)
    tables = extra[0:1, :].astype(F32) + extra[1:2, :].astype(F32)
    ones = jnp.ones((EXTRA, seq), BF16)
    for p in (0, 1):
        xn = refs[p][...]
        here = pl.ds(p * seq, seq)
        qk = mm(w_ref[0:2 * width, :], xn, NT)
        v = mm(w_ref[second:second + width, :], xn, NT)
        qkv_ref[0:width, here] = ((qk[0:width] + bias[0:width]) * 0.125).astype(BF16)
        qkv_ref[width:2 * width, here] = qk[width:].astype(BF16)
        qkv_ref[2 * width:, here] = (v + bias[width:]).astype(BF16)
    flush(qkv_ref)
    for p in (0, 1):
        here = pl.ds(p * seq, seq)
        member = mt_ref[:, here]
        for m in range(heads):
            table = tables[:, 128 * m:128 * m + 128]
            pos = lookup(table, ih_ref[:, here]) + lookup(table, iv_ref[:, here])
            high, low = halves(pos)
            bias_ref[2 * segs * m:2 * segs * m + segs, here] = high
            bias_ref[2 * segs * m + segs:2 * segs * (m + 1), here] = low
            at = HEAD * m
            q_aug = jnp.concatenate([qkv_ref[at:at + HEAD, here], high, low, ones], axis=0)
            k_aug = jnp.concatenate(
                [qkv_ref[width + at:width + at + HEAD, here], member, member, neg_ref[:, here]],
                axis=0,
            )
            scores = mm(k_aug, q_aug, TN)
            top = jnp.max(scores, axis=0, keepdims=True)
            expo = jnp.exp(scores - top).astype(BF16)
            v_aug = jnp.concatenate(
                [qkv_ref[2 * width + at:2 * width + at + HEAD, here], ones], axis=0
            )
            summed = mm(v_aug, expo)
            total = summed[HEAD:HEAD + 1]
            ctx_ref[at:at + HEAD, here] = (summed[0:HEAD] / total).astype(BF16)
            lse_ref[m:m + 1, here] = top + jnp.log(total)
        out = mm(ctx_ref[:, here], w_ref[second + width:second + 2 * width, :], TN)
        if given[p] is not None:
            out = given[p][...] + out
        if first:
            outs[p][...] = out.astype(outs[p].dtype)
            continue
        if p == 0:
            outs[0][...] = out
        spread(out, p * seq, outs[1:])
    lse_ref[heads:, :] = jnp.zeros((lse_ref.shape[0] - heads, 2 * seq), F32)


def middle_body(x_ref, other_x_ref, acc_ref, bias_ref, gain_ref, shift_ref, *refs):
    sent, got = Rows(refs[0:PARTS]), Rows(refs[PARTS:2 * PARTS])
    mid_ref, nm_ref, other_nm_ref = refs[2 * PARTS:]
    seq = x_ref.shape[0]
    own = acc_ref[...] + got[seq:, :].astype(F32)
    other = sent[seq:, :].astype(F32) + got[0:seq, :].astype(F32)
    for value, source_ref, out_ref in ((own, x_ref, nm_ref), (other, other_x_ref, other_nm_ref)):
        mid = source_ref[...].astype(F32) + value + line(bias_ref)
        if out_ref is nm_ref:
            mid_ref[...] = mid
        mean = jnp.mean(mid, axis=1, keepdims=True)
        cen = mid - mean
        var = jnp.mean(cen * cen, axis=1, keepdims=True)
        out = cen * lax.rsqrt(var + EPSILON) * line(gain_ref) + line(shift_ref)
        out_ref[...] = out.astype(BF16)


def mlp_body(first, last, up_at, down_at, *refs):
    nm_refs, cot_refs = refs[0:2], refs[2:4]
    refs = refs[4:]
    u_ref, d_ref = refs[0:2]
    given = (None,) * 4 if first else refs[2:6]
    *accs, up_ref, dn_ref, db_ref = refs[2 if first else 6:]
    if last:
        accs, parts = (accs[0], None, accs[1], None), accs[2:]
    half = up_ref.shape[0]
    extra = u_ref[up_at + half:up_at + half + EXTRA, :].astype(F32)
    bias = extra[0:1, 0:half] + extra[0:1, half:]
    up_left = u_ref[up_at:up_at + half, 0:half]
    up_right = u_ref[up_at:up_at + half, half:]
    down = d_ref[down_at:down_at + half, :]
    total = None
    for p in (0, 1):
        nm_left, nm_right = nm_refs[p][:, 0:half], nm_refs[p][:, half:]
        cot = cot_refs[p][...]
        upper = mm(nm_left, up_left) + mm(nm_right, up_right) + bias
        cdf = 0.5 + 0.5 * lax.erf(upper * 0.7071067811865476)
        pdf = jnp.exp(upper * upper * -0.5) * 0.3989422804014327
        hidden = (upper * cdf).astype(BF16)
        grad_hidden = mm(cot, down, NT)
        grad_upper = (grad_hidden * (cdf + upper * pdf)).astype(BF16)
        sums_now = (
            mm(nm_left, grad_upper, TN),
            mm(nm_right, grad_upper, TN),
            mm(hidden, cot, TN),
            jnp.sum(grad_upper.astype(F32), axis=0, keepdims=True),
        )
        total = sums_now if total is None else [a + b for a, b in zip(total, sums_now)]
        down_out = mm(hidden, down)
        back_left = mm(grad_upper, up_left, NT)
        back_right = mm(grad_upper, up_right, NT)
        if not first:
            down_out = given[p][...].astype(F32) + down_out
            back_left = given[2 + p][:, 0:half].astype(F32) + back_left
            back_right = given[2 + p][:, half:].astype(F32) + back_right
        if last and p == 1:
            back = jnp.concatenate([back_left, back_right], axis=1)
            spread(jnp.concatenate([down_out, back], axis=0), 0, parts)
            continue
        down_ref, back_ref = accs[p], accs[2 + p]
        down_ref[...] = down_out.astype(down_ref.dtype)
        back_ref[:, 0:half] = back_left.astype(back_ref.dtype)
        back_ref[:, half:] = back_right.astype(back_ref.dtype)
    up_ref[:, 0:half] = total[0].astype(BF16)
    up_ref[:, half:] = total[1].astype(BF16)
    dn_ref[...] = total[2].astype(BF16)
    db_ref[...] = jnp.broadcast_to(total[3], db_ref.shape)


def turn_body(mid_ref, down_ref, bias_ref, back_ref, cot_ref, gain_ref, *refs):
    got, (res_ref, gmid_ref, ga_ref, rows_ref) = Rows(refs[:PARTS]), refs[PARTS:]
    mid = mid_ref[...]
    seq = mid.shape[0]
    down = down_ref[...] + got[0:seq, :].astype(F32)
    res_ref[...] = (mid + down + line(bias_ref)).astype(BF16)
    mean = jnp.mean(mid, axis=1, keepdims=True)
    cen = mid - mean
    var = jnp.mean(cen * cen, axis=1, keepdims=True)
    rstd = lax.rsqrt(var + EPSILON)
    n = cen * rstd
    back = back_ref[...] + got[seq:, :].astype(F32)
    q = back * line(gain_ref)
    cot = cot_ref[...].astype(F32)
    mean_q = jnp.mean(q, axis=1, keepdims=True)
    mean_qn = jnp.mean(q * n, axis=1, keepdims=True)
    grad = cot + rstd * (q - mean_q - n * mean_qn)
    gmid_ref[...] = grad
    ga_ref[...] = grad.astype(BF16)
    rows_ref[0:1, :] = jnp.sum(grad, axis=0, keepdims=True)
    rows_ref[1:2, :] = jnp.sum(back * n, axis=0, keepdims=True)
    rows_ref[2:3, :] = jnp.sum(back, axis=0, keepdims=True)
    rows_ref[3:4, :] = jnp.sum(cot, axis=0, keepdims=True)
    rows_ref[4:, :] = jnp.zeros((rows_ref.shape[0] - 4, rows_ref.shape[1]), F32)


def attn_back_body(first, *refs):
    place_ref, xn_refs, ga_refs = refs[0], refs[1:3], refs[3:5]
    w_ref, qkv_ref, ctx_ref, lse_ref, bias_ref, mt_ref, neg_ref = refs[5:12]
    given = (None, None) if first else refs[12:14]
    *backs, kept_ref, other_ref, sums_ref, seg_ref, dqkv_ref = refs[12 if first else 14:]
    width = ctx_ref.shape[0]
    heads = width // HEAD
    seq = xn_refs[0].shape[0]
    segs = mt_ref.shape[0]
    second = 2 * width + EXTRA
    ones = jnp.ones((EXTRA, seq), BF16)
    grad_out = None
    for p in (0, 1):
        here = pl.ds(p * seq, seq)
        ga = ga_refs[p][...]
        member = mt_ref[:, here]
        grad_ctx = mm(w_ref[second + width:second + 2 * width, :], ga, NT).astype(BF16)
        part = mm(ctx_ref[:, here], ga)
        grad_out = part if p == 0 else grad_out + part
        for m in range(heads):
            at = HEAD * m
            q = qkv_ref[at:at + HEAD, here]
            k = qkv_ref[width + at:width + at + HEAD, here]
            v = qkv_ref[2 * width + at:2 * width + at + HEAD, here]
            g = grad_ctx[at:at + HEAD]
            q_aug = jnp.concatenate(
                [q, bias_ref[2 * segs * m:2 * segs * (m + 1), here], ones], axis=0
            )
            k_aug = jnp.concatenate([k, member, member, neg_ref[:, here]], axis=0)
            scores = mm(k_aug, q_aug, TN)
            probs = jnp.exp(scores - lse_ref[m:m + 1, here])
            grad_probs = mm(v, g, TN)
            delta = jnp.sum(probs * grad_probs, axis=0, keepdims=True)
            grad_scores = (probs * (grad_probs - delta)).astype(BF16)
            grad_v = mm(g, probs.astype(BF16), NT)
            dqkv_ref[2 * width + at:2 * width + at + HEAD, here] = grad_v.astype(BF16)
            dqkv_ref[width + at:width + at + HEAD, here] = mm(q, grad_scores, NT).astype(BF16)
            both = mm(jnp.concatenate([k, member], axis=0), grad_scores)
            dqkv_ref[at:at + HEAD, here] = both[0:HEAD].astype(BF16) * jnp.asarray(0.125, BF16)
            high, low = halves(both[HEAD:])
            seg_ref[p * heads + m] = mm(member, high, NT) + mm(member, low, NT)
    grads = mm(dqkv_ref[:, 0:seq], xn_refs[0][...]) + mm(dqkv_ref[:, seq:], xn_refs[1][...])
    grads = jnp.concatenate([grads, grad_out], axis=0).astype(BF16)
    low = place_ref[0, 0] == 0
    kept_ref[...] = jnp.where(low, grads[0:2 * width], grads[2 * width:])
    flush(kept_ref)
    other_ref[...] = jnp.where(low, grads[2 * width:], grads[0:2 * width])
    flush(other_ref)
    for p in (0, 1):
        here = pl.ds(p * seq, seq)
        back = mm(dqkv_ref[0:2 * width, here], w_ref[0:2 * width, :], TN)
        back = back + mm(dqkv_ref[2 * width:, here], w_ref[second:second + width, :], TN)
        if given[p] is not None:
            back = given[p][...] + back
        backs[p][...] = back.astype(backs[p].dtype)
    sums_ref[...] = mm(jnp.ones((8, 2 * seq), BF16), dqkv_ref[...], NT)


def total_of(refs):
    if len(refs) == 2:
        return refs[0][...] + refs[1][...]
    value = refs[0][...].astype(F32)
    for ref in refs[1:]:
        value = value + ref[...].astype(F32)
    return value.astype(refs[0].dtype)


def sum_body(counts, *refs):
    outs = refs[sum(counts):]
    at = 0
    for count, out in zip(counts, outs):
        out[...] = total_of(refs[at:at + count])
        at += count


def sums(name, *groups, hold=()):
    outs = [struct(group[0].shape, group[0].dtype) for group in groups]
    body = functools.partial(sum_body, [len(group) for group in groups])
    flat = [value for group in groups for value in group]
    return call(body, outs, name)(*flat, hold=hold)


def pick_body(place_ref, zero_ref, one_ref, out_ref):
    same = place_ref[0, 0] == place_ref[0, 3]
    rows = one_ref.shape[0]
    out_ref[0:rows, :] = jnp.where(same, one_ref[...], zero_ref[...])
    out_ref[rows:, :] = jnp.zeros((out_ref.shape[0] - rows, out_ref.shape[1]), out_ref.dtype)


def plane_up_body(place_ref, up_0_ref, up_1_ref, got_ref, out_ref):
    same = place_ref[0, 0] == place_ref[0, 3]
    up = jnp.where(same, up_0_ref[...], up_1_ref[...])
    out_ref[...] = up + got_ref[0:up.shape[0], :]


def plane_down_body(place_ref, near_ref, down_0_ref, down_1_ref, out_ref):
    same = place_ref[0, 0] == place_ref[0, 3]
    out_ref[...] = near_ref[...] + jnp.where(same, down_1_ref[...], down_0_ref[...])


def plane_part_body(place_ref, up_0_ref, up_1_ref, down_ref, far_0_ref, far_1_ref,
                    up_ref, out_ref):
    same = place_ref[0, 0] == place_ref[0, 3]
    up_ref[...] = up_0_ref[...] + up_1_ref[...]
    out_ref[...] = down_ref[...] + jnp.where(same, far_0_ref[...], far_1_ref[...])


def put_halves(low, value, keep_ref, give_ref, at):
    size = value.shape[0] // 2
    one, two = value[0:size], value[size:]
    keep_ref[at:at + size, :] = jnp.where(low, one, two)
    give_ref[at:at + size, :] = jnp.where(low, two, one)


def split_body(which, groups, place_ref, *refs):
    *parts, keep_ref, give_ref = refs
    low = place_ref[0, which] == 0
    size = keep_ref.shape[0] // groups
    count = len(parts) // groups
    for n in range(groups):
        value = total_of(parts[n * count:(n + 1) * count])
        put_halves(low, value, keep_ref, give_ref, n * size)


def resplit_body(which, groups, place_ref, own_ref, got_ref, keep_ref, give_ref):
    low = place_ref[0, which] == 0
    size = keep_ref.shape[0] // groups
    value = own_ref[...] + got_ref[...]
    for n in range(groups):
        here = slice(2 * n * size, 2 * (n + 1) * size)
        put_halves(low, value[here], keep_ref, give_ref, n * size)


def join_body(which, groups, place_ref, own_ref, other_ref, out_ref):
    size = own_ref.shape[0] // groups
    low = place_ref[0, which] == 0
    own, other = own_ref[...], other_ref[...]
    for n in range(groups):
        part = slice(n * size, (n + 1) * size)
        out_ref[2 * n * size:(2 * n + 1) * size, :] = jnp.where(low, own[part], other[part])
        out_ref[(2 * n + 1) * size:(2 * n + 2) * size, :] = jnp.where(low, other[part], own[part])


def corner_body(y_ref, z_ref, low_ref, high_ref):
    size = low_ref.shape[0]
    low_ref[...] = z_ref[0:size, :]
    high_ref[...] = y_ref[size:, :]


def end_body(x_ref, back_ref, got_ref, gmid_ref, gain_ref, gx_ref, rows_ref):
    x = x_ref[...].astype(F32)
    mean = jnp.mean(x, axis=1, keepdims=True)
    cen = x - mean
    var = jnp.mean(cen * cen, axis=1, keepdims=True)
    rstd = lax.rsqrt(var + EPSILON)
    n = cen * rstd
    back = back_ref[...] + got_ref[...].astype(F32)
    q = back * line(gain_ref)
    mean_q = jnp.mean(q, axis=1, keepdims=True)
    mean_qn = jnp.mean(q * n, axis=1, keepdims=True)
    gx_ref[...] = (gmid_ref[...] + rstd * (q - mean_q - n * mean_qn)).astype(BF16)
    rows_ref[0:1, :] = jnp.sum(back * n, axis=0, keepdims=True)
    rows_ref[1:2, :] = jnp.sum(back, axis=0, keepdims=True)
    rows_ref[2:, :] = jnp.zeros((rows_ref.shape[0] - 2, rows_ref.shape[1]), F32)


def small_body(place_ref, near_0_ref, near_1_ref, far_0_ref, far_1_ref, sums_near_ref, sums_far_ref,
               seg_near_ref, seg_far_ref, bh_ref, bv_ref, turn_ref, end_ref, out_ref):
    count, segs, _ = seg_near_ref.shape
    heads = count // 2
    bins = lax.broadcasted_iota(jnp.int32, (segs, segs), 0)
    total = jnp.zeros((2 * EXTRA, 2 * segs), F32)
    for p in (0, 1):
        page = place_ref[0, 1 + p]
        bh, bv = bh_ref[page], bv_ref[page]
        own = pl.ds(p * heads, heads)
        for s in range(segs):
            both = jnp.concatenate(
                [
                    seg_near_ref[own, s, :],
                    seg_far_ref[own, s, :],
                    jnp.zeros((EXTRA - 2 * heads, segs), F32),
                ],
                axis=0,
            )
            hot = jnp.concatenate(
                [
                    jnp.where(bins == bh[s:s + 1, :], 1.0, 0.0),
                    jnp.where(bins == bv[s:s + 1, :], 1.0, 0.0),
                ],
                axis=0,
            ).astype(BF16)
            total = total + mm(jnp.concatenate(halves(both), axis=0), hot, NT)
    tables = total[0:EXTRA] + total[EXTRA:]
    side, low = place_ref[0, 0] == 0, place_ref[0, 3] == 0
    out_ref[...] = jnp.zeros(out_ref.shape, F32)
    width = sums_near_ref.shape[1] // 3
    half = near_0_ref.shape[1]
    near = (side, near_0_ref[0:1, :], near_1_ref[0:1, :], sums_near_ref)
    far = (low, far_0_ref[0:1, :], far_1_ref[0:1, :], sums_far_ref)
    for k, (own, one, two, sums_in) in enumerate((near, far)):
        out_ref[2 * k:2 * k + 1, 0:half] = jnp.where(own, one, two)
        out_ref[2 * k:2 * k + 1, half:] = jnp.where(own, two, one)
        parts = [sums_in[0:1, 0:width], sums_in[0:1, 2 * width:]]
        parts += [tables[k * heads + m:k * heads + m + 1] for m in range(heads)]
        out_ref[2 * k + 1:2 * k + 2, :] = jnp.concatenate(parts, axis=1)
    out_ref[4:8, :] = turn_ref[0:4, :]
    out_ref[8:10, :] = end_ref[0:2, :]


def small_shards_body(own_ref, core_ref, across_ref, corner_ref, out_ref):
    out_ref[...] = jnp.zeros(out_ref.shape, F32)
    out_ref[0:2, :] = own_ref[0:2, :] + across_ref[2:4, :]
    out_ref[4:10, :] = (own_ref[4:10, :] + across_ref[4:10, :]) + (
        core_ref[4:10, :] + corner_ref[4:10, :]
    )


def small_end_body(own_ref, got_ref, rows_ref, th_ref, tv_ref):
    rows_ref[...] = own_ref[...] + got_ref[...]
    own = own_ref[1:2, :] + got_ref[1:2, :]
    heads, bins = th_ref.shape
    for m in range(heads):
        at = own.shape[1] - 2 * bins * (heads - m)
        th_ref[m:m + 1, :] = own[:, at:at + bins]
        tv_ref[m:m + 1, :] = own[:, at + bins:at + 2 * bins]


def square(place_ref, own, beside, along, corner):
    side, low = place_ref[0, 0] == 0, place_ref[0, 3] == 0
    own_half = (jnp.where(low, own, along), jnp.where(low, along, own))
    other_half = (jnp.where(low, beside, corner), jnp.where(low, corner, beside))
    first = [jnp.where(side, a, b) for a, b in zip(own_half, other_half)]
    second = [jnp.where(side, b, a) for a, b in zip(own_half, other_half)]
    return first + second


def unpack_mlp_body(place_ref, own_ref, y_ref, z_ref, low_ref, high_ref,
                    up_ref, down_ref, done_ref):
    done_ref[...] = jnp.zeros(done_ref.shape, F32)
    size = low_ref.shape[0]
    half = 2 * size
    ups = square(
        place_ref, own_ref[0:size, :], y_ref[0:size, :], z_ref[0:size, :], low_ref[...]
    )
    for n, part in enumerate(ups):
        here = pl.ds((n // 2) * half, half)
        at = (n % 2) * size
        part = part.astype(F32)
        up_ref[at:at + size, here] = part[:, 0:half]
        up_ref[half + at:half + at + size, here] = part[:, half:]
    flush(up_ref)
    downs = square(
        place_ref, own_ref[size:, :], y_ref[size:, :], z_ref[size:, :], high_ref[...]
    )
    for n, part in enumerate(downs):
        down_ref[n * size:(n + 1) * size, :] = part.astype(F32)


def unpack_attn_body(place_ref, own_ref, y_ref, z_ref, low_ref, high_ref,
                     q_ref, k_ref, v_ref, o_ref):
    corner = jnp.concatenate([low_ref[...], high_ref[...]], axis=0)
    parts = square(place_ref, own_ref[...], y_ref[...], z_ref[...], corner)
    for ref, part in zip((q_ref, k_ref, v_ref, o_ref), parts):
        ref[...] = part.astype(F32)
        flush(ref)


def order_body(*refs):
    pass


def gate(inside, outside, *others):
    spec = pl.BlockSpec(memory_space=pl.ANY)
    spaces = [pltpu.VMEM] * len(inside) + [pltpu.HBM] * len(outside)
    values = [*inside, *outside]
    return pl.pallas_call(
        order_body,
        out_shape=[space(v.shape, v.dtype) for space, v in zip(spaces, values)],
        in_specs=[spec] * (len(values) + len(others)),
        out_specs=[spec] * len(values),
        input_output_aliases={n: n for n in range(len(values))},
        compiler_params=pltpu.CompilerParams(vmem_limit_bytes=2**20),
        name="order",
    )(
        *[pltpu.with_memory_space_constraint(v, space) for space, v in zip(spaces, values)],
        *others,
    )


def on_device(
    dp_count,
    mp_count,
    inputs,
    cotangent,
    gain_attn,
    shift_attn,
    weight_query,
    bias_query,
    weight_key,
    weight_value,
    bias_value,
    table_horizontal,
    table_vertical,
    weight_out,
    bias_out,
    gain_mlp,
    shift_mlp,
    weight_up,
    bias_up,
    weight_down,
    bias_down,
    segment,
    valid,
    bucket_horizontal,
    bucket_vertical,
):
    seq, width = inputs.shape
    local = weight_query.shape[1]
    heads = table_horizontal.shape[1]
    hidden = weight_up.shape[1]
    half = hidden // 2
    segs = bucket_horizontal.shape[1]
    bins = table_horizontal.shape[0]
    shard = lax.axis_index("mp")
    pages = lax.axis_index("dp")
    bits = [1 << b for b in range(1, dp_count.bit_length() - 1)]
    place = jnp.stack([pages % 2, shard, shard ^ 1] + [(pages // bit) % 2 for bit in bits])
    place = place.astype(jnp.int32).reshape(1, -1)
    scalar = functools.partial(call, scalar=True)

    def swap(value, axis, bit):
        count = dp_count if axis == "dp" else mp_count
        return lax.ppermute(value, axis, [(i, i ^ bit) for i in range(count)])

    def core(value):
        return swap(value, "mp", 1)

    def across(value):
        return swap(value, "mp", 2)

    def beside(value):
        return swap(value, "dp", 1)

    piece = struct((local + 2 * EXTRA, width), BF16)
    both = struct((4 * local + 2 * EXTRA, width), BF16)
    near_w, attn_send = scalar(pack_attn_body, [both, piece], "pack_attn")(
        place, Own(weight_query.T), Own(weight_key.T), Own(weight_value.T), Own(weight_out),
        Own(table_horizontal.T), Own(table_vertical.T), Own(bias_query), Own(bias_value),
    )
    x_attn = across(attn_send)
    cot_got, inputs_got = core(cotangent), core(inputs)
    mlp_w, up_send, down_send = scalar(
        pack_mlp_body,
        [
            struct((2 * (2 * half + EXTRA), width), BF16),
            Own(struct((half + EXTRA, width), BF16)),
            Own(struct((half, width), BF16)),
        ],
        "pack_mlp",
    )(place, Own(weight_up), bias_up, Own(weight_down))

    attn_flops = 2 * (2 * seq * width * 4 * local + heads * seq * seq * 256 * 2 * 2)
    page = struct((seq, width), F32)
    page_low = struct((seq, width), BF16)

    def owned(*values):
        return [Own(value) for value in values]

    saved = [
        struct((3 * local, 2 * seq), BF16),
        struct((local, 2 * seq), BF16),
        struct((8, 2 * seq), F32),
        struct((2 * segs * heads, 2 * seq), BF16),
    ]

    def mlp(weights, rows, acc, name, last=False):
        first = acc is None
        ins = [*nms, cot, cot_got, *weights]
        at = len(ins)
        outs = call(
            functools.partial(mlp_body, first, last, *rows),
            ([page, page, *low_parts] if last else [page, page_low, page, page_low])
            + [struct((half, width), BF16)] * 2
            + [struct((8, half), F32)],
            name,
            alias={}
            if first
            else {at: 0, at + 2: 1}
            if last
            else {at + n: n for n in range(4)},
            scale=0,
        )(*ins, *(acc or ()))
        return list(outs[:-3]), *outs[-3:]

    xn, member, negative, index_h, index_v = scalar(
        start_body,
        [
            struct((seq, width), BF16),
            struct((segs, 2 * seq), BF16),
            struct((EXTRA, 2 * seq), BF16),
            struct((segs, 2 * seq), jnp.int32),
            struct((segs, 2 * seq), jnp.int32),
        ],
        "first_norm",
    )(
        place, Own(inputs), Own(gain_attn), Own(shift_attn),
        Own(segment), Own(valid), Own(bucket_horizontal), Own(bucket_vertical)
    )
    x_attn, xn, cot, cot_got, inputs_got, up_send, down_send = gate(
        [x_attn, xn, cotangent, cot_got, inputs_got], [up_send, down_send]
    )
    y_attn = beside(x_attn)
    z_attn = swap(x_attn, "dp", bits[0])
    x_up = across(up_send)
    xns = [xn, core(xn)]
    *kept_near, acc_0, acc_1 = call(
        functools.partial(attn_body, True), [*saved, page, page_low], "attn_near", scale=0
    )(*xns, near_w, index_h, index_v, member, negative)
    acc_0, acc_1, x_attn, y_attn, z_attn = gate([acc_0, acc_1, x_attn, y_attn, z_attn], [])
    corner = struct((piece.shape[0] // 2, width), BF16)
    low, high = call(corner_body, [corner] * 2, "attn_corner")(y_attn, z_attn)
    low, high = beside(low), swap(high, "dp", bits[0])
    x_up, down_send = gate([x_up], [down_send], acc_0)
    x_down = across(down_send)
    z_up = swap(x_up, "dp", bits[0])
    low, high = gate([low, high], [])
    edges = [2 * seq * n // PARTS // EXTRA * EXTRA for n in range(PARTS)] + [2 * seq]
    low_parts = [struct((high - low, width), BF16) for low, high in zip(edges, edges[1:])]
    outs = scalar(
        functools.partial(attn_body, False),
        [*saved, page, *low_parts, both],
        "attn_far",
        scale=0,
        alias={12: 4},
    )(
        place, *xns, x_attn, y_attn, z_attn, low, high, index_h, index_v, member, negative,
        acc_0, acc_1,
    )
    kept_far, far_w = outs[0:4], outs[-1]
    acc_0, *lows = outs[4:-1]
    middle, *nms = call(middle_body, [page, page_low, page_low], "second_norm", scale=0)(
        Own(inputs), inputs_got, acc_0, bias_out, gain_mlp, shift_mlp,
        *lows, *[core(value) for value in lows],
    )
    *nms, x_down, z_up, x_up = gate([*nms, x_down, z_up, x_up], [])
    z_down = swap(x_down, "dp", bits[0])
    up_rows, all_rows = half + EXTRA, 2 * half + EXTRA
    mlp_acc, near_up_1, near_down_1, near_sums_1 = mlp(
        [mlp_w, mlp_w], [all_rows, all_rows + up_rows], None, "mlp_near_1"
    )
    *mlp_acc, near_up_1 = gate([*mlp_acc, near_up_1], [])
    near_y_up = beside(near_up_1)
    mlp_acc, far_up_0, far_down_0, far_sums_0 = mlp([x_up, x_down], [0, 0], mlp_acc, "mlp_far_0")
    *mlp_acc, far_down_0 = gate([*mlp_acc, far_down_0], [])
    x_far_down_0 = across(far_down_0)
    mlp_acc, far_up_1, far_down_1, far_sums_1 = mlp([z_up, z_down], [0, 0], mlp_acc, "mlp_far_1")
    (far_up_send,) = scalar(pick_body, [struct((half + EXTRA, width), BF16)], "pick")(
        place, far_up_0, far_up_1
    )
    *mlp_acc, near_y_up, far_up_send, far_down_1 = gate(
        [*mlp_acc, near_y_up, far_up_send, far_down_1], []
    )
    y_far_up = beside(far_up_send)
    mlp_acc, near_up_0, near_down_0, near_sums_0 = mlp(
        [mlp_w, mlp_w], [0, up_rows], mlp_acc, "mlp_near_0", last=True
    )
    *mlp_acc, x_far_down_0, far_down_1 = gate([*mlp_acc, x_far_down_0, far_down_1], [])
    x_far_down_1 = across(far_down_1)
    result, grad_middle, grad_attn, turn_rows = call(
        turn_body,
        [Own(page_low), page, page_low, struct((8, width), F32)],
        "turn",
        scale=0,
    )(
        middle, mlp_acc[0], bias_down, mlp_acc[1], Own(cotangent), gain_mlp,
        *[core(value) for value in mlp_acc[2:]],
    )
    quarters = [struct((half, width), BF16)] * 2
    (up_send,) = scalar(plane_up_body, quarters[:1], "plane_up")(
        place, far_up_0, far_up_1, y_far_up, hold=[grad_attn]
    )
    grad_attn, up_send, x_far_down_1 = gate([grad_attn, up_send, x_far_down_1], [])
    x_up = across(up_send)
    (down_send,) = scalar(plane_down_body, quarters[:1], "plane_down")(
        place, near_down_1, x_far_down_0, x_far_down_1
    )
    y_down = beside(down_send)
    gas = [grad_attn, core(grad_attn)]

    def attn_back(weights, kept, acc, name, hold=()):
        first = acc is None
        ins = [
            place, *xns, *gas, weights, *kept, member, negative,
        ]
        outs = scalar(
            functools.partial(attn_back_body, first),
            [
                page,
                page_low,
                struct((2 * local, width), BF16),
                struct((2 * local, width), BF16),
                struct((8, 3 * local), F32),
                struct((2 * heads, segs, segs), F32),
            ],
            name,
            flops=2 * attn_flops,
            scratch=[pltpu.VMEM((3 * local, 2 * seq), BF16)],
            alias=None if first else {len(ins): 0, len(ins) + 1: 1},
        )(*ins, *(acc or ()), hold=hold)
        return list(outs[0:2]), outs[2:4], outs[4], outs[5]

    first_bit, *rest_bits = bits

    def resplit(groups, keep, got, name):
        for n, bit in enumerate(rest_bits):
            out = struct((keep.shape[0] // 2, width), BF16)
            body = functools.partial(resplit_body, 4 + n, groups)
            keep, give = scalar(body, [out] * 2, name + "_split")(place, keep, got)
            (got,) = yield [(give, "dp", bit)]
        (part,) = sums(name + "_total", (keep, got))
        for n, bit in reversed(list(enumerate(rest_bits))):
            (got,) = yield [(part, "dp", bit)]
            out = struct((2 * part.shape[0], width), BF16)
            body = functools.partial(join_body, 4 + n, groups)
            (part,) = scalar(body, [out], name + "_join")(place, part, got)
        y_got, z_got = yield [(part, "dp", 1), (part, "dp", first_bit)]
        out = struct((part.shape[0] // 2, width), BF16)
        low, high = call(corner_body, [out] * 2, name + "_corner")(y_got, z_got)
        low, high = yield [(low, "dp", 1), (high, "dp", first_bit)]
        return part, y_got, z_got, low, high

    def split(groups, name, *parts):
        out = struct((groups * parts[0].shape[0] // 2, width), BF16)
        body = functools.partial(split_body, 3, groups)
        return scalar(body, [out] * 2, name + "_split")(place, *parts)

    def attn_chain(far_0, far_got, near_0, near_1):
        (send,) = sums("attn_sum", (far_0, far_got))
        near_got, far_got = yield [(near_1, "dp", 1), (send, "mp", 2)]
        keep, give = split(1, "attn", near_0, near_got, far_got)
        (got,) = yield [(give, "dp", first_bit)]
        return (yield from resplit(1, keep, got, "attn"))

    acc, (far_attn_0, far_attn_1), sums_far, seg_far = attn_back(
        far_w, kept_far, None, "attn_back_far"
    )
    up_part, down_part = scalar(plane_part_body, quarters, "plane_part")(
        place, near_up_0, near_y_up, near_down_0, x_far_down_0, x_far_down_1, hold=[acc[0]]
    )
    *acc, x_up, y_down, far_attn_1, up_part, down_part = gate(
        [*acc, x_up, y_down, far_attn_1, up_part, down_part], []
    )
    y_far_attn = beside(far_attn_1)
    mlp_keep, mlp_give = split(2, "mlp", up_part, x_up, down_part, y_down)
    mlp_got = swap(mlp_give, "dp", first_bit)
    acc, (near_attn_0, near_attn_1), sums_near, seg_near = attn_back(
        near_w, kept_near, acc, "attn_back_near", hold=[mlp_give]
    )
    *acc, y_far_attn, near_attn_1 = gate([*acc, y_far_attn, near_attn_1], [])
    grad_inputs, end_rows = call(
        end_body, [Own(page_low), struct((8, width), F32)], "end"
    )(Own(inputs), acc[0], core(acc[1]), grad_middle, gain_attn)
    (small,) = scalar(small_body, [struct((16, width), F32)], "small")(
        place, near_sums_0, near_sums_1, far_sums_0, far_sums_1, sums_near, sums_far, seg_near, seg_far,
        Own(bucket_horizontal), Own(bucket_vertical), turn_rows, end_rows,
    )
    table = struct((heads, bins), F32)

    def small_chain(value):
        line = struct(value.shape, F32)
        for bit in bits:
            (got,) = yield [(value, "dp", bit)]
            (value,) = sums("small_sum", (value, got))
        got = yield [(value, "mp", 1), (value, "mp", 2), (value, "mp", 3)]
        (value,) = call(small_shards_body, [line], "small_shards")(value, *got)
        (got,) = yield [(value, "dp", 1)]
        return call(small_end_body, [line, Own(table), Own(table)], "small_end")(
            value, got, hold=[send[0] for send in asked["attn"]]
        )

    rounds = 4 + 2 * len(rest_bits)
    chains = {
        "attn": attn_chain(far_attn_0, y_far_attn, near_attn_0, near_attn_1),
    }
    asked = {"attn": next(chains["attn"])}
    (mlp_got,) = gate([mlp_got], [], asked["attn"][1][0])
    chains["mlp"] = resplit(2, mlp_keep, mlp_got, "mlp")
    asked["mlp"] = next(chains["mlp"])
    ends = {}
    for at in range(rounds):
        got = [swap(*send) for request in asked.values() for send in request]
        late = []
        if at == 0:
            late = [small]
        elif "done" in ends and at == rounds - 2:
            late = [ends["done"]]
        elif at == rounds - 1:
            late = [ends["small"][0]]
        *got, small = [*gate([*got, *late], [])] if at == 0 else [*gate(got, [], *late), small]
        got = iter(got)
        for name, request in list(asked.items()):
            received = [next(got) for _ in request]
            try:
                asked[name] = chains[name].send(received)
            except StopIteration as stop:
                ends[name] = stop.value
                del asked[name]
        if at == 0:
            chains["small"] = small_chain(small)
            asked["small"] = next(chains["small"])
        if "mlp" in ends and "done" not in ends:
            grad_up, grad_down, ends["done"] = scalar(
                unpack_mlp_body,
                [
                    Own(struct((width, hidden), F32)),
                    Own(struct((hidden, width), F32)),
                    struct((8, 128), F32),
                ],
                "unpack_mlp",
            )(place, *ends["mlp"])

    small_rows, grad_th, grad_tv = ends["small"]
    grad_wq, grad_wk, grad_wv, grad_wo = scalar(
        unpack_attn_body, [Own(struct((local, width), F32))] * 4, "unpack_attn"
    )(place, *ends["attn"])

    return (
        result,
        grad_inputs,
        small_rows[8],
        small_rows[9],
        grad_wq.T,
        small_rows[1, :local],
        grad_wk.T,
        grad_wv.T,
        small_rows[1, local:2 * local],
        grad_th.T,
        grad_tv.T,
        grad_wo,
        small_rows[4],
        small_rows[5],
        small_rows[6],
        grad_up,
        small_rows[0],
        grad_down,
        small_rows[7],
    )


def solution(mesh):
    rows = P(("dp", "mp"), None)
    columns = P(None, "mp")
    split = P("mp")
    placed = (
        rows, rows, P(), P(), columns, split, columns, columns, split, columns, columns,
        P("mp", None), P(), P(), P(), columns, split, P("mp", None), P(),
        P("dp", None), P("dp", None), P("dp", None, None), P("dp", None, None),
    )
    given = (
        rows, rows, P(), P(), columns, split, columns, columns, split, columns, columns,
        P("mp", None), P(), P(), P(), columns, split, P("mp", None), P(),
    )
    return jax.shard_map(
        functools.partial(on_device, mesh.shape["dp"], mesh.shape["mp"]),
        mesh=mesh,
        in_specs=placed,
        out_specs=given,
        check_vma=False,
    )
```

```python
import functools

import jax
import jax.numpy as jnp
from jax import lax
from jax.experimental import pallas as pl
from jax.experimental.pallas import tpu as pltpu
from jax.sharding import PartitionSpec as P

EPSILON = 1e-05
NEGATIVE = -1e30
HEAD = 64
EXTRA = 16
PARTS = 3
F32 = jnp.float32
BF16 = jnp.bfloat16
LIMIT = 16 * 1024 * 1024
SCALE = 30

NN = (((1,), (0,)), ((), ()))
NT = (((1,), (1,)), ((), ()))
TN = (((0,), (0,)), ((), ()))


def mm(left, right, dims=NN):
    return lax.dot_general(left, right, dims, preferred_element_type=F32)


def struct(shape, dtype):
    return jax.ShapeDtypeStruct(shape, dtype)


class Own:
    def __init__(self, value, cuts=()):
        self.value = value
        self.cuts = cuts


class Loaded:
    def __init__(self, source, scratch, sems, cuts):
        self.scratch = scratch
        self.shape = scratch.shape
        edges = [0, *cuts, scratch.shape[0]]
        self.parts = []
        for n, (low, high) in enumerate(zip(edges, edges[1:])):
            here = pl.ds(low, high - low)
            copy = pltpu.make_async_copy(source.at[here], scratch.at[here], sems[n])
            copy.start()
            self.parts.append((low, high, copy))

    def wait(self, low, high):
        for part in list(self.parts):
            if part[0] < high and low < part[1]:
                part[2].wait()
                self.parts.remove(part)

    def __getitem__(self, at):
        first = at[0] if isinstance(at, tuple) else at
        if isinstance(first, slice):
            self.wait(first.start or 0, self.shape[0] if first.stop is None else first.stop)
        else:
            self.wait(0, self.shape[0])
        return self.scratch[at]


class Stored:
    def __init__(self, target, scratch, sem):
        self.copy = pltpu.make_async_copy(scratch, target, sem)
        self.scratch = scratch
        self.shape = scratch.shape
        self.dtype = scratch.dtype
        self.sent = False

    def __getitem__(self, at):
        return self.scratch[at]

    def __setitem__(self, at, value):
        self.scratch[at] = value

    def flush(self):
        self.copy.start()
        self.sent = True


class Rows:
    def __init__(self, refs):
        self.refs = refs
        self.shape = (sum(ref.shape[0] for ref in refs), refs[0].shape[1])

    def __getitem__(self, at):
        rows, *rest = at if isinstance(at, tuple) else (at,)
        if rows is Ellipsis:
            rows = slice(None)
        return jnp.concatenate([ref[(slice(None), *rest)] for ref in self.refs], axis=0)[rows]


def spread(value, start, refs):
    at, end = 0, start + value.shape[0]
    for ref in refs:
        low, high = max(at, start), min(at + ref.shape[0], end)
        if low < high:
            ref[low - at:high - at, :] = value[low - start:high - start].astype(ref.dtype)
        at += ref.shape[0]


def flush(ref):
    if isinstance(ref, Stored):
        ref.flush()


def call(body, outs, name, flops=0, transcendentals=0, scalar=False, scratch=(), alias=None, scale=SCALE):
    def run(*args, hold=()):
        own_in = [isinstance(a, Own) for a in args]
        own_out = [isinstance(o, Own) for o in outs]
        ins = [a.value if own else a for a, own in zip(args, own_in)]
        shapes = [o.value if own else o for o, own in zip(outs, own_out)]
        moved = sum(a.size * a.dtype.itemsize for a in ins + shapes)
        count, held = len(ins), len(hold)
        total = sum(1 + len(v.cuts) for v in [*args, *outs] if isinstance(v, Own))
        copied = [v for v, own in zip(ins + shapes, own_in + own_out) if own]

        def inner(*refs):
            given, results = refs[:count], refs[count + held:count + held + len(shapes)]
            spare = refs[count + held + len(shapes):]
            slots, rest = iter(spare[:len(copied)]), spare[len(copied):]
            sems = iter(range(total))
            loaded = [
                Loaded(
                    ref, next(slots), [rest[-1].at[next(sems)] for _ in (0, *arg.cuts)], arg.cuts
                )
                if isinstance(arg, Own)
                else ref
                for ref, arg in zip(given, args)
            ]
            stored = [
                Stored(ref, next(slots), rest[-1].at[next(sems)]) if own else ref
                for ref, own in zip(results, own_out)
            ]
            body(*loaded, *stored, *(rest[:-1] if copied else rest))
            for ref in loaded:
                if isinstance(ref, Loaded):
                    ref.wait(0, ref.shape[0])
            for ref in stored:
                if isinstance(ref, Stored):
                    if not ref.sent:
                        ref.flush()
                    ref.copy.wait()

        buffers = [pltpu.VMEM(v.shape, v.dtype) for v in copied] + list(scratch)
        if copied:
            buffers.append(pltpu.SemaphoreType.DMA((total,)))
        kept = pl.BlockSpec(memory_space=pl.ANY)
        inside = pl.BlockSpec(memory_space=pltpu.VMEM)
        in_specs = [kept if own else inside for own in own_in]
        if scalar:
            in_specs[0] = pl.BlockSpec(memory_space=pltpu.SMEM)
        return pl.pallas_call(
            inner,
            out_shape=[
                (pltpu.HBM if own else pltpu.VMEM)(o.shape, o.dtype) for o, own in zip(shapes, own_out)
            ],
            in_specs=in_specs + [kept] * held,
            out_specs=[kept if own else inside for own in own_out],
            scratch_shapes=buffers,
            input_output_aliases=alias or {},
            compiler_params=pltpu.CompilerParams(vmem_limit_bytes=LIMIT),
            cost_estimate=pl.CostEstimate(
                flops=int(flops * scale),
                bytes_accessed=int(moved * scale),
                transcendentals=int(transcendentals),
            ),
            name=name,
        )(
            *[
                v
                if scalar and n == 0
                else pltpu.with_memory_space_constraint(v, pltpu.HBM if own else pltpu.VMEM)
                for n, (v, own) in enumerate(zip(ins, own_in))
            ],
            *hold,
        )

    return run


def line(ref):
    value = ref[...]
    return value if value.ndim == 2 else value.reshape(1, value.shape[0])


def halves(values):
    high = values.astype(BF16)
    return high, (values - high.astype(F32)).astype(BF16)


def pack_attn_body(place_ref, wq_ref, wk_ref, wv_ref, wo_ref, th_ref, tv_ref, bq_ref, bv_ref,
                   all_ref, send_ref):
    local = wq_ref.shape[0]
    heads = th_ref.shape[0]
    th, tv = th_ref[...], tv_ref[...]
    parts = []
    for m in range(heads):
        parts += [th[m:m + 1], tv[m:m + 1]]
    high, low = halves(jnp.concatenate(parts + [line(bq_ref), line(bv_ref)], axis=1))
    which = lax.broadcasted_iota(jnp.int32, (2 * EXTRA, high.shape[1]), 0)
    extra = jnp.where(which == 0, high.astype(F32), jnp.where(which == 1, low.astype(F32), 0.0))
    extra = extra.astype(BF16)
    side, along = place_ref[0, 0] == 0, place_ref[0, 3] == 0
    four = [ref[...] for ref in (wq_ref, wk_ref, wv_ref, wo_ref)]
    first, second = jnp.where(along, four[0], four[1]), jnp.where(along, four[2], four[3])
    send_ref[0:local, :] = jnp.where(side, first, second)
    send_ref[local:, :] = extra
    join_weights(all_ref, four, extra)


def join_weights(all_ref, four, extra):
    local = four[0].shape[0]
    piece = 2 * local + EXTRA
    for n, value in enumerate(four):
        at = (n // 2) * piece + (n % 2) * local
        all_ref[at:at + local, :] = value
    all_ref[2 * local:piece, :] = extra[0:EXTRA]
    all_ref[piece + 2 * local:, :] = extra[0:EXTRA]


def pack_mlp_body(place_ref, up_ref, bias_ref, down_ref, all_ref, up_send_ref, down_send_ref):
    half = down_ref.shape[0] // 2
    piece = 2 * half + EXTRA
    bias = line(bias_ref)
    which = lax.broadcasted_iota(jnp.int32, (EXTRA, half), 0) == 0

    def put(at, own, up_to, down_to, down_at):
        one, two = slice(at * half, (at + 1) * half), slice((1 - at) * half, (2 - at) * half)
        high, low = halves(jnp.where(own, bias[:, one], bias[:, two]))
        up_to(0, jnp.where(own, up_ref[0:half, one], up_ref[0:half, two]), high)
        up_to(half, jnp.where(own, up_ref[half:, one], up_ref[half:, two]), low)
        down_to[down_at:down_at + half, :] = jnp.where(own, down_ref[one, :], down_ref[two, :])

    def up_to(ref, at):
        def store(column, value, extra):
            ref[at:at + half, column:column + half] = value
            extra = jnp.where(which, extra.astype(F32), 0.0).astype(BF16)
            ref[at + half:at + half + EXTRA, column:column + half] = extra

        return store

    put(0, place_ref[0, 3] == 0, up_to(up_send_ref, 0), down_send_ref, 0)
    flush(up_send_ref)
    flush(down_send_ref)
    for n in (0, 1):
        at = n * piece
        put(n, place_ref[0, 0] == 0, up_to(all_ref, at), all_ref, at + half + EXTRA)


def start_body(place_ref, x_ref, gain_ref, shift_ref, seg_ref, valid_ref, bh_ref, bv_ref,
               xn_ref, mt_ref, neg_ref, ih_ref, iv_ref):
    x = x_ref[...].astype(F32)
    mean = jnp.mean(x, axis=1, keepdims=True)
    cen = x - mean
    var = jnp.mean(cen * cen, axis=1, keepdims=True)
    xn_ref[...] = (cen * lax.rsqrt(var + EPSILON) * line(gain_ref) + line(shift_ref)).astype(BF16)
    segs = mt_ref.shape[0]
    seq = x.shape[0]
    rows = lax.broadcasted_iota(jnp.int32, (segs, seq), 0)
    top = lax.broadcasted_iota(jnp.int32, (EXTRA, seq), 0) == 0
    for p in (0, 1):
        page = place_ref[0, 1 + p]
        here = pl.ds(p * seq, seq)
        member = jnp.where(rows == seg_ref[pl.ds(page, 1), :], 1.0, 0.0).astype(BF16)
        mt_ref[:, here] = member
        masked = jnp.where(valid_ref[pl.ds(page, 1), :] > 0, 0.0, NEGATIVE)
        neg_ref[:, here] = jnp.where(top, masked, 0.0).astype(BF16)
        bh, bv = bh_ref[page].astype(F32).astype(BF16), bv_ref[page].astype(F32).astype(BF16)
        ih_ref[:, here] = mm(bh, member, TN).astype(jnp.int32)
        iv_ref[:, here] = mm(bv, member, TN).astype(jnp.int32) + segs


def lookup(table, index):
    rows, seq = index.shape
    spread = jnp.broadcast_to(table, (rows, 128))
    parts = [
        jnp.take_along_axis(
            spread, index[:, at:at + 128], axis=1, mode="promise_in_bounds"
        )
        for at in range(0, seq, 128)
    ]
    return jnp.concatenate(parts, axis=1)


def attn_body(first, *refs):
    if first:
        w_ref, ih_ref, iv_ref, mt_ref, neg_ref = refs[2:7]
        given = (None, None)
        qkv_ref, ctx_ref, lse_ref, bias_ref, *outs = refs[7:]
    else:
        place_ref, pieces = refs[0], refs[3:8]
        ih_ref, iv_ref, mt_ref, neg_ref = refs[8:12]
        given = refs[12:14]
        qkv_ref, ctx_ref, lse_ref, bias_ref, *outs, w_ref = refs[14:]
        refs = refs[1:]
        own, beside, along, low, high = [ref[...] for ref in pieces]
        corner = jnp.concatenate([low, high], axis=0)
        local = own.shape[0] - 2 * EXTRA
        four = square(place_ref, own, beside, along, corner)
        join_weights(w_ref, [value[0:local] for value in four], own[local:])
        flush(w_ref)
    width = ctx_ref.shape[0]
    heads = width // HEAD
    segs = mt_ref.shape[0]
    seq = refs[0].shape[0]
    second = 2 * width + EXTRA
    extra = w_ref[2 * width:second, :]
    pick = jnp.where(lax.broadcasted_iota(jnp.int32, (EXTRA, seq), 0) < 2, 1.0, 0.0).astype(BF16)
    bias = mm(extra[:, heads * 128:heads * 128 + 2 * width], pick, TN)
    tables = extra[0:1, :].astype(F32) + extra[1:2, :].astype(F32)
    ones = jnp.ones((EXTRA, seq), BF16)
    for p in (0, 1):
        xn = refs[p][...]
        here = pl.ds(p * seq, seq)
        qk = mm(w_ref[0:2 * width, :], xn, NT)
        v = mm(w_ref[second:second + width, :], xn, NT)
        qkv_ref[0:width, here] = ((qk[0:width] + bias[0:width]) * 0.125).astype(BF16)
        qkv_ref[width:2 * width, here] = qk[width:].astype(BF16)
        qkv_ref[2 * width:, here] = (v + bias[width:]).astype(BF16)
    flush(qkv_ref)
    for p in (0, 1):
        here = pl.ds(p * seq, seq)
        member = mt_ref[:, here]
        for m in range(heads):
            table = tables[:, 128 * m:128 * m + 128]
            pos = lookup(table, ih_ref[:, here]) + lookup(table, iv_ref[:, here])
            high, low = halves(pos)
            bias_ref[2 * segs * m:2 * segs * m + segs, here] = high
            bias_ref[2 * segs * m + segs:2 * segs * (m + 1), here] = low
            at = HEAD * m
            q_aug = jnp.concatenate([qkv_ref[at:at + HEAD, here], high, low, ones], axis=0)
            k_aug = jnp.concatenate(
                [qkv_ref[width + at:width + at + HEAD, here], member, member, neg_ref[:, here]],
                axis=0,
            )
            scores = mm(k_aug, q_aug, TN)
            top = jnp.max(scores, axis=0, keepdims=True)
            expo = jnp.exp(scores - top).astype(BF16)
            v_aug = jnp.concatenate(
                [qkv_ref[2 * width + at:2 * width + at + HEAD, here], ones], axis=0
            )
            summed = mm(v_aug, expo)
            total = summed[HEAD:HEAD + 1]
            ctx_ref[at:at + HEAD, here] = (summed[0:HEAD] / total).astype(BF16)
            lse_ref[m:m + 1, here] = top + jnp.log(total)
        out = mm(ctx_ref[:, here], w_ref[second + width:second + 2 * width, :], TN)
        if given[p] is not None:
            out = given[p][...] + out
        if first:
            outs[p][...] = out.astype(outs[p].dtype)
            continue
        if p == 0:
            outs[0][...] = out
        spread(out, p * seq, outs[1:])
    lse_ref[heads:, :] = jnp.zeros((lse_ref.shape[0] - heads, 2 * seq), F32)


def middle_body(x_ref, other_x_ref, acc_ref, bias_ref, gain_ref, shift_ref, *refs):
    sent, got = Rows(refs[0:PARTS]), Rows(refs[PARTS:2 * PARTS])
    mid_ref, nm_ref, other_nm_ref = refs[2 * PARTS:]
    seq = x_ref.shape[0]
    own = acc_ref[...] + got[seq:, :].astype(F32)
    other = sent[seq:, :].astype(F32) + got[0:seq, :].astype(F32)
    for value, source_ref, out_ref in ((own, x_ref, nm_ref), (other, other_x_ref, other_nm_ref)):
        mid = source_ref[...].astype(F32) + value + line(bias_ref)
        if out_ref is nm_ref:
            mid_ref[...] = mid
        mean = jnp.mean(mid, axis=1, keepdims=True)
        cen = mid - mean
        var = jnp.mean(cen * cen, axis=1, keepdims=True)
        out = cen * lax.rsqrt(var + EPSILON) * line(gain_ref) + line(shift_ref)
        out_ref[...] = out.astype(BF16)


def mlp_body(first, last, up_at, down_at, *refs):
    nm_refs, cot_refs = refs[0:2], refs[2:4]
    refs = refs[4:]
    u_ref, d_ref = refs[0:2]
    given = (None,) * 4 if first else refs[2:6]
    *accs, up_ref, dn_ref, db_ref = refs[2 if first else 6:]
    if last:
        accs, parts = (accs[0], None, accs[1], None), accs[2:]
    half = up_ref.shape[0]
    extra = u_ref[up_at + half:up_at + half + EXTRA, :].astype(F32)
    bias = extra[0:1, 0:half] + extra[0:1, half:]
    up = jnp.concatenate(
        [u_ref[up_at:up_at + half, 0:half], u_ref[up_at:up_at + half, half:]], axis=0
    )
    down = d_ref[down_at:down_at + half, :]
    total = None
    for p in (0, 1):
        nm = nm_refs[p][...]
        cot = cot_refs[p][...]
        upper = mm(nm, up) + bias
        cdf = 0.5 + 0.5 * lax.erf(upper * 0.7071067811865476)
        pdf = jnp.exp(upper * upper * -0.5) * 0.3989422804014327
        hidden = (upper * cdf).astype(BF16)
        grad_hidden = mm(cot, down, NT)
        grad_upper = (grad_hidden * (cdf + upper * pdf)).astype(BF16)
        sums_now = (
            mm(nm, grad_upper, TN),
            mm(hidden, cot, TN),
            jnp.sum(grad_upper.astype(F32), axis=0, keepdims=True),
        )
        total = sums_now if total is None else [a + b for a, b in zip(total, sums_now)]
        down_out = mm(hidden, down)
        back = mm(grad_upper, up, NT)
        if not first:
            down_out = given[p][...].astype(F32) + down_out
            back = given[2 + p][...].astype(F32) + back
        if last and p == 1:
            spread(jnp.concatenate([down_out, back], axis=0), 0, parts)
            continue
        down_ref, back_ref = accs[p], accs[2 + p]
        down_ref[...] = down_out.astype(down_ref.dtype)
        back_ref[...] = back.astype(back_ref.dtype)
    up_ref[:, 0:half] = total[0][0:half].astype(BF16)
    up_ref[:, half:] = total[0][half:].astype(BF16)
    dn_ref[...] = total[1].astype(BF16)
    db_ref[...] = jnp.broadcast_to(total[2], db_ref.shape)


def turn_body(mid_ref, down_ref, bias_ref, back_ref, cot_ref, gain_ref, *refs):
    got, (res_ref, gmid_ref, ga_ref, rows_ref) = Rows(refs[:PARTS]), refs[PARTS:]
    mid = mid_ref[...]
    seq = mid.shape[0]
    down = down_ref[...] + got[0:seq, :].astype(F32)
    res_ref[...] = (mid + down + line(bias_ref)).astype(BF16)
    mean = jnp.mean(mid, axis=1, keepdims=True)
    cen = mid - mean
    var = jnp.mean(cen * cen, axis=1, keepdims=True)
    rstd = lax.rsqrt(var + EPSILON)
    n = cen * rstd
    back = back_ref[...] + got[seq:, :].astype(F32)
    q = back * line(gain_ref)
    cot = cot_ref[...].astype(F32)
    mean_q = jnp.mean(q, axis=1, keepdims=True)
    mean_qn = jnp.mean(q * n, axis=1, keepdims=True)
    grad = cot + rstd * (q - mean_q - n * mean_qn)
    gmid_ref[...] = grad
    ga_ref[...] = grad.astype(BF16)
    rows_ref[0:1, :] = jnp.sum(grad, axis=0, keepdims=True)
    rows_ref[1:2, :] = jnp.sum(back * n, axis=0, keepdims=True)
    rows_ref[2:3, :] = jnp.sum(back, axis=0, keepdims=True)
    rows_ref[3:4, :] = jnp.sum(cot, axis=0, keepdims=True)
    rows_ref[4:, :] = jnp.zeros((rows_ref.shape[0] - 4, rows_ref.shape[1]), F32)


def attn_back_body(first, *refs):
    place_ref, xn_refs, ga_refs = refs[0], refs[1:3], refs[3:5]
    w_ref, qkv_ref, ctx_ref, lse_ref, bias_ref, mt_ref, neg_ref = refs[5:12]
    given = (None, None) if first else refs[12:14]
    *backs, kept_ref, other_ref, sums_ref, seg_ref, dqkv_ref = refs[12 if first else 14:]
    width = ctx_ref.shape[0]
    heads = width // HEAD
    seq = xn_refs[0].shape[0]
    segs = mt_ref.shape[0]
    second = 2 * width + EXTRA
    ones = jnp.ones((EXTRA, seq), BF16)
    grad_out = None
    for p in (0, 1):
        here = pl.ds(p * seq, seq)
        ga = ga_refs[p][...]
        member = mt_ref[:, here]
        grad_ctx = mm(w_ref[second + width:second + 2 * width, :], ga, NT).astype(BF16)
        part = mm(ctx_ref[:, here], ga)
        grad_out = part if p == 0 else grad_out + part
        for m in range(heads):
            at = HEAD * m
            q = qkv_ref[at:at + HEAD, here]
            k = qkv_ref[width + at:width + at + HEAD, here]
            v = qkv_ref[2 * width + at:2 * width + at + HEAD, here]
            g = grad_ctx[at:at + HEAD]
            q_aug = jnp.concatenate(
                [q, bias_ref[2 * segs * m:2 * segs * (m + 1), here], ones], axis=0
            )
            k_aug = jnp.concatenate([k, member, member, neg_ref[:, here]], axis=0)
            scores = mm(k_aug, q_aug, TN)
            probs = jnp.exp(scores - lse_ref[m:m + 1, here])
            grad_probs = mm(v, g, TN)
            delta = jnp.sum(probs * grad_probs, axis=0, keepdims=True)
            grad_scores = (probs * (grad_probs - delta)).astype(BF16)
            grad_v = mm(g, probs.astype(BF16), NT)
            dqkv_ref[2 * width + at:2 * width + at + HEAD, here] = grad_v.astype(BF16)
            dqkv_ref[width + at:width + at + HEAD, here] = mm(q, grad_scores, NT).astype(BF16)
            both = mm(jnp.concatenate([k, member], axis=0), grad_scores)
            dqkv_ref[at:at + HEAD, here] = both[0:HEAD].astype(BF16) * jnp.asarray(0.125, BF16)
            high, low = halves(both[HEAD:])
            seg_ref[p * heads + m] = mm(member, high, NT) + mm(member, low, NT)
    grads = mm(dqkv_ref[:, 0:seq], xn_refs[0][...]) + mm(dqkv_ref[:, seq:], xn_refs[1][...])
    grads = jnp.concatenate([grads, grad_out], axis=0).astype(BF16)
    low = place_ref[0, 0] == 0
    kept_ref[...] = jnp.where(low, grads[0:2 * width], grads[2 * width:])
    flush(kept_ref)
    other_ref[...] = jnp.where(low, grads[2 * width:], grads[0:2 * width])
    flush(other_ref)
    for p in (0, 1):
        here = pl.ds(p * seq, seq)
        back = mm(dqkv_ref[0:2 * width, here], w_ref[0:2 * width, :], TN)
        back = back + mm(dqkv_ref[2 * width:, here], w_ref[second:second + width, :], TN)
        if given[p] is not None:
            back = given[p][...] + back
        backs[p][...] = back.astype(backs[p].dtype)
    sums_ref[...] = mm(jnp.ones((8, 2 * seq), BF16), dqkv_ref[...], NT)


def total_of(refs):
    if len(refs) == 2:
        return refs[0][...] + refs[1][...]
    value = refs[0][...].astype(F32)
    for ref in refs[1:]:
        value = value + ref[...].astype(F32)
    return value.astype(refs[0].dtype)


def sum_body(counts, *refs):
    outs = refs[sum(counts):]
    at = 0
    for count, out in zip(counts, outs):
        out[...] = total_of(refs[at:at + count])
        at += count


def sums(name, *groups, hold=()):
    outs = [struct(group[0].shape, group[0].dtype) for group in groups]
    body = functools.partial(sum_body, [len(group) for group in groups])
    flat = [value for group in groups for value in group]
    return call(body, outs, name)(*flat, hold=hold)


def pick_body(place_ref, zero_ref, one_ref, out_ref):
    same = place_ref[0, 0] == place_ref[0, 3]
    rows = one_ref.shape[0]
    out_ref[0:rows, :] = jnp.where(same, one_ref[...], zero_ref[...])
    out_ref[rows:, :] = jnp.zeros((out_ref.shape[0] - rows, out_ref.shape[1]), out_ref.dtype)


def plane_up_body(place_ref, up_0_ref, up_1_ref, got_ref, out_ref):
    same = place_ref[0, 0] == place_ref[0, 3]
    up = jnp.where(same, up_0_ref[...], up_1_ref[...])
    out_ref[...] = up + got_ref[0:up.shape[0], :]


def plane_down_body(place_ref, near_ref, down_0_ref, down_1_ref, out_ref):
    same = place_ref[0, 0] == place_ref[0, 3]
    out_ref[...] = near_ref[...] + jnp.where(same, down_1_ref[...], down_0_ref[...])


def plane_part_body(place_ref, up_0_ref, up_1_ref, down_ref, far_0_ref, far_1_ref,
                    up_ref, out_ref):
    same = place_ref[0, 0] == place_ref[0, 3]
    up_ref[...] = up_0_ref[...] + up_1_ref[...]
    out_ref[...] = down_ref[...] + jnp.where(same, far_0_ref[...], far_1_ref[...])


def put_halves(low, value, keep_ref, give_ref, at):
    size = value.shape[0] // 2
    one, two = value[0:size], value[size:]
    keep_ref[at:at + size, :] = jnp.where(low, one, two)
    give_ref[at:at + size, :] = jnp.where(low, two, one)


def split_body(which, groups, place_ref, *refs):
    *parts, keep_ref, give_ref = refs
    low = place_ref[0, which] == 0
    size = keep_ref.shape[0] // groups
    count = len(parts) // groups
    for n in range(groups):
        value = total_of(parts[n * count:(n + 1) * count])
        put_halves(low, value, keep_ref, give_ref, n * size)


def resplit_body(which, groups, place_ref, own_ref, got_ref, keep_ref, give_ref):
    low = place_ref[0, which] == 0
    size = keep_ref.shape[0] // groups
    value = own_ref[...] + got_ref[...]
    for n in range(groups):
        here = slice(2 * n * size, 2 * (n + 1) * size)
        put_halves(low, value[here], keep_ref, give_ref, n * size)


def join_body(which, groups, place_ref, own_ref, other_ref, out_ref):
    size = own_ref.shape[0] // groups
    low = place_ref[0, which] == 0
    own, other = own_ref[...], other_ref[...]
    for n in range(groups):
        part = slice(n * size, (n + 1) * size)
        out_ref[2 * n * size:(2 * n + 1) * size, :] = jnp.where(low, own[part], other[part])
        out_ref[(2 * n + 1) * size:(2 * n + 2) * size, :] = jnp.where(low, other[part], own[part])


def corner_body(y_ref, z_ref, low_ref, high_ref):
    size = low_ref.shape[0]
    low_ref[...] = z_ref[0:size, :]
    high_ref[...] = y_ref[size:, :]


def end_body(x_ref, back_ref, got_ref, gmid_ref, gain_ref, gx_ref, rows_ref):
    x = x_ref[...].astype(F32)
    mean = jnp.mean(x, axis=1, keepdims=True)
    cen = x - mean
    var = jnp.mean(cen * cen, axis=1, keepdims=True)
    rstd = lax.rsqrt(var + EPSILON)
    n = cen * rstd
    back = back_ref[...] + got_ref[...].astype(F32)
    q = back * line(gain_ref)
    mean_q = jnp.mean(q, axis=1, keepdims=True)
    mean_qn = jnp.mean(q * n, axis=1, keepdims=True)
    gx_ref[...] = (gmid_ref[...] + rstd * (q - mean_q - n * mean_qn)).astype(BF16)
    rows_ref[0:1, :] = jnp.sum(back * n, axis=0, keepdims=True)
    rows_ref[1:2, :] = jnp.sum(back, axis=0, keepdims=True)
    rows_ref[2:, :] = jnp.zeros((rows_ref.shape[0] - 2, rows_ref.shape[1]), F32)


def small_body(place_ref, near_0_ref, near_1_ref, far_0_ref, far_1_ref, sums_near_ref, sums_far_ref,
               seg_near_ref, seg_far_ref, bh_ref, bv_ref, turn_ref, end_ref, out_ref):
    count, segs, _ = seg_near_ref.shape
    heads = count // 2
    bins = lax.broadcasted_iota(jnp.int32, (segs, segs), 0)
    total = jnp.zeros((2 * EXTRA, 2 * segs), F32)
    for p in (0, 1):
        page = place_ref[0, 1 + p]
        bh, bv = bh_ref[page], bv_ref[page]
        own = pl.ds(p * heads, heads)
        for s in range(segs):
            both = jnp.concatenate(
                [
                    seg_near_ref[own, s, :],
                    seg_far_ref[own, s, :],
                    jnp.zeros((EXTRA - 2 * heads, segs), F32),
                ],
                axis=0,
            )
            hot = jnp.concatenate(
                [
                    jnp.where(bins == bh[s:s + 1, :], 1.0, 0.0),
                    jnp.where(bins == bv[s:s + 1, :], 1.0, 0.0),
                ],
                axis=0,
            ).astype(BF16)
            total = total + mm(jnp.concatenate(halves(both), axis=0), hot, NT)
    tables = total[0:EXTRA] + total[EXTRA:]
    side, low = place_ref[0, 0] == 0, place_ref[0, 3] == 0
    out_ref[...] = jnp.zeros(out_ref.shape, F32)
    width = sums_near_ref.shape[1] // 3
    half = near_0_ref.shape[1]
    near = (side, near_0_ref[0:1, :], near_1_ref[0:1, :], sums_near_ref)
    far = (low, far_0_ref[0:1, :], far_1_ref[0:1, :], sums_far_ref)
    for k, (own, one, two, sums_in) in enumerate((near, far)):
        out_ref[2 * k:2 * k + 1, 0:half] = jnp.where(own, one, two)
        out_ref[2 * k:2 * k + 1, half:] = jnp.where(own, two, one)
        parts = [sums_in[0:1, 0:width], sums_in[0:1, 2 * width:]]
        parts += [tables[k * heads + m:k * heads + m + 1] for m in range(heads)]
        out_ref[2 * k + 1:2 * k + 2, :] = jnp.concatenate(parts, axis=1)
    out_ref[4:8, :] = turn_ref[0:4, :]
    out_ref[8:10, :] = end_ref[0:2, :]


def small_shards_body(own_ref, core_ref, across_ref, corner_ref, out_ref):
    out_ref[...] = jnp.zeros(out_ref.shape, F32)
    out_ref[0:2, :] = own_ref[0:2, :] + across_ref[2:4, :]
    out_ref[4:10, :] = (own_ref[4:10, :] + across_ref[4:10, :]) + (
        core_ref[4:10, :] + corner_ref[4:10, :]
    )


def small_end_body(own_ref, got_ref, rows_ref, th_ref, tv_ref):
    rows_ref[...] = own_ref[...] + got_ref[...]
    own = own_ref[1:2, :] + got_ref[1:2, :]
    heads, bins = th_ref.shape
    for m in range(heads):
        at = own.shape[1] - 2 * bins * (heads - m)
        th_ref[m:m + 1, :] = own[:, at:at + bins]
        tv_ref[m:m + 1, :] = own[:, at + bins:at + 2 * bins]


def square(place_ref, own, beside, along, corner):
    side, low = place_ref[0, 0] == 0, place_ref[0, 3] == 0
    own_half = (jnp.where(low, own, along), jnp.where(low, along, own))
    other_half = (jnp.where(low, beside, corner), jnp.where(low, corner, beside))
    first = [jnp.where(side, a, b) for a, b in zip(own_half, other_half)]
    second = [jnp.where(side, b, a) for a, b in zip(own_half, other_half)]
    return first + second


def unpack_mlp_body(place_ref, own_ref, y_ref, z_ref, low_ref, high_ref,
                    up_ref, down_ref, done_ref):
    done_ref[...] = jnp.zeros(done_ref.shape, F32)
    size = low_ref.shape[0]
    half = 2 * size
    ups = square(
        place_ref, own_ref[0:size, :], y_ref[0:size, :], z_ref[0:size, :], low_ref[...]
    )
    for n, part in enumerate(ups):
        here = pl.ds((n // 2) * half, half)
        at = (n % 2) * size
        part = part.astype(F32)
        up_ref[at:at + size, here] = part[:, 0:half]
        up_ref[half + at:half + at + size, here] = part[:, half:]
    flush(up_ref)
    downs = square(
        place_ref, own_ref[size:, :], y_ref[size:, :], z_ref[size:, :], high_ref[...]
    )
    for n, part in enumerate(downs):
        down_ref[n * size:(n + 1) * size, :] = part.astype(F32)


def unpack_attn_body(place_ref, own_ref, y_ref, z_ref, low_ref, high_ref,
                     q_ref, k_ref, v_ref, o_ref):
    corner = jnp.concatenate([low_ref[...], high_ref[...]], axis=0)
    parts = square(place_ref, own_ref[...], y_ref[...], z_ref[...], corner)
    for ref, part in zip((q_ref, k_ref, v_ref, o_ref), parts):
        ref[...] = part.astype(F32)
        flush(ref)


def order_body(*refs):
    pass


def gate(inside, outside, *others):
    spec = pl.BlockSpec(memory_space=pl.ANY)
    spaces = [pltpu.VMEM] * len(inside) + [pltpu.HBM] * len(outside)
    values = [*inside, *outside]
    return pl.pallas_call(
        order_body,
        out_shape=[space(v.shape, v.dtype) for space, v in zip(spaces, values)],
        in_specs=[spec] * (len(values) + len(others)),
        out_specs=[spec] * len(values),
        input_output_aliases={n: n for n in range(len(values))},
        compiler_params=pltpu.CompilerParams(vmem_limit_bytes=2**20),
        name="order",
    )(
        *[pltpu.with_memory_space_constraint(v, space) for space, v in zip(spaces, values)],
        *others,
    )


def on_device(
    dp_count,
    mp_count,
    inputs,
    cotangent,
    gain_attn,
    shift_attn,
    weight_query,
    bias_query,
    weight_key,
    weight_value,
    bias_value,
    table_horizontal,
    table_vertical,
    weight_out,
    bias_out,
    gain_mlp,
    shift_mlp,
    weight_up,
    bias_up,
    weight_down,
    bias_down,
    segment,
    valid,
    bucket_horizontal,
    bucket_vertical,
):
    seq, width = inputs.shape
    local = weight_query.shape[1]
    heads = table_horizontal.shape[1]
    hidden = weight_up.shape[1]
    half = hidden // 2
    segs = bucket_horizontal.shape[1]
    bins = table_horizontal.shape[0]
    shard = lax.axis_index("mp")
    pages = lax.axis_index("dp")
    bits = [1 << b for b in range(1, dp_count.bit_length() - 1)]
    place = jnp.stack([pages % 2, shard, shard ^ 1] + [(pages // bit) % 2 for bit in bits])
    place = place.astype(jnp.int32).reshape(1, -1)
    scalar = functools.partial(call, scalar=True)

    def swap(value, axis, bit):
        count = dp_count if axis == "dp" else mp_count
        return lax.ppermute(value, axis, [(i, i ^ bit) for i in range(count)])

    def core(value):
        return swap(value, "mp", 1)

    def across(value):
        return swap(value, "mp", 2)

    def beside(value):
        return swap(value, "dp", 1)

    piece = struct((local + 2 * EXTRA, width), BF16)
    both = struct((4 * local + 2 * EXTRA, width), BF16)
    near_w, attn_send = scalar(pack_attn_body, [both, piece], "pack_attn")(
        place, Own(weight_query.T), Own(weight_key.T), Own(weight_value.T), Own(weight_out),
        Own(table_horizontal.T), Own(table_vertical.T), Own(bias_query), Own(bias_value),
    )
    x_attn = across(attn_send)
    cot_got, inputs_got = core(cotangent), core(inputs)
    mlp_w, up_send, down_send = scalar(
        pack_mlp_body,
        [
            struct((2 * (2 * half + EXTRA), width), BF16),
            Own(struct((half + EXTRA, width), BF16)),
            Own(struct((half, width), BF16)),
        ],
        "pack_mlp",
    )(place, Own(weight_up), bias_up, Own(weight_down))

    attn_flops = 2 * (2 * seq * width * 4 * local + heads * seq * seq * 256 * 2 * 2)
    page = struct((seq, width), F32)
    page_low = struct((seq, width), BF16)

    def owned(*values):
        return [Own(value) for value in values]

    saved = [
        struct((3 * local, 2 * seq), BF16),
        struct((local, 2 * seq), BF16),
        struct((8, 2 * seq), F32),
        struct((2 * segs * heads, 2 * seq), BF16),
    ]

    def mlp(weights, rows, acc, name, last=False):
        first = acc is None
        ins = [*nms, cot, cot_got, *weights]
        at = len(ins)
        outs = call(
            functools.partial(mlp_body, first, last, *rows),
            ([page, page, *low_parts] if last else [page, page_low, page, page_low])
            + [struct((half, width), BF16)] * 2
            + [struct((8, half), F32)],
            name,
            alias={}
            if first
            else {at: 0, at + 2: 1}
            if last
            else {at + n: n for n in range(4)},
            scale=0,
        )(*ins, *(acc or ()))
        return list(outs[:-3]), *outs[-3:]

    xn, member, negative, index_h, index_v = scalar(
        start_body,
        [
            struct((seq, width), BF16),
            struct((segs, 2 * seq), BF16),
            struct((EXTRA, 2 * seq), BF16),
            struct((segs, 2 * seq), jnp.int32),
            struct((segs, 2 * seq), jnp.int32),
        ],
        "first_norm",
    )(
        place, Own(inputs), Own(gain_attn), Own(shift_attn),
        Own(segment), Own(valid), Own(bucket_horizontal), Own(bucket_vertical)
    )
    x_attn, xn, cot, cot_got, inputs_got, up_send, down_send = gate(
        [x_attn, xn, cotangent, cot_got, inputs_got], [up_send, down_send]
    )
    y_attn = beside(x_attn)
    z_attn = swap(x_attn, "dp", bits[0])
    x_up = across(up_send)
    xns = [xn, core(xn)]
    *kept_near, acc_0, acc_1 = call(
        functools.partial(attn_body, True), [*saved, page, page_low], "attn_near", scale=0
    )(*xns, near_w, index_h, index_v, member, negative)
    acc_0, acc_1, x_attn, y_attn, z_attn = gate([acc_0, acc_1, x_attn, y_attn, z_attn], [])
    corner = struct((piece.shape[0] // 2, width), BF16)
    low, high = call(corner_body, [corner] * 2, "attn_corner")(y_attn, z_attn)
    low, high = beside(low), swap(high, "dp", bits[0])
    x_up, down_send = gate([x_up], [down_send], acc_0)
    x_down = across(down_send)
    z_up = swap(x_up, "dp", bits[0])
    low, high = gate([low, high], [])
    edges = [2 * seq * n // PARTS // EXTRA * EXTRA for n in range(PARTS)] + [2 * seq]
    low_parts = [struct((high - low, width), BF16) for low, high in zip(edges, edges[1:])]
    outs = scalar(
        functools.partial(attn_body, False),
        [*saved, page, *low_parts, both],
        "attn_far",
        scale=0,
        alias={12: 4},
    )(
        place, *xns, x_attn, y_attn, z_attn, low, high, index_h, index_v, member, negative,
        acc_0, acc_1,
    )
    kept_far, far_w = outs[0:4], outs[-1]
    acc_0, *lows = outs[4:-1]
    middle, *nms = call(middle_body, [page, page_low, page_low], "second_norm", scale=0)(
        Own(inputs), inputs_got, acc_0, bias_out, gain_mlp, shift_mlp,
        *lows, *[core(value) for value in lows],
    )
    *nms, x_down, z_up, x_up = gate([*nms, x_down, z_up, x_up], [])
    z_down = swap(x_down, "dp", bits[0])
    up_rows, all_rows = half + EXTRA, 2 * half + EXTRA
    mlp_acc, far_up_0, far_down_0, far_sums_0 = mlp([x_up, x_down], [0, 0], None, "mlp_far_0")
    *mlp_acc, far_down_0 = gate([*mlp_acc, far_down_0], [])
    x_far_down_0 = across(far_down_0)
    mlp_acc, near_up_1, near_down_1, near_sums_1 = mlp(
        [mlp_w, mlp_w], [all_rows, all_rows + up_rows], mlp_acc, "mlp_near_1"
    )
    *mlp_acc, near_up_1 = gate([*mlp_acc, near_up_1], [])
    near_y_up = beside(near_up_1)
    mlp_acc, far_up_1, far_down_1, far_sums_1 = mlp([z_up, z_down], [0, 0], mlp_acc, "mlp_far_1")
    (far_up_send,) = scalar(pick_body, [struct((half + EXTRA, width), BF16)], "pick")(
        place, far_up_0, far_up_1
    )
    *mlp_acc, x_far_down_0, far_up_send, far_down_1 = gate(
        [*mlp_acc, x_far_down_0, far_up_send, far_down_1], []
    )
    y_far_up = beside(far_up_send)
    x_far_down_1 = across(far_down_1)
    mlp_acc, near_up_0, near_down_0, near_sums_0 = mlp(
        [mlp_w, mlp_w], [0, up_rows], mlp_acc, "mlp_near_0", last=True
    )
    *mlp_acc, near_y_up = gate([*mlp_acc, near_y_up], [])
    result, grad_middle, grad_attn, turn_rows = call(
        turn_body,
        [Own(page_low), page, page_low, struct((8, width), F32)],
        "turn",
        scale=0,
    )(
        middle, mlp_acc[0], bias_down, mlp_acc[1], Own(cotangent), gain_mlp,
        *[core(value) for value in mlp_acc[2:]],
    )
    quarters = [struct((half, width), BF16)] * 2
    (down_send,) = scalar(plane_down_body, quarters[:1], "plane_down")(
        place, near_down_1, x_far_down_0, x_far_down_1, hold=[grad_attn]
    )
    grad_attn, down_send, y_far_up = gate([grad_attn, down_send, y_far_up], [])
    y_down = beside(down_send)
    (up_send,) = scalar(plane_up_body, quarters[:1], "plane_up")(
        place, far_up_0, far_up_1, y_far_up
    )
    x_up = across(up_send)
    gas = [grad_attn, core(grad_attn)]

    def attn_back(weights, kept, acc, name, hold=()):
        first = acc is None
        ins = [
            place, *xns, *gas, weights, *kept, member, negative,
        ]
        outs = scalar(
            functools.partial(attn_back_body, first),
            [
                page,
                page_low,
                struct((2 * local, width), BF16),
                struct((2 * local, width), BF16),
                struct((8, 3 * local), F32),
                struct((2 * heads, segs, segs), F32),
            ],
            name,
            flops=2 * attn_flops,
            scratch=[pltpu.VMEM((3 * local, 2 * seq), BF16)],
            alias=None if first else {len(ins): 0, len(ins) + 1: 1},
        )(*ins, *(acc or ()), hold=hold)
        return list(outs[0:2]), outs[2:4], outs[4], outs[5]

    first_bit, *rest_bits = bits

    def resplit(groups, keep, got, name):
        for n, bit in enumerate(rest_bits):
            out = struct((keep.shape[0] // 2, width), BF16)
            body = functools.partial(resplit_body, 4 + n, groups)
            keep, give = scalar(body, [out] * 2, name + "_split")(place, keep, got)
            (got,) = yield [(give, "dp", bit)]
        (part,) = sums(name + "_total", (keep, got))
        for n, bit in reversed(list(enumerate(rest_bits))):
            (got,) = yield [(part, "dp", bit)]
            out = struct((2 * part.shape[0], width), BF16)
            body = functools.partial(join_body, 4 + n, groups)
            (part,) = scalar(body, [out], name + "_join")(place, part, got)
        y_got, z_got = yield [(part, "dp", 1), (part, "dp", first_bit)]
        out = struct((part.shape[0] // 2, width), BF16)
        low, high = call(corner_body, [out] * 2, name + "_corner")(y_got, z_got)
        low, high = yield [(low, "dp", 1), (high, "dp", first_bit)]
        return part, y_got, z_got, low, high

    def split(groups, name, *parts):
        out = struct((groups * parts[0].shape[0] // 2, width), BF16)
        body = functools.partial(split_body, 3, groups)
        return scalar(body, [out] * 2, name + "_split")(place, *parts)

    def attn_chain(far_0, far_got, near_0, near_1):
        (send,) = sums("attn_sum", (far_0, far_got))
        near_got, far_got = yield [(near_1, "dp", 1), (send, "mp", 2)]
        keep, give = split(1, "attn", near_0, near_got, far_got)
        (got,) = yield [(give, "dp", first_bit)]
        return (yield from resplit(1, keep, got, "attn"))

    acc, (far_attn_0, far_attn_1), sums_far, seg_far = attn_back(
        far_w, kept_far, None, "attn_back_far"
    )
    up_part, down_part = scalar(plane_part_body, quarters, "plane_part")(
        place, near_up_0, near_y_up, near_down_0, x_far_down_0, x_far_down_1, hold=[acc[0]]
    )
    *acc, x_up, y_down, far_attn_1, up_part, down_part = gate(
        [*acc, x_up, y_down, far_attn_1, up_part, down_part], []
    )
    y_far_attn = beside(far_attn_1)
    mlp_keep, mlp_give = split(2, "mlp", up_part, x_up, down_part, y_down)
    mlp_got = swap(mlp_give, "dp", first_bit)
    acc, (near_attn_0, near_attn_1), sums_near, seg_near = attn_back(
        near_w, kept_near, acc, "attn_back_near", hold=[mlp_give]
    )
    *acc, y_far_attn, near_attn_1 = gate([*acc, y_far_attn, near_attn_1], [])
    grad_inputs, end_rows = call(
        end_body, [Own(page_low), struct((8, width), F32)], "end"
    )(Own(inputs), acc[0], core(acc[1]), grad_middle, gain_attn)
    (small,) = scalar(small_body, [struct((16, width), F32)], "small")(
        place, near_sums_0, near_sums_1, far_sums_0, far_sums_1, sums_near, sums_far, seg_near, seg_far,
        Own(bucket_horizontal), Own(bucket_vertical), turn_rows, end_rows,
    )
    table = struct((heads, bins), F32)

    def small_chain(value):
        line = struct(value.shape, F32)
        for bit in bits:
            (got,) = yield [(value, "dp", bit)]
            (value,) = sums("small_sum", (value, got))
        got = yield [(value, "mp", 1), (value, "mp", 2), (value, "mp", 3)]
        (value,) = call(small_shards_body, [line], "small_shards")(value, *got)
        (got,) = yield [(value, "dp", 1)]
        return call(small_end_body, [line, Own(table), Own(table)], "small_end")(
            value, got, hold=[send[0] for send in asked["attn"]]
        )

    rounds = 4 + 2 * len(rest_bits)
    chains = {
        "attn": attn_chain(far_attn_0, y_far_attn, near_attn_0, near_attn_1),
    }
    asked = {"attn": next(chains["attn"])}
    (mlp_got,) = gate([mlp_got], [], asked["attn"][1][0])
    chains["mlp"] = resplit(2, mlp_keep, mlp_got, "mlp")
    asked["mlp"] = next(chains["mlp"])
    ends = {}
    for at in range(rounds):
        got = [swap(*send) for request in asked.values() for send in request]
        late = []
        if at == 0:
            late = [small]
        elif "done" in ends and at == rounds - 2:
            late = [ends["done"]]
        elif at == rounds - 1:
            late = [ends["small"][0]]
        *got, small = [*gate([*got, *late], [])] if at == 0 else [*gate(got, [], *late), small]
        got = iter(got)
        for name, request in list(asked.items()):
            received = [next(got) for _ in request]
            try:
                asked[name] = chains[name].send(received)
            except StopIteration as stop:
                ends[name] = stop.value
                del asked[name]
        if at == 0:
            chains["small"] = small_chain(small)
            asked["small"] = next(chains["small"])
        if "mlp" in ends and "done" not in ends:
            grad_up, grad_down, ends["done"] = scalar(
                unpack_mlp_body,
                [
                    Own(struct((width, hidden), F32)),
                    Own(struct((hidden, width), F32)),
                    struct((8, 128), F32),
                ],
                "unpack_mlp",
            )(place, *ends["mlp"])

    small_rows, grad_th, grad_tv = ends["small"]
    grad_wq, grad_wk, grad_wv, grad_wo = scalar(
        unpack_attn_body, [Own(struct((local, width), F32))] * 4, "unpack_attn"
    )(place, *ends["attn"])

    return (
        result,
        grad_inputs,
        small_rows[8],
        small_rows[9],
        grad_wq.T,
        small_rows[1, :local],
        grad_wk.T,
        grad_wv.T,
        small_rows[1, local:2 * local],
        grad_th.T,
        grad_tv.T,
        grad_wo,
        small_rows[4],
        small_rows[5],
        small_rows[6],
        grad_up,
        small_rows[0],
        grad_down,
        small_rows[7],
    )


def solution(mesh):
    rows = P(("dp", "mp"), None)
    columns = P(None, "mp")
    split = P("mp")
    placed = (
        rows, rows, P(), P(), columns, split, columns, columns, split, columns, columns,
        P("mp", None), P(), P(), P(), columns, split, P("mp", None), P(),
        P("dp", None), P("dp", None), P("dp", None, None), P("dp", None, None),
    )
    given = (
        rows, rows, P(), P(), columns, split, columns, columns, split, columns, columns,
        P("mp", None), P(), P(), P(), columns, split, P("mp", None), P(),
    )
    return jax.shard_map(
        functools.partial(on_device, mesh.shape["dp"], mesh.shape["mp"]),
        mesh=mesh,
        in_specs=placed,
        out_specs=given,
        check_vma=False,
    )
```

```python
import functools

import jax
import jax.numpy as jnp
from jax import lax
from jax.experimental import pallas as pl
from jax.experimental.pallas import tpu as pltpu
from jax.sharding import PartitionSpec as P

EPSILON = 1e-05
NEGATIVE = -1e30
HEAD = 64
EXTRA = 16
PARTS = 3
F32 = jnp.float32
BF16 = jnp.bfloat16
LIMIT = 16 * 1024 * 1024
SCALE = 1

NN = (((1,), (0,)), ((), ()))
NT = (((1,), (1,)), ((), ()))
TN = (((0,), (0,)), ((), ()))


def mm(left, right, dims=NN):
    return lax.dot_general(left, right, dims, preferred_element_type=F32)


def struct(shape, dtype):
    return jax.ShapeDtypeStruct(shape, dtype)


class Own:
    def __init__(self, value, cuts=()):
        self.value = value
        self.cuts = cuts


class Loaded:
    def __init__(self, source, scratch, sems, cuts):
        self.scratch = scratch
        self.shape = scratch.shape
        edges = [0, *cuts, scratch.shape[0]]
        self.parts = []
        for n, (low, high) in enumerate(zip(edges, edges[1:])):
            here = pl.ds(low, high - low)
            copy = pltpu.make_async_copy(source.at[here], scratch.at[here], sems[n])
            copy.start()
            self.parts.append((low, high, copy))

    def wait(self, low, high):
        for part in list(self.parts):
            if part[0] < high and low < part[1]:
                part[2].wait()
                self.parts.remove(part)

    def __getitem__(self, at):
        first = at[0] if isinstance(at, tuple) else at
        if isinstance(first, slice):
            self.wait(first.start or 0, self.shape[0] if first.stop is None else first.stop)
        else:
            self.wait(0, self.shape[0])
        return self.scratch[at]


class Stored:
    def __init__(self, target, scratch, sem):
        self.copy = pltpu.make_async_copy(scratch, target, sem)
        self.scratch = scratch
        self.shape = scratch.shape
        self.dtype = scratch.dtype
        self.sent = False

    def __getitem__(self, at):
        return self.scratch[at]

    def __setitem__(self, at, value):
        self.scratch[at] = value

    def flush(self):
        self.copy.start()
        self.sent = True


class Rows:
    def __init__(self, refs):
        self.refs = refs
        self.shape = (sum(ref.shape[0] for ref in refs), refs[0].shape[1])

    def __getitem__(self, at):
        rows, *rest = at if isinstance(at, tuple) else (at,)
        if rows is Ellipsis:
            rows = slice(None)
        return jnp.concatenate([ref[(slice(None), *rest)] for ref in self.refs], axis=0)[rows]


def spread(value, start, refs):
    at, end = 0, start + value.shape[0]
    for ref in refs:
        low, high = max(at, start), min(at + ref.shape[0], end)
        if low < high:
            ref[low - at:high - at, :] = value[low - start:high - start].astype(ref.dtype)
        at += ref.shape[0]


def flush(ref):
    if isinstance(ref, Stored):
        ref.flush()


def call(body, outs, name, flops=0, transcendentals=0, scalar=False, scratch=(), alias=None, scale=SCALE):
    def run(*args, hold=()):
        own_in = [isinstance(a, Own) for a in args]
        own_out = [isinstance(o, Own) for o in outs]
        ins = [a.value if own else a for a, own in zip(args, own_in)]
        shapes = [o.value if own else o for o, own in zip(outs, own_out)]
        moved = sum(a.size * a.dtype.itemsize for a in ins + shapes)
        count, held = len(ins), len(hold)
        total = sum(1 + len(v.cuts) for v in [*args, *outs] if isinstance(v, Own))
        copied = [v for v, own in zip(ins + shapes, own_in + own_out) if own]

        def inner(*refs):
            given, results = refs[:count], refs[count + held:count + held + len(shapes)]
            spare = refs[count + held + len(shapes):]
            slots, rest = iter(spare[:len(copied)]), spare[len(copied):]
            sems = iter(range(total))
            loaded = [
                Loaded(
                    ref, next(slots), [rest[-1].at[next(sems)] for _ in (0, *arg.cuts)], arg.cuts
                )
                if isinstance(arg, Own)
                else ref
                for ref, arg in zip(given, args)
            ]
            stored = [
                Stored(ref, next(slots), rest[-1].at[next(sems)]) if own else ref
                for ref, own in zip(results, own_out)
            ]
            body(*loaded, *stored, *(rest[:-1] if copied else rest))
            for ref in loaded:
                if isinstance(ref, Loaded):
                    ref.wait(0, ref.shape[0])
            for ref in stored:
                if isinstance(ref, Stored):
                    if not ref.sent:
                        ref.flush()
                    ref.copy.wait()

        buffers = [pltpu.VMEM(v.shape, v.dtype) for v in copied] + list(scratch)
        if copied:
            buffers.append(pltpu.SemaphoreType.DMA((total,)))
        kept = pl.BlockSpec(memory_space=pl.ANY)
        inside = pl.BlockSpec(memory_space=pltpu.VMEM)
        in_specs = [kept if own else inside for own in own_in]
        if scalar:
            in_specs[0] = pl.BlockSpec(memory_space=pltpu.SMEM)
        return pl.pallas_call(
            inner,
            out_shape=[
                (pltpu.HBM if own else pltpu.VMEM)(o.shape, o.dtype) for o, own in zip(shapes, own_out)
            ],
            in_specs=in_specs + [kept] * held,
            out_specs=[kept if own else inside for own in own_out],
            scratch_shapes=buffers,
            input_output_aliases=alias or {},
            compiler_params=pltpu.CompilerParams(vmem_limit_bytes=LIMIT),
            cost_estimate=pl.CostEstimate(
                flops=int(flops * scale),
                bytes_accessed=int(moved * scale),
                transcendentals=int(transcendentals),
            ),
            name=name,
        )(
            *[
                v
                if scalar and n == 0
                else pltpu.with_memory_space_constraint(v, pltpu.HBM if own else pltpu.VMEM)
                for n, (v, own) in enumerate(zip(ins, own_in))
            ],
            *hold,
        )

    return run


def line(ref):
    value = ref[...]
    return value if value.ndim == 2 else value.reshape(1, value.shape[0])


def halves(values):
    high = values.astype(BF16)
    return high, (values - high.astype(F32)).astype(BF16)


def pack_attn_body(place_ref, wq_ref, wk_ref, wv_ref, wo_ref, th_ref, tv_ref, bq_ref, bv_ref,
                   all_ref, send_ref):
    local = wq_ref.shape[0]
    heads = th_ref.shape[0]
    th, tv = th_ref[...], tv_ref[...]
    parts = []
    for m in range(heads):
        parts += [th[m:m + 1], tv[m:m + 1]]
    high, low = halves(jnp.concatenate(parts + [line(bq_ref), line(bv_ref)], axis=1))
    which = lax.broadcasted_iota(jnp.int32, (2 * EXTRA, high.shape[1]), 0)
    extra = jnp.where(which == 0, high.astype(F32), jnp.where(which == 1, low.astype(F32), 0.0))
    extra = extra.astype(BF16)
    side, along = place_ref[0, 0] == 0, place_ref[0, 3] == 0
    four = [ref[...] for ref in (wq_ref, wk_ref, wv_ref, wo_ref)]
    first, second = jnp.where(along, four[0], four[1]), jnp.where(along, four[2], four[3])
    send_ref[0:local, :] = jnp.where(side, first, second)
    send_ref[local:, :] = extra
    join_weights(all_ref, four, extra)


def join_weights(all_ref, four, extra):
    local = four[0].shape[0]
    piece = 2 * local + EXTRA
    for n, value in enumerate(four):
        at = (n // 2) * piece + (n % 2) * local
        all_ref[at:at + local, :] = value
    all_ref[2 * local:piece, :] = extra[0:EXTRA]
    all_ref[piece + 2 * local:, :] = extra[0:EXTRA]


def pack_mlp_body(place_ref, up_ref, bias_ref, down_ref, all_ref, up_send_ref, down_send_ref):
    half = down_ref.shape[0] // 2
    piece = 2 * half + EXTRA
    bias = line(bias_ref)
    which = lax.broadcasted_iota(jnp.int32, (EXTRA, half), 0) == 0

    def put(at, own, up_to, down_to, down_at):
        one, two = slice(at * half, (at + 1) * half), slice((1 - at) * half, (2 - at) * half)
        high, low = halves(jnp.where(own, bias[:, one], bias[:, two]))
        up_to(0, jnp.where(own, up_ref[0:half, one], up_ref[0:half, two]), high)
        up_to(half, jnp.where(own, up_ref[half:, one], up_ref[half:, two]), low)
        down_to[down_at:down_at + half, :] = jnp.where(own, down_ref[one, :], down_ref[two, :])

    def up_to(ref, at):
        def store(column, value, extra):
            ref[at:at + half, column:column + half] = value
            extra = jnp.where(which, extra.astype(F32), 0.0).astype(BF16)
            ref[at + half:at + half + EXTRA, column:column + half] = extra

        return store

    put(0, place_ref[0, 3] == 0, up_to(up_send_ref, 0), down_send_ref, 0)
    flush(up_send_ref)
    flush(down_send_ref)
    for n in (0, 1):
        at = n * piece
        put(n, place_ref[0, 0] == 0, up_to(all_ref, at), all_ref, at + half + EXTRA)


def start_body(place_ref, x_ref, gain_ref, shift_ref, seg_ref, valid_ref, bh_ref, bv_ref,
               xn_ref, mt_ref, neg_ref, ih_ref, iv_ref):
    x = x_ref[...].astype(F32)
    mean = jnp.mean(x, axis=1, keepdims=True)
    cen = x - mean
    var = jnp.mean(cen * cen, axis=1, keepdims=True)
    xn_ref[...] = (cen * lax.rsqrt(var + EPSILON) * line(gain_ref) + line(shift_ref)).astype(BF16)
    segs = mt_ref.shape[0]
    seq = x.shape[0]
    rows = lax.broadcasted_iota(jnp.int32, (segs, seq), 0)
    top = lax.broadcasted_iota(jnp.int32, (EXTRA, seq), 0) == 0
    for p in (0, 1):
        page = place_ref[0, 1 + p]
        here = pl.ds(p * seq, seq)
        member = jnp.where(rows == seg_ref[pl.ds(page, 1), :], 1.0, 0.0).astype(BF16)
        mt_ref[:, here] = member
        masked = jnp.where(valid_ref[pl.ds(page, 1), :] > 0, 0.0, NEGATIVE)
        neg_ref[:, here] = jnp.where(top, masked, 0.0).astype(BF16)
        bh, bv = bh_ref[page].astype(F32).astype(BF16), bv_ref[page].astype(F32).astype(BF16)
        ih_ref[:, here] = mm(bh, member, TN).astype(jnp.int32)
        iv_ref[:, here] = mm(bv, member, TN).astype(jnp.int32) + segs


def lookup(table, index):
    rows, seq = index.shape
    spread = jnp.broadcast_to(table, (rows, 128))
    parts = [
        jnp.take_along_axis(
            spread, index[:, at:at + 128], axis=1, mode="promise_in_bounds"
        )
        for at in range(0, seq, 128)
    ]
    return jnp.concatenate(parts, axis=1)


def attn_body(first, *refs):
    if first:
        w_ref, ih_ref, iv_ref, mt_ref, neg_ref = refs[2:7]
        given = (None, None)
        qkv_ref, ctx_ref, lse_ref, bias_ref, *outs = refs[7:]
    else:
        place_ref, pieces = refs[0], refs[3:8]
        ih_ref, iv_ref, mt_ref, neg_ref = refs[8:12]
        given = refs[12:14]
        qkv_ref, ctx_ref, lse_ref, bias_ref, *outs, w_ref = refs[14:]
        refs = refs[1:]
        own, beside, along, low, high = [ref[...] for ref in pieces]
        corner = jnp.concatenate([low, high], axis=0)
        local = own.shape[0] - 2 * EXTRA
        four = square(place_ref, own, beside, along, corner)
        join_weights(w_ref, [value[0:local] for value in four], own[local:])
        flush(w_ref)
    width = ctx_ref.shape[0]
    heads = width // HEAD
    segs = mt_ref.shape[0]
    seq = refs[0].shape[0]
    second = 2 * width + EXTRA
    extra = w_ref[2 * width:second, :]
    pick = jnp.where(lax.broadcasted_iota(jnp.int32, (EXTRA, seq), 0) < 2, 1.0, 0.0).astype(BF16)
    bias = mm(extra[:, heads * 128:heads * 128 + 2 * width], pick, TN)
    tables = extra[0:1, :].astype(F32) + extra[1:2, :].astype(F32)
    ones = jnp.ones((EXTRA, seq), BF16)
    for p in (0, 1):
        xn = refs[p][...]
        here = pl.ds(p * seq, seq)
        qk = mm(w_ref[0:2 * width, :], xn, NT)
        v = mm(w_ref[second:second + width, :], xn, NT)
        qkv_ref[0:width, here] = ((qk[0:width] + bias[0:width]) * 0.125).astype(BF16)
        qkv_ref[width:2 * width, here] = qk[width:].astype(BF16)
        qkv_ref[2 * width:, here] = (v + bias[width:]).astype(BF16)
    flush(qkv_ref)
    for p in (0, 1):
        here = pl.ds(p * seq, seq)
        member = mt_ref[:, here]
        for m in range(heads):
            table = tables[:, 128 * m:128 * m + 128]
            pos = lookup(table, ih_ref[:, here]) + lookup(table, iv_ref[:, here])
            high, low = halves(pos)
            bias_ref[2 * segs * m:2 * segs * m + segs, here] = high
            bias_ref[2 * segs * m + segs:2 * segs * (m + 1), here] = low
            at = HEAD * m
            q_aug = jnp.concatenate([qkv_ref[at:at + HEAD, here], high, low, ones], axis=0)
            k_aug = jnp.concatenate(
                [qkv_ref[width + at:width + at + HEAD, here], member, member, neg_ref[:, here]],
                axis=0,
            )
            scores = mm(k_aug, q_aug, TN)
            top = jnp.max(scores, axis=0, keepdims=True)
            expo = jnp.exp(scores - top).astype(BF16)
            v_aug = jnp.concatenate(
                [qkv_ref[2 * width + at:2 * width + at + HEAD, here], ones], axis=0
            )
            summed = mm(v_aug, expo)
            total = summed[HEAD:HEAD + 1]
            ctx_ref[at:at + HEAD, here] = (summed[0:HEAD] / total).astype(BF16)
            lse_ref[m:m + 1, here] = top + jnp.log(total)
        out = mm(ctx_ref[:, here], w_ref[second + width:second + 2 * width, :], TN)
        if given[p] is not None:
            out = given[p][...] + out
        if first:
            outs[p][...] = out.astype(outs[p].dtype)
            continue
        if p == 0:
            outs[0][...] = out
        spread(out, p * seq, outs[1:])
    lse_ref[heads:, :] = jnp.zeros((lse_ref.shape[0] - heads, 2 * seq), F32)


def middle_body(x_ref, other_x_ref, acc_ref, bias_ref, gain_ref, shift_ref, *refs):
    sent, got = Rows(refs[0:PARTS]), Rows(refs[PARTS:2 * PARTS])
    mid_ref, nm_ref, other_nm_ref = refs[2 * PARTS:]
    seq = x_ref.shape[0]
    own = acc_ref[...] + got[seq:, :].astype(F32)
    other = sent[seq:, :].astype(F32) + got[0:seq, :].astype(F32)
    for value, source_ref, out_ref in ((own, x_ref, nm_ref), (other, other_x_ref, other_nm_ref)):
        mid = source_ref[...].astype(F32) + value + line(bias_ref)
        if out_ref is nm_ref:
            mid_ref[...] = mid
        mean = jnp.mean(mid, axis=1, keepdims=True)
        cen = mid - mean
        var = jnp.mean(cen * cen, axis=1, keepdims=True)
        out = cen * lax.rsqrt(var + EPSILON) * line(gain_ref) + line(shift_ref)
        out_ref[...] = out.astype(BF16)


def mlp_body(first, last, up_at, down_at, *refs):
    nm_refs, cot_refs = refs[0:2], refs[2:4]
    refs = refs[4:]
    u_ref, d_ref = refs[0:2]
    given = (None,) * 4 if first else refs[2:6]
    *accs, up_ref, dn_ref, db_ref = refs[2 if first else 6:]
    if last:
        accs, parts = (accs[0], None, accs[1], None), accs[2:]
    half = up_ref.shape[0]
    extra = u_ref[up_at + half:up_at + half + EXTRA, :].astype(F32)
    bias = extra[0:1, 0:half] + extra[0:1, half:]
    up = jnp.concatenate(
        [u_ref[up_at:up_at + half, 0:half], u_ref[up_at:up_at + half, half:]], axis=0
    )
    down = d_ref[down_at:down_at + half, :]
    total = None
    for p in (0, 1):
        nm = nm_refs[p][...]
        cot = cot_refs[p][...]
        upper = mm(nm, up) + bias
        cdf = 0.5 + 0.5 * lax.erf(upper * 0.7071067811865476)
        pdf = jnp.exp(upper * upper * -0.5) * 0.3989422804014327
        hidden = (upper * cdf).astype(BF16)
        grad_hidden = mm(cot, down, NT)
        grad_upper = (grad_hidden * (cdf + upper * pdf)).astype(BF16)
        sums_now = (
            mm(nm, grad_upper, TN),
            mm(hidden, cot, TN),
            jnp.sum(grad_upper.astype(F32), axis=0, keepdims=True),
        )
        total = sums_now if total is None else [a + b for a, b in zip(total, sums_now)]
        down_out = mm(hidden, down)
        back = mm(grad_upper, up, NT)
        if not first:
            down_out = given[p][...].astype(F32) + down_out
            back = given[2 + p][...].astype(F32) + back
        if last and p == 1:
            spread(jnp.concatenate([down_out, back], axis=0), 0, parts)
            continue
        down_ref, back_ref = accs[p], accs[2 + p]
        down_ref[...] = down_out.astype(down_ref.dtype)
        back_ref[...] = back.astype(back_ref.dtype)
    up_ref[:, 0:half] = total[0][0:half].astype(BF16)
    up_ref[:, half:] = total[0][half:].astype(BF16)
    dn_ref[...] = total[1].astype(BF16)
    db_ref[...] = jnp.broadcast_to(total[2], db_ref.shape)


def turn_body(mid_ref, down_ref, bias_ref, back_ref, cot_ref, gain_ref, *refs):
    got, (res_ref, gmid_ref, ga_ref, rows_ref) = Rows(refs[:PARTS]), refs[PARTS:]
    mid = mid_ref[...]
    seq = mid.shape[0]
    down = down_ref[...] + got[0:seq, :].astype(F32)
    res_ref[...] = (mid + down + line(bias_ref)).astype(BF16)
    mean = jnp.mean(mid, axis=1, keepdims=True)
    cen = mid - mean
    var = jnp.mean(cen * cen, axis=1, keepdims=True)
    rstd = lax.rsqrt(var + EPSILON)
    n = cen * rstd
    back = back_ref[...] + got[seq:, :].astype(F32)
    q = back * line(gain_ref)
    cot = cot_ref[...].astype(F32)
    mean_q = jnp.mean(q, axis=1, keepdims=True)
    mean_qn = jnp.mean(q * n, axis=1, keepdims=True)
    grad = cot + rstd * (q - mean_q - n * mean_qn)
    gmid_ref[...] = grad
    ga_ref[...] = grad.astype(BF16)
    rows_ref[0:1, :] = jnp.sum(grad, axis=0, keepdims=True)
    rows_ref[1:2, :] = jnp.sum(back * n, axis=0, keepdims=True)
    rows_ref[2:3, :] = jnp.sum(back, axis=0, keepdims=True)
    rows_ref[3:4, :] = jnp.sum(cot, axis=0, keepdims=True)
    rows_ref[4:, :] = jnp.zeros((rows_ref.shape[0] - 4, rows_ref.shape[1]), F32)


def attn_back_body(first, *refs):
    place_ref, xn_refs, ga_refs = refs[0], refs[1:3], refs[3:5]
    w_ref, qkv_ref, ctx_ref, lse_ref, bias_ref, mt_ref, neg_ref = refs[5:12]
    given = (None, None) if first else refs[12:14]
    *backs, kept_ref, other_ref, sums_ref, seg_ref, dqkv_ref = refs[12 if first else 14:]
    width = ctx_ref.shape[0]
    heads = width // HEAD
    seq = xn_refs[0].shape[0]
    segs = mt_ref.shape[0]
    second = 2 * width + EXTRA
    ones = jnp.ones((EXTRA, seq), BF16)
    grad_out = None
    for p in (0, 1):
        here = pl.ds(p * seq, seq)
        ga = ga_refs[p][...]
        member = mt_ref[:, here]
        grad_ctx = mm(w_ref[second + width:second + 2 * width, :], ga, NT).astype(BF16)
        part = mm(ctx_ref[:, here], ga)
        grad_out = part if p == 0 else grad_out + part
        for m in range(heads):
            at = HEAD * m
            q = qkv_ref[at:at + HEAD, here]
            k = qkv_ref[width + at:width + at + HEAD, here]
            v = qkv_ref[2 * width + at:2 * width + at + HEAD, here]
            g = grad_ctx[at:at + HEAD]
            q_aug = jnp.concatenate(
                [q, bias_ref[2 * segs * m:2 * segs * (m + 1), here], ones], axis=0
            )
            k_aug = jnp.concatenate([k, member, member, neg_ref[:, here]], axis=0)
            scores = mm(k_aug, q_aug, TN)
            probs = jnp.exp(scores - lse_ref[m:m + 1, here])
            grad_probs = mm(v, g, TN)
            delta = jnp.sum(probs * grad_probs, axis=0, keepdims=True)
            grad_scores = (probs * (grad_probs - delta)).astype(BF16)
            grad_v = mm(g, probs.astype(BF16), NT)
            dqkv_ref[2 * width + at:2 * width + at + HEAD, here] = grad_v.astype(BF16)
            dqkv_ref[width + at:width + at + HEAD, here] = mm(q, grad_scores, NT).astype(BF16)
            both = mm(jnp.concatenate([k, member], axis=0), grad_scores)
            dqkv_ref[at:at + HEAD, here] = both[0:HEAD].astype(BF16) * jnp.asarray(0.125, BF16)
            high, low = halves(both[HEAD:])
            seg_ref[p * heads + m] = mm(member, high, NT) + mm(member, low, NT)
    grads = mm(dqkv_ref[:, 0:seq], xn_refs[0][...]) + mm(dqkv_ref[:, seq:], xn_refs[1][...])
    grads = jnp.concatenate([grads, grad_out], axis=0).astype(BF16)
    low = place_ref[0, 0] == 0
    kept_ref[...] = jnp.where(low, grads[0:2 * width], grads[2 * width:])
    flush(kept_ref)
    other_ref[...] = jnp.where(low, grads[2 * width:], grads[0:2 * width])
    flush(other_ref)
    for p in (0, 1):
        here = pl.ds(p * seq, seq)
        back = mm(dqkv_ref[0:2 * width, here], w_ref[0:2 * width, :], TN)
        back = back + mm(dqkv_ref[2 * width:, here], w_ref[second:second + width, :], TN)
        if given[p] is not None:
            back = given[p][...] + back
        backs[p][...] = back.astype(backs[p].dtype)
    sums_ref[...] = mm(jnp.ones((8, 2 * seq), BF16), dqkv_ref[...], NT)


def total_of(refs):
    if len(refs) == 2:
        return refs[0][...] + refs[1][...]
    value = refs[0][...].astype(F32)
    for ref in refs[1:]:
        value = value + ref[...].astype(F32)
    return value.astype(refs[0].dtype)


def sum_body(counts, *refs):
    outs = refs[sum(counts):]
    at = 0
    for count, out in zip(counts, outs):
        out[...] = total_of(refs[at:at + count])
        at += count


def sums(name, *groups, hold=()):
    outs = [struct(group[0].shape, group[0].dtype) for group in groups]
    body = functools.partial(sum_body, [len(group) for group in groups])
    flat = [value for group in groups for value in group]
    return call(body, outs, name)(*flat, hold=hold)


def pick_body(place_ref, zero_ref, one_ref, out_ref):
    same = place_ref[0, 0] == place_ref[0, 3]
    rows = one_ref.shape[0]
    out_ref[0:rows, :] = jnp.where(same, one_ref[...], zero_ref[...])
    out_ref[rows:, :] = jnp.zeros((out_ref.shape[0] - rows, out_ref.shape[1]), out_ref.dtype)


def plane_up_body(place_ref, up_0_ref, up_1_ref, got_ref, out_ref):
    same = place_ref[0, 0] == place_ref[0, 3]
    up = jnp.where(same, up_0_ref[...], up_1_ref[...])
    out_ref[...] = up + got_ref[0:up.shape[0], :]


def plane_down_body(place_ref, near_ref, down_0_ref, down_1_ref, out_ref):
    same = place_ref[0, 0] == place_ref[0, 3]
    out_ref[...] = near_ref[...] + jnp.where(same, down_1_ref[...], down_0_ref[...])


def plane_part_body(place_ref, up_0_ref, up_1_ref, down_ref, far_0_ref, far_1_ref,
                    up_ref, out_ref):
    same = place_ref[0, 0] == place_ref[0, 3]
    up_ref[...] = up_0_ref[...] + up_1_ref[...]
    out_ref[...] = down_ref[...] + jnp.where(same, far_0_ref[...], far_1_ref[...])


def put_halves(low, value, keep_ref, give_ref, at):
    size = value.shape[0] // 2
    one, two = value[0:size], value[size:]
    keep_ref[at:at + size, :] = jnp.where(low, one, two)
    give_ref[at:at + size, :] = jnp.where(low, two, one)


def split_body(which, groups, place_ref, *refs):
    *parts, keep_ref, give_ref = refs
    low = place_ref[0, which] == 0
    size = keep_ref.shape[0] // groups
    count = len(parts) // groups
    for n in range(groups):
        value = total_of(parts[n * count:(n + 1) * count])
        put_halves(low, value, keep_ref, give_ref, n * size)


def resplit_body(which, groups, place_ref, own_ref, got_ref, keep_ref, give_ref):
    low = place_ref[0, which] == 0
    size = keep_ref.shape[0] // groups
    value = own_ref[...] + got_ref[...]
    for n in range(groups):
        here = slice(2 * n * size, 2 * (n + 1) * size)
        put_halves(low, value[here], keep_ref, give_ref, n * size)


def join_body(which, groups, place_ref, own_ref, other_ref, out_ref):
    size = own_ref.shape[0] // groups
    low = place_ref[0, which] == 0
    own, other = own_ref[...], other_ref[...]
    for n in range(groups):
        part = slice(n * size, (n + 1) * size)
        out_ref[2 * n * size:(2 * n + 1) * size, :] = jnp.where(low, own[part], other[part])
        out_ref[(2 * n + 1) * size:(2 * n + 2) * size, :] = jnp.where(low, other[part], own[part])


def corner_body(y_ref, z_ref, low_ref, high_ref):
    size = low_ref.shape[0]
    low_ref[...] = z_ref[0:size, :]
    high_ref[...] = y_ref[size:, :]


def end_body(x_ref, back_ref, got_ref, gmid_ref, gain_ref, gx_ref, rows_ref):
    x = x_ref[...].astype(F32)
    mean = jnp.mean(x, axis=1, keepdims=True)
    cen = x - mean
    var = jnp.mean(cen * cen, axis=1, keepdims=True)
    rstd = lax.rsqrt(var + EPSILON)
    n = cen * rstd
    back = back_ref[...] + got_ref[...].astype(F32)
    q = back * line(gain_ref)
    mean_q = jnp.mean(q, axis=1, keepdims=True)
    mean_qn = jnp.mean(q * n, axis=1, keepdims=True)
    gx_ref[...] = (gmid_ref[...] + rstd * (q - mean_q - n * mean_qn)).astype(BF16)
    rows_ref[0:1, :] = jnp.sum(back * n, axis=0, keepdims=True)
    rows_ref[1:2, :] = jnp.sum(back, axis=0, keepdims=True)
    rows_ref[2:, :] = jnp.zeros((rows_ref.shape[0] - 2, rows_ref.shape[1]), F32)


def small_body(place_ref, near_0_ref, near_1_ref, far_0_ref, far_1_ref, sums_near_ref, sums_far_ref,
               seg_near_ref, seg_far_ref, bh_ref, bv_ref, turn_ref, end_ref, out_ref):
    count, segs, _ = seg_near_ref.shape
    heads = count // 2
    bins = lax.broadcasted_iota(jnp.int32, (segs, segs), 0)
    total = jnp.zeros((2 * EXTRA, 2 * segs), F32)
    for p in (0, 1):
        page = place_ref[0, 1 + p]
        bh, bv = bh_ref[page], bv_ref[page]
        own = pl.ds(p * heads, heads)
        for s in range(segs):
            both = jnp.concatenate(
                [
                    seg_near_ref[own, s, :],
                    seg_far_ref[own, s, :],
                    jnp.zeros((EXTRA - 2 * heads, segs), F32),
                ],
                axis=0,
            )
            hot = jnp.concatenate(
                [
                    jnp.where(bins == bh[s:s + 1, :], 1.0, 0.0),
                    jnp.where(bins == bv[s:s + 1, :], 1.0, 0.0),
                ],
                axis=0,
            ).astype(BF16)
            total = total + mm(jnp.concatenate(halves(both), axis=0), hot, NT)
    tables = total[0:EXTRA] + total[EXTRA:]
    side, low = place_ref[0, 0] == 0, place_ref[0, 3] == 0
    out_ref[...] = jnp.zeros(out_ref.shape, F32)
    width = sums_near_ref.shape[1] // 3
    half = near_0_ref.shape[1]
    near = (side, near_0_ref[0:1, :], near_1_ref[0:1, :], sums_near_ref)
    far = (low, far_0_ref[0:1, :], far_1_ref[0:1, :], sums_far_ref)
    for k, (own, one, two, sums_in) in enumerate((near, far)):
        out_ref[2 * k:2 * k + 1, 0:half] = jnp.where(own, one, two)
        out_ref[2 * k:2 * k + 1, half:] = jnp.where(own, two, one)
        parts = [sums_in[0:1, 0:width], sums_in[0:1, 2 * width:]]
        parts += [tables[k * heads + m:k * heads + m + 1] for m in range(heads)]
        out_ref[2 * k + 1:2 * k + 2, :] = jnp.concatenate(parts, axis=1)
    out_ref[4:8, :] = turn_ref[0:4, :]
    out_ref[8:10, :] = end_ref[0:2, :]


def small_shards_body(own_ref, core_ref, across_ref, corner_ref, out_ref):
    out_ref[...] = jnp.zeros(out_ref.shape, F32)
    out_ref[0:2, :] = own_ref[0:2, :] + across_ref[2:4, :]
    out_ref[4:10, :] = (own_ref[4:10, :] + across_ref[4:10, :]) + (
        core_ref[4:10, :] + corner_ref[4:10, :]
    )


def small_end_body(own_ref, got_ref, rows_ref, th_ref, tv_ref):
    rows_ref[...] = own_ref[...] + got_ref[...]
    own = own_ref[1:2, :] + got_ref[1:2, :]
    heads, bins = th_ref.shape
    for m in range(heads):
        at = own.shape[1] - 2 * bins * (heads - m)
        th_ref[m:m + 1, :] = own[:, at:at + bins]
        tv_ref[m:m + 1, :] = own[:, at + bins:at + 2 * bins]


def square(place_ref, own, beside, along, corner):
    side, low = place_ref[0, 0] == 0, place_ref[0, 3] == 0
    own_half = (jnp.where(low, own, along), jnp.where(low, along, own))
    other_half = (jnp.where(low, beside, corner), jnp.where(low, corner, beside))
    first = [jnp.where(side, a, b) for a, b in zip(own_half, other_half)]
    second = [jnp.where(side, b, a) for a, b in zip(own_half, other_half)]
    return first + second


def unpack_mlp_body(place_ref, own_ref, y_ref, z_ref, low_ref, high_ref,
                    up_ref, down_ref, done_ref):
    done_ref[...] = jnp.zeros(done_ref.shape, F32)
    size = low_ref.shape[0]
    half = 2 * size
    ups = square(
        place_ref, own_ref[0:size, :], y_ref[0:size, :], z_ref[0:size, :], low_ref[...]
    )
    for n, part in enumerate(ups):
        here = pl.ds((n // 2) * half, half)
        at = (n % 2) * size
        part = part.astype(F32)
        up_ref[at:at + size, here] = part[:, 0:half]
        up_ref[half + at:half + at + size, here] = part[:, half:]
    flush(up_ref)
    downs = square(
        place_ref, own_ref[size:, :], y_ref[size:, :], z_ref[size:, :], high_ref[...]
    )
    for n, part in enumerate(downs):
        down_ref[n * size:(n + 1) * size, :] = part.astype(F32)


def unpack_attn_body(place_ref, own_ref, y_ref, z_ref, low_ref, high_ref,
                     q_ref, k_ref, v_ref, o_ref):
    corner = jnp.concatenate([low_ref[...], high_ref[...]], axis=0)
    parts = square(place_ref, own_ref[...], y_ref[...], z_ref[...], corner)
    for ref, part in zip((q_ref, k_ref, v_ref, o_ref), parts):
        ref[...] = part.astype(F32)
        flush(ref)


def order_body(*refs):
    pass


def gate(inside, outside, *others):
    spec = pl.BlockSpec(memory_space=pl.ANY)
    spaces = [pltpu.VMEM] * len(inside) + [pltpu.HBM] * len(outside)
    values = [*inside, *outside]
    return pl.pallas_call(
        order_body,
        out_shape=[space(v.shape, v.dtype) for space, v in zip(spaces, values)],
        in_specs=[spec] * (len(values) + len(others)),
        out_specs=[spec] * len(values),
        input_output_aliases={n: n for n in range(len(values))},
        compiler_params=pltpu.CompilerParams(vmem_limit_bytes=2**20),
        name="order",
    )(
        *[pltpu.with_memory_space_constraint(v, space) for space, v in zip(spaces, values)],
        *others,
    )


def on_device(
    dp_count,
    mp_count,
    inputs,
    cotangent,
    gain_attn,
    shift_attn,
    weight_query,
    bias_query,
    weight_key,
    weight_value,
    bias_value,
    table_horizontal,
    table_vertical,
    weight_out,
    bias_out,
    gain_mlp,
    shift_mlp,
    weight_up,
    bias_up,
    weight_down,
    bias_down,
    segment,
    valid,
    bucket_horizontal,
    bucket_vertical,
):
    seq, width = inputs.shape
    local = weight_query.shape[1]
    heads = table_horizontal.shape[1]
    hidden = weight_up.shape[1]
    half = hidden // 2
    segs = bucket_horizontal.shape[1]
    bins = table_horizontal.shape[0]
    shard = lax.axis_index("mp")
    pages = lax.axis_index("dp")
    bits = [1 << b for b in range(1, dp_count.bit_length() - 1)]
    place = jnp.stack([pages % 2, shard, shard ^ 1] + [(pages // bit) % 2 for bit in bits])
    place = place.astype(jnp.int32).reshape(1, -1)
    scalar = functools.partial(call, scalar=True)

    def swap(value, axis, bit):
        count = dp_count if axis == "dp" else mp_count
        return lax.ppermute(value, axis, [(i, i ^ bit) for i in range(count)])

    def core(value):
        return swap(value, "mp", 1)

    def across(value):
        return swap(value, "mp", 2)

    def beside(value):
        return swap(value, "dp", 1)

    piece = struct((local + 2 * EXTRA, width), BF16)
    both = struct((4 * local + 2 * EXTRA, width), BF16)
    near_w, attn_send = scalar(pack_attn_body, [both, piece], "pack_attn")(
        place, Own(weight_query.T), Own(weight_key.T), Own(weight_value.T), Own(weight_out),
        Own(table_horizontal.T), Own(table_vertical.T), Own(bias_query), Own(bias_value),
    )
    x_attn = across(attn_send)
    cot_got, inputs_got = core(cotangent), core(inputs)
    mlp_w, up_send, down_send = scalar(
        pack_mlp_body,
        [
            struct((2 * (2 * half + EXTRA), width), BF16),
            Own(struct((half + EXTRA, width), BF16)),
            Own(struct((half, width), BF16)),
        ],
        "pack_mlp",
    )(place, Own(weight_up), bias_up, Own(weight_down))

    attn_flops = 2 * (2 * seq * width * 4 * local + heads * seq * seq * 256 * 2 * 2)
    page = struct((seq, width), F32)
    page_low = struct((seq, width), BF16)

    def owned(*values):
        return [Own(value) for value in values]

    saved = [
        struct((3 * local, 2 * seq), BF16),
        struct((local, 2 * seq), BF16),
        struct((8, 2 * seq), F32),
        struct((2 * segs * heads, 2 * seq), BF16),
    ]

    def mlp(weights, rows, acc, name, last=False):
        first = acc is None
        ins = [*nms, cot, cot_got, *weights]
        at = len(ins)
        outs = call(
            functools.partial(mlp_body, first, last, *rows),
            ([page, page, *low_parts] if last else [page, page_low, page, page_low])
            + [struct((half, width), BF16)] * 2
            + [struct((8, half), F32)],
            name,
            alias={}
            if first
            else {at: 0, at + 2: 1}
            if last
            else {at + n: n for n in range(4)},
            scale=0,
        )(*ins, *(acc or ()))
        return list(outs[:-3]), *outs[-3:]

    xn, member, negative, index_h, index_v = scalar(
        start_body,
        [
            struct((seq, width), BF16),
            struct((segs, 2 * seq), BF16),
            struct((EXTRA, 2 * seq), BF16),
            struct((segs, 2 * seq), jnp.int32),
            struct((segs, 2 * seq), jnp.int32),
        ],
        "first_norm",
    )(
        place, Own(inputs), Own(gain_attn), Own(shift_attn),
        Own(segment), Own(valid), Own(bucket_horizontal), Own(bucket_vertical)
    )
    x_attn, xn, cot, cot_got, inputs_got, up_send, down_send = gate(
        [x_attn, xn, cotangent, cot_got, inputs_got], [up_send, down_send]
    )
    y_attn = beside(x_attn)
    z_attn = swap(x_attn, "dp", bits[0])
    x_up = across(up_send)
    xns = [xn, core(xn)]
    *kept_near, acc_0, acc_1 = call(
        functools.partial(attn_body, True), [*saved, page, page_low], "attn_near", scale=0
    )(*xns, near_w, index_h, index_v, member, negative)
    acc_0, acc_1, x_attn, y_attn, z_attn = gate([acc_0, acc_1, x_attn, y_attn, z_attn], [])
    corner = struct((piece.shape[0] // 2, width), BF16)
    low, high = call(corner_body, [corner] * 2, "attn_corner")(y_attn, z_attn)
    low, high = beside(low), swap(high, "dp", bits[0])
    x_up, down_send = gate([x_up], [down_send], acc_0)
    x_down = across(down_send)
    z_up = swap(x_up, "dp", bits[0])
    low, high = gate([low, high], [])
    edges = [2 * seq * n // PARTS // EXTRA * EXTRA for n in range(PARTS)] + [2 * seq]
    low_parts = [struct((high - low, width), BF16) for low, high in zip(edges, edges[1:])]
    outs = scalar(
        functools.partial(attn_body, False),
        [*saved, page, *low_parts, both],
        "attn_far",
        scale=0,
        alias={12: 4},
    )(
        place, *xns, x_attn, y_attn, z_attn, low, high, index_h, index_v, member, negative,
        acc_0, acc_1,
    )
    kept_far, far_w = outs[0:4], outs[-1]
    acc_0, *lows = outs[4:-1]
    middle, *nms = call(middle_body, [page, page_low, page_low], "second_norm", scale=0)(
        Own(inputs), inputs_got, acc_0, bias_out, gain_mlp, shift_mlp,
        *lows, *[core(value) for value in lows],
    )
    *nms, x_down, z_up, x_up = gate([*nms, x_down, z_up, x_up], [])
    z_down = swap(x_down, "dp", bits[0])
    up_rows, all_rows = half + EXTRA, 2 * half + EXTRA
    mlp_acc, far_up_0, far_down_0, far_sums_0 = mlp([x_up, x_down], [0, 0], None, "mlp_far_0")
    *mlp_acc, far_down_0 = gate([*mlp_acc, far_down_0], [])
    x_far_down_0 = across(far_down_0)
    mlp_acc, near_up_1, near_down_1, near_sums_1 = mlp(
        [mlp_w, mlp_w], [all_rows, all_rows + up_rows], mlp_acc, "mlp_near_1"
    )
    *mlp_acc, near_up_1 = gate([*mlp_acc, near_up_1], [])
    near_y_up = beside(near_up_1)
    mlp_acc, far_up_1, far_down_1, far_sums_1 = mlp([z_up, z_down], [0, 0], mlp_acc, "mlp_far_1")
    (far_up_send,) = scalar(pick_body, [struct((half + EXTRA, width), BF16)], "pick")(
        place, far_up_0, far_up_1
    )
    *mlp_acc, x_far_down_0, far_up_send, far_down_1 = gate(
        [*mlp_acc, x_far_down_0, far_up_send, far_down_1], []
    )
    y_far_up = beside(far_up_send)
    x_far_down_1 = across(far_down_1)
    mlp_acc, near_up_0, near_down_0, near_sums_0 = mlp(
        [mlp_w, mlp_w], [0, up_rows], mlp_acc, "mlp_near_0", last=True
    )
    *mlp_acc, near_y_up = gate([*mlp_acc, near_y_up], [])
    result, grad_middle, grad_attn, turn_rows = call(
        turn_body,
        [Own(page_low), page, page_low, struct((8, width), F32)],
        "turn",
        scale=0,
    )(
        middle, mlp_acc[0], bias_down, mlp_acc[1], Own(cotangent), gain_mlp,
        *[core(value) for value in mlp_acc[2:]],
    )
    quarters = [struct((half, width), BF16)] * 2
    (down_send,) = scalar(plane_down_body, quarters[:1], "plane_down")(
        place, near_down_1, x_far_down_0, x_far_down_1, hold=[grad_attn]
    )
    grad_attn, down_send, y_far_up = gate([grad_attn, down_send, y_far_up], [])
    y_down = beside(down_send)
    (up_send,) = scalar(plane_up_body, quarters[:1], "plane_up")(
        place, far_up_0, far_up_1, y_far_up
    )
    x_up = across(up_send)
    gas = [grad_attn, core(grad_attn)]

    def attn_back(weights, kept, acc, name, hold=()):
        first = acc is None
        ins = [
            place, *xns, *gas, weights, *kept, member, negative,
        ]
        outs = scalar(
            functools.partial(attn_back_body, first),
            [
                page,
                page_low,
                struct((2 * local, width), BF16),
                struct((2 * local, width), BF16),
                struct((8, 3 * local), F32),
                struct((2 * heads, segs, segs), F32),
            ],
            name,
            flops=2 * attn_flops,
            scratch=[pltpu.VMEM((3 * local, 2 * seq), BF16)],
            alias=None if first else {len(ins): 0, len(ins) + 1: 1},
        )(*ins, *(acc or ()), hold=hold)
        return list(outs[0:2]), outs[2:4], outs[4], outs[5]

    first_bit, *rest_bits = bits

    def resplit(groups, keep, got, name):
        for n, bit in enumerate(rest_bits):
            out = struct((keep.shape[0] // 2, width), BF16)
            body = functools.partial(resplit_body, 4 + n, groups)
            keep, give = scalar(body, [out] * 2, name + "_split")(place, keep, got)
            (got,) = yield [(give, "dp", bit)]
        (part,) = sums(name + "_total", (keep, got))
        for n, bit in reversed(list(enumerate(rest_bits))):
            (got,) = yield [(part, "dp", bit)]
            out = struct((2 * part.shape[0], width), BF16)
            body = functools.partial(join_body, 4 + n, groups)
            (part,) = scalar(body, [out], name + "_join")(place, part, got)
        y_got, z_got = yield [(part, "dp", 1), (part, "dp", first_bit)]
        out = struct((part.shape[0] // 2, width), BF16)
        low, high = call(corner_body, [out] * 2, name + "_corner")(y_got, z_got)
        low, high = yield [(low, "dp", 1), (high, "dp", first_bit)]
        return part, y_got, z_got, low, high

    def split(groups, name, *parts):
        out = struct((groups * parts[0].shape[0] // 2, width), BF16)
        body = functools.partial(split_body, 3, groups)
        return scalar(body, [out] * 2, name + "_split")(place, *parts)

    def attn_chain(far_0, far_got, near_0, near_1):
        (send,) = sums("attn_sum", (far_0, far_got))
        near_got, far_got = yield [(near_1, "dp", 1), (send, "mp", 2)]
        keep, give = split(1, "attn", near_0, near_got, far_got)
        (got,) = yield [(give, "dp", first_bit)]
        return (yield from resplit(1, keep, got, "attn"))

    acc, (far_attn_0, far_attn_1), sums_far, seg_far = attn_back(
        far_w, kept_far, None, "attn_back_far"
    )
    up_part, down_part = scalar(plane_part_body, quarters, "plane_part")(
        place, near_up_0, near_y_up, near_down_0, x_far_down_0, x_far_down_1, hold=[acc[0]]
    )
    *acc, x_up, y_down, far_attn_1, up_part, down_part = gate(
        [*acc, x_up, y_down, far_attn_1, up_part, down_part], []
    )
    y_far_attn = beside(far_attn_1)
    mlp_keep, mlp_give = split(2, "mlp", up_part, x_up, down_part, y_down)
    mlp_got = swap(mlp_give, "dp", first_bit)
    acc, (near_attn_0, near_attn_1), sums_near, seg_near = attn_back(
        near_w, kept_near, acc, "attn_back_near", hold=[mlp_give]
    )
    *acc, y_far_attn, near_attn_1 = gate([*acc, y_far_attn, near_attn_1], [])
    grad_inputs, end_rows = call(
        end_body, [Own(page_low), struct((8, width), F32)], "end"
    )(Own(inputs), acc[0], core(acc[1]), grad_middle, gain_attn)
    (small,) = scalar(small_body, [struct((16, width), F32)], "small")(
        place, near_sums_0, near_sums_1, far_sums_0, far_sums_1, sums_near, sums_far, seg_near, seg_far,
        Own(bucket_horizontal), Own(bucket_vertical), turn_rows, end_rows,
    )
    table = struct((heads, bins), F32)

    def small_chain(value):
        line = struct(value.shape, F32)
        for bit in bits:
            (got,) = yield [(value, "dp", bit)]
            (value,) = sums("small_sum", (value, got))
        got = yield [(value, "mp", 1), (value, "mp", 2), (value, "mp", 3)]
        (value,) = call(small_shards_body, [line], "small_shards")(value, *got)
        (got,) = yield [(value, "dp", 1)]
        return call(small_end_body, [line, Own(table), Own(table)], "small_end")(
            value, got, hold=[send[0] for send in asked["attn"]]
        )

    rounds = 4 + 2 * len(rest_bits)
    chains = {
        "attn": attn_chain(far_attn_0, y_far_attn, near_attn_0, near_attn_1),
    }
    asked = {"attn": next(chains["attn"])}
    (mlp_got,) = gate([mlp_got], [], asked["attn"][1][0])
    chains["mlp"] = resplit(2, mlp_keep, mlp_got, "mlp")
    asked["mlp"] = next(chains["mlp"])
    ends = {}
    for at in range(rounds):
        got = [swap(*send) for request in asked.values() for send in request]
        late = []
        if at == 0:
            late = [small]
        elif "done" in ends and at == rounds - 2:
            late = [ends["done"]]
        elif at == rounds - 1:
            late = [ends["small"][0]]
        *got, small = [*gate([*got, *late], [])] if at == 0 else [*gate(got, [], *late), small]
        got = iter(got)
        for name, request in list(asked.items()):
            received = [next(got) for _ in request]
            try:
                asked[name] = chains[name].send(received)
            except StopIteration as stop:
                ends[name] = stop.value
                del asked[name]
        if at == 0:
            chains["small"] = small_chain(small)
            asked["small"] = next(chains["small"])
        if "mlp" in ends and "done" not in ends:
            grad_up, grad_down, ends["done"] = scalar(
                unpack_mlp_body,
                [
                    Own(struct((width, hidden), F32)),
                    Own(struct((hidden, width), F32)),
                    struct((8, 128), F32),
                ],
                "unpack_mlp",
            )(place, *ends["mlp"])

    small_rows, grad_th, grad_tv = ends["small"]
    grad_wq, grad_wk, grad_wv, grad_wo = scalar(
        unpack_attn_body, [Own(struct((local, width), F32))] * 4, "unpack_attn"
    )(place, *ends["attn"])

    return (
        result,
        grad_inputs,
        small_rows[8],
        small_rows[9],
        grad_wq.T,
        small_rows[1, :local],
        grad_wk.T,
        grad_wv.T,
        small_rows[1, local:2 * local],
        grad_th.T,
        grad_tv.T,
        grad_wo,
        small_rows[4],
        small_rows[5],
        small_rows[6],
        grad_up,
        small_rows[0],
        grad_down,
        small_rows[7],
    )


def solution(mesh):
    rows = P(("dp", "mp"), None)
    columns = P(None, "mp")
    split = P("mp")
    placed = (
        rows, rows, P(), P(), columns, split, columns, columns, split, columns, columns,
        P("mp", None), P(), P(), P(), columns, split, P("mp", None), P(),
        P("dp", None), P("dp", None), P("dp", None, None), P("dp", None, None),
    )
    given = (
        rows, rows, P(), P(), columns, split, columns, columns, split, columns, columns,
        P("mp", None), P(), P(), P(), columns, split, P("mp", None), P(),
    )
    return jax.shard_map(
        functools.partial(on_device, mesh.shape["dp"], mesh.shape["mp"]),
        mesh=mesh,
        in_specs=placed,
        out_specs=given,
        check_vma=False,
    )
```
